256 devices in a mesh: grp: 8 (over x, core), shard: 32 (over z, y).
Axes of the slice: x: 4, y: 4, z: 8, core: 2. Of those that a mesh axis runs over, the one named last changes fastest.
Arguments:
- queries: bfloat16 [32768, 768], P(('grp', 'shard')), may hold values from -6 to 6
- positives: bfloat16 [32768, 768], P(('grp', 'shard')), may hold values from -6 to 6
- negative_ids: int32 [32768, 16], P(('grp', 'shard')), may hold values from 0 to 131071, as said below
- passage_table: bfloat16 [131072, 768], P('shard'), may hold values from -6 to 6
- inner_weight: bfloat16 [768, 2048], P('shard'), may hold values from -0.21875 to 0.21875
- outer_weight: bfloat16 [2048, 768], P('shard'), may hold values from -0.125 to 0.125
Outputs:
- loss_values: float32 [32768], P(('grp', 'shard'))
- inner_grad: float32 [768, 2048], P('shard')
- outer_grad: float32 [2048, 768], P('shard')
The draws below stay inside these ranges and needn't reach their ends.
Inputs may be any that keep to these rules, and one draw needn't show every extreme that they name: `negative_ids`: the owner of a row id is id // 4096. The 2048 ids of one block of 128 consecutive queries name at most 128 rows of one owner; one owner gets exactly 128 from every block. Owners 2 j and 2 j + 1 form a pair, and each block names exactly 128 rows of each pair. Rows may repeat.
All inputs are finite; a program needn't handle non-finite values.
Results may differ from the reference program's by a relative error of at most 0.025.
Values may be sent and summed in bfloat16 or wider, within the bound.
No kernel may reach another device: no remote copies, remote signals or barrier semaphores. Data moves between devices by JAX's collectives and lax.ppermute only.
A program may use at most 128 MiB of HBM per device.

```python
import jax
import jax.numpy as jnp
from jax import lax

D = 768
HID = 2048
Q_DEV = 128
NEG = 16
ROWS_DEV = 4096
QUERIES = 32768
ROWS = 131072
N_SHARD = 32


def draw_negative_ids(key, part):
    key = jax.random.fold_in(key, 7)
    blocks = QUERIES // Q_DEV
    per_block = Q_DEV * NEG
    mean_load = per_block // N_SHARD
    pair_count = N_SHARD // 2
    keys = jax.random.split(key, 7)
    pair_order = jax.random.permutation(keys[0], pair_count).astype(jnp.int32)
    flips = jax.random.randint(keys[6], (pair_count,), 0, 2).astype(jnp.int32)
    owner_order = jnp.stack([2 * pair_order + flips, 2 * pair_order + 1 - flips], axis=1).reshape(-1).astype(jnp.int32)
    shifts = jax.random.randint(keys[1], (blocks, pair_count), 0, mean_load + 1).astype(jnp.int32)
    shifts = shifts.at[:, 0].set(mean_load)
    positions = jnp.arange(per_block, dtype=jnp.int32)
    pair_of = positions // (2 * mean_load)
    within = positions % (2 * mean_load)
    first_side = within[None, :] < mean_load + shifts[:, pair_of]
    owners = jnp.where(first_side, owner_order[2 * pair_of][None, :], owner_order[2 * pair_of + 1][None, :])
    block_keys = jax.random.split(keys[2], blocks)
    shuffles = jax.vmap(lambda block_key: jax.random.permutation(block_key, per_block))(block_keys).astype(jnp.int32)
    owners = jnp.take_along_axis(owners, shuffles, axis=1)
    first_pick = jax.random.randint(keys[3], (blocks, per_block), 0, ROWS_DEV).astype(jnp.int32)
    second_pick = jax.random.randint(keys[4], (blocks, per_block), 0, ROWS_DEV).astype(jnp.int32)
    skewed = first_pick * second_pick // ROWS_DEV
    offsets = jax.random.randint(keys[5], (N_SHARD,), 0, ROWS_DEV).astype(jnp.int32)
    local_rows = (skewed + offsets[owners]) % ROWS_DEV
    return (owners * ROWS_DEV + local_rows).reshape(QUERIES, NEG).astype(jnp.int32)


def shard_levels(own_key, extent, cuts, low, largest):
    factor_of = 1.0
    for axis_at, shards_of in cuts:
        steps = jax.random.uniform(jax.random.fold_in(jax.random.fold_in(own_key, 6), axis_at), (shards_of,), jnp.float32, low / len(cuts), largest / len(cuts))
        factor_of = factor_of * jnp.repeat(jnp.exp(steps), extent[axis_at] // shards_of).reshape((-1,) + (1,) * (len(extent) - 1 - axis_at))
    return factor_of


def bell_draw(own_key, dims, width, limit, pieces=(), kind=jnp.bfloat16):
    loudness = shard_levels(own_key, dims, pieces, -0.22, 0.18) if pieces else 1.0
    array = jax.random.normal(own_key, dims, jnp.float32) * width * loudness
    return jnp.minimum(jnp.maximum(array, -limit), limit).astype(kind)


def setup_inputs(seed: int = 0) -> dict:
    splits = jax.random.split(jax.random.key(seed), 7)
    return {
        "queries": bell_draw(splits[0], (QUERIES, D), 1.0, 6.0, ((0, 256),)),
        "positives": bell_draw(splits[1], (QUERIES, D), 1.0, 6.0, ((0, 256),)),
        "negative_ids": draw_negative_ids(jax.random.fold_in(splits[6], 71), 0),
        "passage_table": bell_draw(splits[3], (ROWS, D), 1.0, 6.0, ((0, 32),)),
        "inner_weight": bell_draw(splits[4], (D, HID), D ** -0.5, 0.21875, ((0, 32),)),
        "outer_weight": bell_draw(splits[5], (HID, D), HID ** -0.5, 0.125, ((0, 32),)),
    }


def gelu_value(pre_act):
    return pre_act * 0.5 * (1.0 + lax.erf(pre_act * 0.7071067811865476))


def gelu_slope(pre_act):
    return 0.5 * (1.0 + lax.erf(pre_act * 0.7071067811865476)) + pre_act * jnp.exp(-0.5 * pre_act * pre_act) * 0.3989422804014327


def reference(queries, positives, negative_ids, passage_table, inner_weight, outer_weight):
    scale = float(D) ** -0.5
    blocks = QUERIES // Q_DEV
    query_blocks = queries.reshape(blocks, Q_DEV, D)
    positive_blocks = positives.reshape(blocks, Q_DEV, D)
    id_blocks = negative_ids.reshape(blocks, Q_DEV, NEG)

    def block_step(carry, inputs):
        inner_sum, outer_sum = carry
        features, positive, block_ids = inputs
        pre_act = jnp.dot(features, inner_weight, preferred_element_type=jnp.float32)
        hidden = gelu_value(pre_act).astype(jnp.bfloat16)
        embedded = (features.astype(jnp.float32) + jnp.dot(hidden, outer_weight, preferred_element_type=jnp.float32)).astype(jnp.bfloat16)
        negatives = jnp.take(passage_table, block_ids, axis=0)
        emb_wide = embedded.astype(jnp.float32)
        neg_wide = negatives.astype(jnp.float32)
        pos_wide = positive.astype(jnp.float32)
        neg_scores = jnp.einsum("qd,qkd->qk", emb_wide, neg_wide, precision=lax.Precision.HIGHEST) * scale
        pos_scores = jnp.sum(emb_wide * pos_wide, axis=1) * scale
        scores = jnp.concatenate([pos_scores[:, None], neg_scores], axis=1)
        log_total = jnp.log(jnp.sum(jnp.exp(scores), axis=1))
        losses = log_total - pos_scores
        score_grad = jnp.exp(scores - log_total[:, None]).at[:, 0].add(-1.0)
        neg_term = jnp.einsum("qk,qkd->qd", score_grad[:, 1:], neg_wide, precision=lax.Precision.HIGHEST)
        query_grad = ((score_grad[:, 0:1] * pos_wide + neg_term) * scale).astype(jnp.bfloat16)
        hidden_grad = jnp.dot(query_grad, outer_weight.T, preferred_element_type=jnp.float32)
        pre_grad = (hidden_grad * gelu_slope(pre_act)).astype(jnp.bfloat16)
        inner_term = jnp.dot(features.T, pre_grad, preferred_element_type=jnp.float32).astype(jnp.bfloat16)
        outer_term = jnp.dot(hidden.T, query_grad, preferred_element_type=jnp.float32).astype(jnp.bfloat16)
        inner_term = lax.optimization_barrier(inner_term)
        outer_term = lax.optimization_barrier(outer_term)
        inner_sum = inner_sum + inner_term.astype(jnp.float32)
        outer_sum = outer_sum + outer_term.astype(jnp.float32)
        return (inner_sum, outer_sum), losses

    start_carry = (jnp.zeros((D, HID), jnp.float32), jnp.zeros((HID, D), jnp.float32))
    (inner_grad, outer_grad), loss_blocks = lax.scan(block_step, start_carry, (query_blocks, positive_blocks, id_blocks))
    return loss_blocks.reshape(QUERIES), inner_grad, outer_grad
```

```python
import functools

import jax
import jax.numpy as jnp
from jax import lax
from jax.experimental import pallas as pl
from jax.experimental.pallas import tpu as pltpu
from jax.sharding import Mesh, PartitionSpec as P

X, CORE, Z, Y = 4, 2, 8, 4
GRP, SHARD = X * CORE, Z * Y
PAIRS = SHARD // 2
CHUNKS = 4
VMEM = 50 * 1024 * 1024


def gelu_value(pre_act):
    return pre_act * 0.5 * (1.0 + lax.erf(pre_act * 0.7071067811865476))


def gelu_slope(pre_act):
    return (
        0.5 * (1.0 + lax.erf(pre_act * 0.7071067811865476))
        + pre_act * jnp.exp(-0.5 * pre_act * pre_act) * 0.3989422804014327
    )


def contract_first(left, right):
    return lax.dot_general(
        left, right, (((0,), (0,)), ((), ())), preferred_element_type=jnp.float32
    )


def contract_last(left, right):
    return lax.dot_general(
        left, right, (((1,), (1,)), ((), ())), preferred_element_type=jnp.float32
    )


def exchange(value, axes):
    return lax.all_to_all(value, axes, split_axis=0, concat_axis=0, tiled=True)


def spread(value, axes, count):
    return exchange(jnp.broadcast_to(value[None], (count, *value.shape)), axes)


def request_kernel(shift, ids_ref, rows_ref, even_ref, query_ref):
    ids = ids_ref[...]
    q_dev, neg = ids.shape
    lane = lax.broadcasted_iota(jnp.int32, (q_dev, q_dev), 1)
    query = lax.broadcasted_iota(jnp.int32, (q_dev, q_dev), 0)
    before = (lane < query).astype(jnp.float32).astype(jnp.bfloat16)
    kind, pair_lane = lane // PAIRS, lane % PAIRS
    seen = jnp.zeros((1, q_dev), jnp.float32)
    placed = jnp.zeros((q_dev, q_dev), jnp.float32)
    for k in range(neg):
        id_k = ids[:, k : k + 1]
        owner = id_k >> shift
        odd = owner & 1
        member = owner == lane
        ones = member.astype(jnp.float32)
        counts = seen + jnp.dot(before, ones.astype(jnp.bfloat16), preferred_element_type=jnp.float32)
        rank = jnp.sum(jnp.where(member, counts, 0.0), axis=1, keepdims=True).astype(jnp.int32)
        seen = seen + jnp.sum(ones, axis=0, keepdims=True)
        slot = jnp.where(odd == 1, q_dev - 1 - rank, rank)
        at_slot = (slot == lane).astype(jnp.float32).astype(jnp.bfloat16)
        code = (odd << shift) + (id_k - (owner << shift))
        item = jnp.where(
            kind == 0, code >> 6, jnp.where(kind == 1, code & 63, jnp.where(kind == 2, query, 0))
        )
        item = jnp.where((owner >> 1) == pair_lane, item, 0)
        placed = placed + contract_first(item.astype(jnp.float32).astype(jnp.bfloat16), at_slot)
    code = (placed[:PAIRS] * 64.0 + placed[PAIRS : 2 * PAIRS]).astype(jnp.int32)
    rows_ref[...] = code & ((1 << shift) - 1)
    even_ref[...] = 1 - (code >> shift)
    query_ref[...] = placed[2 * PAIRS : 3 * PAIRS].astype(jnp.int32)


def score_kernel(scale, embedded_ref, positives_ref, hidden_ref, query_ref, *refs):
    row_refs, (loss_ref, grad_ref, outer_ref) = refs[:CHUNKS], refs[CHUNKS:]
    embedded = embedded_ref[...]
    positives = positives_ref[...].astype(jnp.float32)
    q_dev, width = embedded.shape
    pos_scores = (
        jnp.sum(embedded.astype(jnp.float32) * positives, axis=1, keepdims=True) * scale
    )
    total = jnp.exp(pos_scores)
    per = row_refs[0].shape[0]
    query = lax.broadcasted_iota(jnp.int32, (q_dev, per), 0)
    scores, members = [], []
    for c in range(CHUNKS):
        score = contract_last(embedded, row_refs[c][...]) * scale
        member = query_ref[:, c * per : (c + 1) * per] == query
        total = total + jnp.sum(jnp.where(member, jnp.exp(score), 0.0), axis=1, keepdims=True)
        scores.append(score)
        members.append(member)
    log_total = jnp.log(total)
    loss_ref[...] = log_total - pos_scores
    grad = (jnp.exp(pos_scores - log_total) - 1.0) * positives
    for c in range(CHUNKS):
        weight = jnp.where(members[c], jnp.exp(scores[c] - log_total), 0.0)
        high = weight.astype(jnp.bfloat16)
        low = (weight - high.astype(jnp.float32)).astype(jnp.bfloat16)
        rows = row_refs[c][...]
        grad = grad + jnp.dot(high, rows, preferred_element_type=jnp.float32)
        grad = grad + jnp.dot(low, rows, preferred_element_type=jnp.float32)
    query_grad = (grad * scale).astype(jnp.bfloat16)
    grad_ref[...] = query_grad
    hid = hidden_ref.shape[1]
    deep, part, half = hid // SHARD // X, hid // Z, width // CORE
    for z in range(Z):
        outer = contract_first(hidden_ref[:, z * part : (z + 1) * part], query_grad).astype(
            jnp.bfloat16
        )
        for y in range(Y):
            for x in range(X):
                rows = outer[(y * X + x) * deep : (y * X + x + 1) * deep]
                at = (x * Z + z) * deep
                for core in range(CORE):
                    outer_ref[core, y, at : at + deep, :] = rows[:, core * half : (core + 1) * half]


def inner_kernel(queries_ref, grad_ref, slope_ref, weight_ref, inner_ref):
    queries, query_grad = queries_ref[...], grad_ref[...]
    part = weight_ref.shape[0] // GRP
    for x in range(X):
        for core in range(CORE):
            at = (x * CORE + core) * part
            hidden_grad = contract_last(query_grad, weight_ref[at : at + part, :])
            pre_grad = (hidden_grad * slope_ref[:, at : at + part]).astype(jnp.bfloat16)
            inner_ref[core, x] = contract_first(queries, pre_grad).astype(jnp.bfloat16)


def total_of(parts, dtype=jnp.bfloat16):
    return jnp.sum(parts.astype(jnp.float32), axis=0).astype(dtype)


def shards(queries, positives, negative_ids, passage_table, inner_weight, outer_weight):
    q_dev, width = queries.shape
    rows_dev = passage_table.shape[0]
    hid = inner_weight.shape[1]
    inner_rows, outer_rows = inner_weight.shape[0], outer_weight.shape[0]
    scale = float(width) ** (-0.5)
    call = functools.partial(
        pl.pallas_call, compiler_params=pltpu.CompilerParams(vmem_limit_bytes=VMEM)
    )
    group = lax.axis_index("x") * CORE + lax.axis_index("core")

    slots = jax.ShapeDtypeStruct((PAIRS, q_dev), jnp.int32)
    wanted, even, slot_query = call(
        functools.partial(request_kernel, rows_dev.bit_length() - 1), out_shape=[slots] * 3
    )(negative_ids)
    requests = exchange(
        jnp.broadcast_to(wanted[:, None], (PAIRS, 2, q_dev)).reshape(SHARD, q_dev), ("z", "y")
    )
    requests = requests.reshape(Z, Y, q_dev).transpose(1, 0, 2)
    even = exchange(even, "z").reshape(Z, 2, q_dev).transpose(1, 0, 2)

    per = q_dev // CHUNKS
    chunks = []
    for c in range(CHUNKS):
        ids = requests[:, :, c * per : (c + 1) * per].reshape(-1)
        found = passage_table.at[ids].get(mode="promise_in_bounds")
        near = exchange(found, "y").reshape(2, 2, Z, per, width)
        merged = jnp.where(
            even[:, :, c * per : (c + 1) * per, None] == 1, near[:, 0], near[:, 1]
        )
        merged = merged.transpose(1, 0, 2, 3).reshape(-1, width)
        chunks.append(exchange(merged, "z"))
    slot_query = jnp.concatenate(
        [slot_query[:, c * per : (c + 1) * per].reshape(1, -1) for c in range(CHUNKS)], axis=1
    )

    wide = hid // GRP
    inner_piece = lax.dynamic_slice(inner_weight, (0, group * wide), (inner_rows, wide))
    blocks = width // wide
    deep = outer_rows * blocks // GRP
    outer_piece = lax.dynamic_slice(
        outer_weight.reshape(outer_rows, blocks, wide).transpose(1, 0, 2).reshape(-1, wide),
        (group * deep, 0),
        (deep, wide),
    )
    piece = jnp.concatenate([inner_piece, outer_piece], axis=0)
    gathered = spread(piece, ("z", "y"), SHARD)
    gathered = spread(gathered, "x", X)
    gathered = spread(gathered, "core", CORE).reshape(CORE, X, SHARD, inner_rows + deep, wide)
    inner_full = gathered[:, :, :, :inner_rows].transpose(2, 3, 1, 0, 4).reshape(-1, hid)
    outer_full = (
        gathered[:, :, :, inner_rows:]
        .transpose(2, 1, 0, 3, 4)
        .reshape(SHARD, blocks, outer_rows, wide)
        .transpose(0, 2, 1, 3)
        .reshape(hid, width)
    )

    pre_act = jnp.dot(queries, inner_full, preferred_element_type=jnp.float32)
    hidden = gelu_value(pre_act).astype(jnp.bfloat16)
    slope = gelu_slope(pre_act)
    projected = jnp.dot(hidden, outer_full, preferred_element_type=jnp.float32)
    embedded = (queries.astype(jnp.float32) + projected).astype(jnp.bfloat16)

    losses, query_grad, outer = call(
        functools.partial(score_kernel, scale),
        out_shape=[
            jax.ShapeDtypeStruct((q_dev, 1), jnp.float32),
            jax.ShapeDtypeStruct((q_dev, width), jnp.bfloat16),
            jax.ShapeDtypeStruct((CORE, Y, hid // Y, width // CORE), jnp.bfloat16),
        ],
    )(embedded, positives, hidden, slot_query, *chunks)
    inner = call(
        inner_kernel,
        out_shape=jax.ShapeDtypeStruct((CORE, X, width, wide), jnp.bfloat16),
    )(queries, query_grad, slope, outer_full)

    outer = total_of(exchange(outer, "core"))
    inner = total_of(exchange(inner, "core"))
    outer = total_of(exchange(outer, "y")).reshape(X, -1, width // CORE)
    inner = total_of(exchange(inner, "x"))
    outer = total_of(exchange(outer, "x")).reshape(Z, -1, width // CORE)
    inner = exchange(inner.reshape(SHARD, inner_rows, wide), ("z", "y"))
    outer = total_of(exchange(outer, "z"), jnp.float32)
    inner = total_of(inner, jnp.float32)
    outer = spread(outer, ("x", "core"), GRP)
    inner = spread(inner, ("x", "core"), GRP)
    outer = (
        outer.reshape(X, CORE, -1, width // CORE).transpose(0, 2, 1, 3).reshape(outer_rows, width)
    )
    inner = inner.transpose(1, 0, 2).reshape(inner_rows, hid)
    return (losses.reshape(-1), inner, outer)


def solution(mesh):
    fine = Mesh(mesh.devices.reshape(X, CORE, Z, Y), ("x", "core", "z", "y"))
    blocks, rows = ("x", "core", "z", "y"), ("z", "y")
    return jax.shard_map(
        shards,
        mesh=fine,
        in_specs=(
            P(blocks, None),
            P(blocks, None),
            P(blocks, None),
            P(rows, None),
            P(rows, None),
            P(rows, None),
        ),
        out_specs=(P(blocks), P(rows, None), P(rows, None)),
        check_vma=False,
    )
```

```python
import functools

import jax
import jax.numpy as jnp
from jax import lax
from jax.experimental import pallas as pl
from jax.experimental.pallas import tpu as pltpu
from jax.sharding import Mesh, PartitionSpec as P

X, CORE, Z, Y = 4, 2, 8, 4
GRP, SHARD = X * CORE, Z * Y
PAIRS = SHARD // 2
CHUNKS = 4
VMEM = 50 * 1024 * 1024


def gelu_value(pre_act):
    return pre_act * 0.5 * (1.0 + lax.erf(pre_act * 0.7071067811865476))


def gelu_slope(pre_act):
    return (
        0.5 * (1.0 + lax.erf(pre_act * 0.7071067811865476))
        + pre_act * jnp.exp(-0.5 * pre_act * pre_act) * 0.3989422804014327
    )


def contract_first(left, right):
    return lax.dot_general(
        left, right, (((0,), (0,)), ((), ())), preferred_element_type=jnp.float32
    )


def contract_last(left, right):
    return lax.dot_general(
        left, right, (((1,), (1,)), ((), ())), preferred_element_type=jnp.float32
    )


def exchange(value, axes):
    return lax.all_to_all(value, axes, split_axis=0, concat_axis=0, tiled=True)


def spread(value, axes, count):
    return exchange(jnp.broadcast_to(value[None], (count, *value.shape)), axes)


def ahead(value, axis, size, by):
    return lax.ppermute(value, axis, [(i, (i + by) % size) for i in range(size)])


def request_kernel(shift, ids_ref, code_ref, query_ref):
    ids = ids_ref[...]
    q_dev, neg = ids.shape
    lane = lax.broadcasted_iota(jnp.int32, (q_dev, q_dev), 1)
    query = lax.broadcasted_iota(jnp.int32, (q_dev, q_dev), 0)
    before = (lane < query).astype(jnp.float32).astype(jnp.bfloat16)
    kind, pair_lane = lane // PAIRS, lane % PAIRS
    seen = jnp.zeros((1, q_dev), jnp.float32)
    placed = jnp.zeros((q_dev, q_dev), jnp.float32)
    for k in range(neg):
        id_k = ids[:, k : k + 1]
        owner = id_k >> shift
        odd = owner & 1
        member = owner == lane
        ones = member.astype(jnp.float32)
        counts = seen + jnp.dot(before, ones.astype(jnp.bfloat16), preferred_element_type=jnp.float32)
        rank = jnp.sum(jnp.where(member, counts, 0.0), axis=1, keepdims=True).astype(jnp.int32)
        seen = seen + jnp.sum(ones, axis=0, keepdims=True)
        slot = jnp.where(odd == 1, q_dev - 1 - rank, rank)
        at_slot = (slot == lane).astype(jnp.float32).astype(jnp.bfloat16)
        code = (odd << shift) + (id_k - (owner << shift))
        item = jnp.where(
            kind == 0, code >> 6, jnp.where(kind == 1, code & 63, jnp.where(kind == 2, query, 0))
        )
        item = jnp.where((owner >> 1) == pair_lane, item, 0)
        placed = placed + contract_first(item.astype(jnp.float32).astype(jnp.bfloat16), at_slot)
    code_ref[...] = (placed[:PAIRS] * 64.0 + placed[PAIRS : 2 * PAIRS]).astype(jnp.int32)
    query_ref[...] = placed[2 * PAIRS : 3 * PAIRS].astype(jnp.int32)


def score_kernel(scale, place_ref, embedded_ref, positives_ref, hidden_ref, query_ref, *refs):
    row_refs, (loss_ref, grad_ref, keep_ref, send_ref) = refs[:CHUNKS], refs[CHUNKS:]
    embedded = embedded_ref[...]
    positives = positives_ref[...].astype(jnp.float32)
    q_dev, width = embedded.shape
    pos_scores = (
        jnp.sum(embedded.astype(jnp.float32) * positives, axis=1, keepdims=True) * scale
    )
    total = jnp.exp(pos_scores)
    per = row_refs[0].shape[0]
    query = lax.broadcasted_iota(jnp.int32, (q_dev, per), 0)
    scores, members = [], []
    for c in range(CHUNKS):
        score = contract_last(embedded, row_refs[c][...]) * scale
        member = query_ref[:, c * per : (c + 1) * per] == query
        total = total + jnp.sum(jnp.where(member, jnp.exp(score), 0.0), axis=1, keepdims=True)
        scores.append(score)
        members.append(member)
    log_total = jnp.log(total)
    loss_ref[...] = log_total - pos_scores
    grad = (jnp.exp(pos_scores - log_total) - 1.0) * positives
    for c in range(CHUNKS):
        weight = jnp.where(members[c], jnp.exp(scores[c] - log_total), 0.0)
        high = weight.astype(jnp.bfloat16)
        low = (weight - high.astype(jnp.float32)).astype(jnp.bfloat16)
        rows = row_refs[c][...]
        grad = grad + jnp.dot(high, rows, preferred_element_type=jnp.float32)
        grad = grad + jnp.dot(low, rows, preferred_element_type=jnp.float32)
    query_grad = (grad * scale).astype(jnp.bfloat16)
    grad_ref[...] = query_grad
    my_x, my_core, my_y = place_ref[0], place_ref[1], place_ref[2]
    hid = hidden_ref.shape[1]
    deep, part, half = hid // SHARD // X, hid // Z, width // CORE
    for z in range(Z):
        outer = contract_first(hidden_ref[:, z * part : (z + 1) * part], query_grad)
        left, right = outer[:, :half], outer[:, half:]
        keep = jnp.where(my_core == 0, left, right).astype(jnp.bfloat16)
        send = jnp.where(my_core == 0, right, left).astype(jnp.bfloat16)
        for y in range(Y):
            for x in range(X):
                rows = slice((y * X + x) * deep, (y * X + x + 1) * deep)
                to_y, to_x = (y - my_y) & (Y - 1), (x - my_x) & (X - 1)
                keep_ref[to_y, to_x, z * deep : (z + 1) * deep, :] = keep[rows]
                send_ref[to_y, to_x, z * deep : (z + 1) * deep, :] = send[rows]


def inner_kernel(place_ref, queries_ref, grad_ref, slope_ref, weight_ref, keep_ref, send_ref):
    queries, query_grad = queries_ref[...], grad_ref[...]
    part = weight_ref.shape[0] // GRP
    for by_core, out_ref in ((1, send_ref), (0, keep_ref)):
        for by_x in range(X):
            group = ((place_ref[0] + by_x) & (X - 1)) * CORE + (place_ref[1] ^ by_core)
            at = pl.ds(pl.multiple_of(group * part, part), part)
            hidden_grad = contract_last(query_grad, weight_ref[at, :])
            pre_grad = (hidden_grad * slope_ref[:, at]).astype(jnp.bfloat16)
            out_ref[by_x] = contract_first(queries, pre_grad).astype(jnp.bfloat16)


def total_of(parts):
    return sum(part.astype(jnp.float32) for part in parts)


def columns_to_rows(value, wide):
    return jnp.concatenate(
        [value[..., i : i + wide] for i in range(0, value.shape[-1], wide)], axis=-2
    )


def rows_to_columns(value, deep):
    return jnp.concatenate(
        [value[..., i : i + deep, :] for i in range(0, value.shape[-2], deep)], axis=-1
    )


def shards(queries, positives, negative_ids, passage_table, inner_weight, outer_weight):
    q_dev, width = queries.shape
    rows_dev = passage_table.shape[0]
    shift = rows_dev.bit_length() - 1
    hid = inner_weight.shape[1]
    inner_rows, outer_rows = inner_weight.shape[0], outer_weight.shape[0]
    scale = float(width) ** (-0.5)
    limits = {"compiler_params": pltpu.CompilerParams(vmem_limit_bytes=VMEM)}
    my_x, my_core, my_y = (lax.axis_index(axis) for axis in ("x", "core", "y"))
    group = my_x * CORE + my_core
    place = jnp.stack([my_x, my_core, my_y]).astype(jnp.int32)
    in_smem = pl.BlockSpec(memory_space=pltpu.SMEM)
    in_vmem = pl.BlockSpec(memory_space=pltpu.VMEM)

    slots = jax.ShapeDtypeStruct((PAIRS, q_dev), jnp.int32)
    code, slot_query = pl.pallas_call(
        functools.partial(request_kernel, shift), out_shape=[slots] * 2, **limits
    )(negative_ids)
    code = exchange(code.reshape(Z, 2, q_dev), "z")
    codes = [code] + [ahead(code, "y", Y, by) for by in range(1, Y)]
    codes = jnp.stack([lax.dynamic_index_in_dim(one, my_y // 2, 1, False) for one in codes])
    wanted = codes & (rows_dev - 1)
    owners = [(my_y + by) % Y for by in range(Y)]
    mine = [
        (lax.dynamic_index_in_dim(code, owner // 2, 1, False) >> shift) == owner % 2
        for owner in owners[::2]
    ]

    per = q_dev // CHUNKS
    odd = my_y % 2 == 1
    chunks = []
    for c in range(CHUNKS):
        cut = slice(c * per, (c + 1) * per)
        found = passage_table.at[wanted[:, :, cut].reshape(-1)].get(mode="promise_in_bounds")
        found = found.reshape(Y, Z, per, width)
        near = [found[0]] + [ahead(found[by], "y", Y, -by) for by in range(1, Y)]
        partner = jnp.where(odd, near[3], near[1])
        other = jnp.where(odd, near[1], near[3])
        merged = jnp.stack(
            [
                jnp.where(mine[0][:, cut, None], near[0], partner),
                jnp.where(mine[1][:, cut, None], near[2], other),
            ],
            axis=1,
        )
        chunks.append(exchange(merged, "z").reshape(-1, width))
    slot_query = slot_query.reshape(Z, 2, q_dev)
    slot_query = jnp.where(my_y // 2 == 0, slot_query, slot_query[:, ::-1])
    slot_query = jnp.concatenate(
        [slot_query[:, :, c * per : (c + 1) * per].reshape(1, -1) for c in range(CHUNKS)], axis=1
    )

    wide, deep = hid // GRP, outer_rows // GRP
    inner_piece = lax.dynamic_slice(inner_weight, (0, group * wide), (inner_rows, wide))
    outer_piece = lax.dynamic_slice(outer_weight, (group * deep, 0), (deep, width))
    piece = jnp.concatenate([rows_to_columns(inner_piece, deep), outer_piece], axis=0)
    gathered = spread(piece, ("z", "y"), SHARD)
    gathered = lax.all_gather(gathered, "x")
    twin = ahead(gathered, "core", CORE, 1)
    halves = [jnp.where(my_core == 0, gathered, twin), jnp.where(my_core == 0, twin, gathered)]
    inner_full = [
        columns_to_rows(halves[g % CORE][g // CORE, :, :deep], wide).reshape(width, wide)
        for g in range(GRP)
    ]
    outer_full = jnp.stack(
        [halves[g % CORE][g // CORE, :, deep:] for g in range(GRP)], axis=1
    ).reshape(hid, width)

    pre_act = jnp.concatenate(
        [jnp.dot(queries, part, preferred_element_type=jnp.float32) for part in inner_full], axis=1
    )
    hidden = gelu_value(pre_act).astype(jnp.bfloat16)
    slope = gelu_slope(pre_act)
    projected = jnp.dot(hidden, outer_full, preferred_element_type=jnp.float32)
    embedded = (queries.astype(jnp.float32) + projected).astype(jnp.bfloat16)

    half = width // CORE
    outer_cut = jax.ShapeDtypeStruct((Y, X, hid // Y // X, half), jnp.bfloat16)
    losses, query_grad, outer, outer_sent = pl.pallas_call(
        functools.partial(score_kernel, scale),
        out_shape=[
            jax.ShapeDtypeStruct((q_dev, 1), jnp.float32),
            jax.ShapeDtypeStruct((q_dev, width), jnp.bfloat16),
            outer_cut,
            outer_cut,
        ],
        in_specs=[in_smem] + [in_vmem] * (4 + CHUNKS),
        **limits,
    )(place, embedded, positives, hidden, slot_query, *chunks)
    outer_sent = ahead(outer_sent, "core", CORE, 1)
    inner, inner_sent = pl.pallas_call(
        inner_kernel,
        out_shape=[jax.ShapeDtypeStruct((X, width, wide), jnp.bfloat16)] * 2,
        in_specs=[in_smem] + [in_vmem] * 4,
        **limits,
    )(place, queries, query_grad, slope, outer_full)
    inner_sent = ahead(inner_sent, "core", CORE, 1)

    narrow = lambda value: value.astype(jnp.bfloat16)
    outer = [narrow(total_of([outer[by], outer_sent[by]])) for by in range(Y)]
    outer = outer[:1] + [ahead(outer[by], "y", Y, by) for by in range(1, Y)]
    inner = [narrow(total_of([inner[by], inner_sent[by]])) for by in range(X)]
    inner = inner[:1] + [ahead(inner[by], "x", X, by) for by in range(1, X)]
    outer = [narrow(total_of([part[by] for part in outer])) for by in range(X)]
    outer = outer[:1] + [ahead(outer[by], "x", X, by) for by in range(1, X)]
    inner = narrow(total_of(inner)).reshape(Z, Y, inner_rows, wide).transpose(1, 0, 2, 3)
    inner = exchange(inner, "y")
    lanes = 128
    both = jnp.concatenate(
        [
            columns_to_rows(total_of(list(inner)), lanes),
            columns_to_rows(total_of(outer).reshape(Z, -1, half), lanes),
        ],
        axis=1,
    )
    both = total_of(list(exchange(narrow(both), "z")))
    both = spread(both, ("x", "core"), GRP)
    inner_deep = inner_rows * wide // lanes
    inner = rows_to_columns(both[:, :inner_deep], inner_rows)
    outer = rows_to_columns(both[:, inner_deep:], outer_rows // X)
    inner = jnp.concatenate(list(inner), axis=1)
    outer = jnp.concatenate(
        [jnp.concatenate([outer[x * CORE + c] for c in range(CORE)], axis=1) for x in range(X)],
        axis=0,
    )
    return (losses.reshape(-1), inner, outer)


def solution(mesh):
    fine = Mesh(mesh.devices.reshape(X, CORE, Z, Y), ("x", "core", "z", "y"))
    blocks, rows = ("x", "core", "z", "y"), ("z", "y")
    return jax.shard_map(
        shards,
        mesh=fine,
        in_specs=(
            P(blocks, None),
            P(blocks, None),
            P(blocks, None),
            P(rows, None),
            P(rows, None),
            P(rows, None),
        ),
        out_specs=(P(blocks), P(rows, None), P(rows, None)),
        check_vma=False,
    )
```

```python
import functools

import jax
import jax.numpy as jnp
from jax import lax
from jax.experimental import pallas as pl
from jax.experimental.pallas import tpu as pltpu
from jax.sharding import Mesh, PartitionSpec as P

X, CORE, Z, Y = 4, 2, 8, 4
GRP, SHARD = X * CORE, Z * Y
PAIRS = SHARD // 2
CHUNKS, AHEAD = 4, 2
VMEM = 50 * 1024 * 1024


def gelu_value(pre_act):
    return pre_act * 0.5 * (1.0 + lax.erf(pre_act * 0.7071067811865476))


def gelu_slope(pre_act):
    return (
        0.5 * (1.0 + lax.erf(pre_act * 0.7071067811865476))
        + pre_act * jnp.exp(-0.5 * pre_act * pre_act) * 0.3989422804014327
    )


def contract_first(left, right):
    return lax.dot_general(
        left, right, (((0,), (0,)), ((), ())), preferred_element_type=jnp.float32
    )


def contract_last(left, right):
    return lax.dot_general(
        left, right, (((1,), (1,)), ((), ())), preferred_element_type=jnp.float32
    )


def exchange(value, axes):
    return lax.all_to_all(value, axes, split_axis=0, concat_axis=0, tiled=True)


def spread(value, axes, count):
    return exchange(jnp.broadcast_to(value[None], (count, *value.shape)), axes)


def ahead(value, axis, size, by):
    return lax.ppermute(value, axis, [(i, (i + by) % size) for i in range(size)])


def after(value, *done):
    return lax.optimization_barrier((value, *done))[0]


def request_kernel(shift, ids_ref, code_ref, query_ref):
    ids = ids_ref[...]
    q_dev, neg = ids.shape
    lane = lax.broadcasted_iota(jnp.int32, (q_dev, q_dev), 1)
    query = lax.broadcasted_iota(jnp.int32, (q_dev, q_dev), 0)
    before = (lane < query).astype(jnp.float32).astype(jnp.bfloat16)
    kind, pair_lane = lane // PAIRS, lane % PAIRS
    seen = jnp.zeros((1, q_dev), jnp.float32)
    placed = jnp.zeros((q_dev, q_dev), jnp.float32)
    for k in range(neg):
        id_k = ids[:, k : k + 1]
        owner = id_k >> shift
        odd = owner & 1
        member = owner == lane
        ones = member.astype(jnp.float32)
        counts = seen + jnp.dot(before, ones.astype(jnp.bfloat16), preferred_element_type=jnp.float32)
        rank = jnp.sum(jnp.where(member, counts, 0.0), axis=1, keepdims=True).astype(jnp.int32)
        seen = seen + jnp.sum(ones, axis=0, keepdims=True)
        slot = jnp.where(odd == 1, q_dev - 1 - rank, rank)
        at_slot = (slot == lane).astype(jnp.float32).astype(jnp.bfloat16)
        code = (odd << shift) + (id_k - (owner << shift))
        item = jnp.where(
            kind == 0, code >> 6, jnp.where(kind == 1, code & 63, jnp.where(kind == 2, query, 0))
        )
        item = jnp.where((owner >> 1) == pair_lane, item, 0)
        placed = placed + contract_first(item.astype(jnp.float32).astype(jnp.bfloat16), at_slot)
    code_ref[...] = (placed[:PAIRS] * 64.0 + placed[PAIRS : 2 * PAIRS]).astype(jnp.int32)
    query_ref[...] = placed[2 * PAIRS : 3 * PAIRS].astype(jnp.int32)


def score_kernel(scale, place_ref, embedded_ref, positives_ref, hidden_ref, query_ref, *refs):
    row_refs, (loss_ref, grad_ref, keep_ref, send_ref) = refs[:CHUNKS], refs[CHUNKS:]
    embedded = embedded_ref[...]
    positives = positives_ref[...].astype(jnp.float32)
    q_dev, width = embedded.shape
    pos_scores = (
        jnp.sum(embedded.astype(jnp.float32) * positives, axis=1, keepdims=True) * scale
    )
    total = jnp.exp(pos_scores)
    per = row_refs[0].shape[0]
    query = lax.broadcasted_iota(jnp.int32, (q_dev, per), 0)
    scores, members = [], []
    for c in range(CHUNKS):
        score = contract_last(embedded, row_refs[c][...]) * scale
        member = query_ref[:, c * per : (c + 1) * per] == query
        total = total + jnp.sum(jnp.where(member, jnp.exp(score), 0.0), axis=1, keepdims=True)
        scores.append(score)
        members.append(member)
    log_total = jnp.log(total)
    loss_ref[...] = log_total - pos_scores
    grad = (jnp.exp(pos_scores - log_total) - 1.0) * positives
    for c in range(CHUNKS):
        weight = jnp.where(members[c], jnp.exp(scores[c] - log_total), 0.0)
        high = weight.astype(jnp.bfloat16)
        low = (weight - high.astype(jnp.float32)).astype(jnp.bfloat16)
        rows = row_refs[c][...]
        grad = grad + jnp.dot(high, rows, preferred_element_type=jnp.float32)
        grad = grad + jnp.dot(low, rows, preferred_element_type=jnp.float32)
    query_grad = (grad * scale).astype(jnp.bfloat16)
    grad_ref[...] = query_grad
    my_x, my_core, my_y = place_ref[0], place_ref[1], place_ref[2]
    hid = hidden_ref.shape[1]
    deep, part, half = hid // SHARD // X, hid // Z, width // CORE
    for z in range(Z):
        outer = contract_first(hidden_ref[:, z * part : (z + 1) * part], query_grad)
        left, right = outer[:, :half], outer[:, half:]
        keep = jnp.where(my_core == 0, left, right).astype(jnp.bfloat16)
        send = jnp.where(my_core == 0, right, left).astype(jnp.bfloat16)
        for y in range(Y):
            for x in range(X):
                rows = slice((y * X + x) * deep, (y * X + x + 1) * deep)
                to_y, to_x = (y - my_y) & (Y - 1), (x - my_x) & (X - 1)
                keep_ref[to_y, to_x, z * deep : (z + 1) * deep, :] = keep[rows]
                send_ref[to_y, to_x, z * deep : (z + 1) * deep, :] = send[rows]


def inner_kernel(place_ref, queries_ref, grad_ref, slope_ref, weight_ref, keep_ref, send_ref):
    queries, query_grad = queries_ref[...], grad_ref[...]
    part = weight_ref.shape[0] // GRP
    for by_core, out_ref in ((1, send_ref), (0, keep_ref)):
        for by_x in range(X):
            group = by_x * CORE + (place_ref[1] ^ by_core)
            at = pl.ds(pl.multiple_of(group * part, part), part)
            hidden_grad = contract_last(query_grad, weight_ref[at, :])
            pre_grad = (hidden_grad * slope_ref[:, at]).astype(jnp.bfloat16)
            out_ref[by_x] = contract_first(queries, pre_grad).astype(jnp.bfloat16)


def total_of(parts):
    return sum(part.astype(jnp.float32) for part in parts)


def columns_to_rows(value, wide):
    return jnp.concatenate(
        [value[..., i : i + wide] for i in range(0, value.shape[-1], wide)], axis=-2
    )


def rows_to_columns(value, deep):
    return jnp.concatenate(
        [value[..., i : i + deep, :] for i in range(0, value.shape[-2], deep)], axis=-1
    )


def shards(queries, positives, negative_ids, passage_table, inner_weight, outer_weight):
    q_dev, width = queries.shape
    rows_dev = passage_table.shape[0]
    shift = rows_dev.bit_length() - 1
    hid = inner_weight.shape[1]
    inner_rows, outer_rows = inner_weight.shape[0], outer_weight.shape[0]
    scale = float(width) ** (-0.5)
    limits = {"compiler_params": pltpu.CompilerParams(vmem_limit_bytes=VMEM)}
    my_x, my_core, my_y = (lax.axis_index(axis) for axis in ("x", "core", "y"))
    group = my_x * CORE + my_core
    place = jnp.stack([my_x, my_core, my_y]).astype(jnp.int32)
    in_smem = pl.BlockSpec(memory_space=pltpu.SMEM)
    in_vmem = pl.BlockSpec(memory_space=pltpu.VMEM)

    slots = jax.ShapeDtypeStruct((PAIRS, q_dev), jnp.int32)
    code, slot_query = pl.pallas_call(
        functools.partial(request_kernel, shift), out_shape=[slots] * 2, **limits
    )(negative_ids)
    code = exchange(code.reshape(Z, 2, q_dev), "z")
    inner_weight, outer_weight = after((inner_weight, outer_weight), code)
    codes = [code] + [ahead(code, "y", Y, by) for by in range(1, Y)]
    codes = jnp.stack([lax.dynamic_index_in_dim(one, my_y // 2, 1, False) for one in codes])
    wanted = codes & (rows_dev - 1)
    owners = [(my_y + by) % Y for by in range(Y)]
    mine = [
        (lax.dynamic_index_in_dim(code, owner // 2, 1, False) >> shift) == owner % 2
        for owner in owners[::2]
    ]

    per = q_dev // CHUNKS
    odd = my_y % 2 == 1
    chunks, ready = [], []
    for c in range(CHUNKS):
        cut = slice(c * per, (c + 1) * per)
        ids = wanted[:, :, cut].reshape(-1)
        if c >= AHEAD:
            ids = after(ids, ready[c - AHEAD])
        found = passage_table.at[ids].get(mode="promise_in_bounds")
        found = found.reshape(Y, Z, per, width)
        near = [found[0]] + [ahead(found[by], "y", Y, -by) for by in range(1, Y)]
        partner = jnp.where(odd, near[3], near[1])
        other = jnp.where(odd, near[1], near[3])
        merged = jnp.stack(
            [
                jnp.where(mine[0][:, cut, None], near[0], partner),
                jnp.where(mine[1][:, cut, None], near[2], other),
            ],
            axis=1,
        )
        ready.append(merged.reshape(-1, width))
        chunks.append(exchange(ready[c], "z"))
    slot_query = slot_query.reshape(Z, 2, q_dev)
    slot_query = jnp.where(my_y // 2 == 0, slot_query, slot_query[:, ::-1])
    slot_query = jnp.concatenate(
        [slot_query[:, :, c * per : (c + 1) * per].reshape(1, -1) for c in range(CHUNKS)], axis=1
    )

    wide, deep = hid // GRP, outer_rows // GRP
    inner_piece = lax.dynamic_slice(inner_weight, (0, group * wide), (inner_rows, wide))
    outer_piece = lax.dynamic_slice(outer_weight, (group * deep, 0), (deep, width))
    piece = jnp.concatenate([rows_to_columns(inner_piece, deep), outer_piece], axis=0)
    gathered = spread(piece, ("z", "y"), SHARD)
    parts = [gathered] + [ahead(gathered, "x", X, by) for by in range(1, X)]
    gathered = jnp.zeros((X, *gathered.shape), gathered.dtype)
    for by in range(X):
        gathered = lax.dynamic_update_index_in_dim(gathered, parts[by], (my_x - by) % X, 0)
    twin = ahead(gathered, "core", CORE, 1)
    halves = jnp.stack(
        [jnp.where(my_core == 0, gathered, twin), jnp.where(my_core == 0, twin, gathered)], axis=1
    )
    inner_full = [
        columns_to_rows(halves[g // CORE, g % CORE, :, :deep], wide).reshape(width, wide)
        for g in range(GRP)
    ]
    outer_full = halves[:, :, :, deep:].transpose(2, 0, 1, 3, 4).reshape(hid, width)

    pre_act = jnp.concatenate(
        [jnp.dot(queries, part, preferred_element_type=jnp.float32) for part in inner_full], axis=1
    )
    hidden = gelu_value(pre_act).astype(jnp.bfloat16)
    slope = gelu_slope(pre_act)
    projected = jnp.dot(hidden, outer_full, preferred_element_type=jnp.float32)
    embedded = (queries.astype(jnp.float32) + projected).astype(jnp.bfloat16)

    half = width // CORE
    outer_cut = jax.ShapeDtypeStruct((Y, X, hid // Y // X, half), jnp.bfloat16)
    losses, query_grad, outer, outer_sent = pl.pallas_call(
        functools.partial(score_kernel, scale),
        out_shape=[
            jax.ShapeDtypeStruct((q_dev, 1), jnp.float32),
            jax.ShapeDtypeStruct((q_dev, width), jnp.bfloat16),
            outer_cut,
            outer_cut,
        ],
        in_specs=[in_smem] + [in_vmem] * (4 + CHUNKS),
        **limits,
    )(place, embedded, positives, hidden, slot_query, *chunks)
    outer_sent = ahead(outer_sent, "core", CORE, 1)
    inner, inner_sent = pl.pallas_call(
        inner_kernel,
        out_shape=[jax.ShapeDtypeStruct((X, width, wide), jnp.bfloat16)] * 2,
        in_specs=[in_smem] + [in_vmem] * 4,
        **limits,
    )(place, queries, query_grad, slope, outer_full)
    inner_sent = ahead(inner_sent, "core", CORE, 1)

    narrow = lambda value: value.astype(jnp.bfloat16)
    outer = [narrow(total_of([outer[by], outer_sent[by]])) for by in range(Y)]
    outer = outer[:1] + [ahead(outer[by], "y", Y, by) for by in range(1, Y)]
    inner = exchange(narrow(total_of([inner, inner_sent])), "x")
    outer = [narrow(total_of([part[by] for part in outer])) for by in range(X)]
    outer = outer[:1] + [ahead(outer[by], "x", X, by) for by in range(1, X)]
    inner = narrow(total_of(list(inner))).reshape(Z, Y, inner_rows, wide).transpose(1, 0, 2, 3)
    inner = exchange(inner, "y")
    lanes = 128
    both = jnp.concatenate(
        [
            columns_to_rows(total_of(list(inner)), lanes),
            columns_to_rows(total_of(outer).reshape(Z, -1, half), lanes),
        ],
        axis=1,
    )
    both = total_of(list(exchange(narrow(both), "z")))
    both = spread(both, ("x", "core"), GRP)
    inner_deep = inner_rows * wide // lanes
    inner = rows_to_columns(both[:, :inner_deep], inner_rows)
    outer = rows_to_columns(both[:, inner_deep:], outer_rows // X)
    inner = jnp.concatenate(list(inner), axis=1)
    outer = jnp.concatenate(
        [jnp.concatenate([outer[x * CORE + c] for c in range(CORE)], axis=1) for x in range(X)],
        axis=0,
    )
    return (losses.reshape(-1), inner, outer)


def solution(mesh):
    fine = Mesh(mesh.devices.reshape(X, CORE, Z, Y), ("x", "core", "z", "y"))
    blocks, rows = ("x", "core", "z", "y"), ("z", "y")
    return jax.shard_map(
        shards,
        mesh=fine,
        in_specs=(
            P(blocks, None),
            P(blocks, None),
            P(blocks, None),
            P(rows, None),
            P(rows, None),
            P(rows, None),
        ),
        out_specs=(P(blocks), P(rows, None), P(rows, None)),
        check_vma=False,
    )
```

```python
import functools

import jax
import jax.numpy as jnp
from jax import lax
from jax.experimental import pallas as pl
from jax.experimental.pallas import tpu as pltpu
from jax.sharding import Mesh, PartitionSpec as P

X, CORE, Z, Y = 4, 2, 8, 4
GRP, SHARD = X * CORE, Z * Y
PAIRS = SHARD // 2
CHUNKS = 4
VMEM = 50 * 1024 * 1024


def gelu_value(pre_act):
    return pre_act * 0.5 * (1.0 + lax.erf(pre_act * 0.7071067811865476))


def gelu_slope(pre_act):
    return (
        0.5 * (1.0 + lax.erf(pre_act * 0.7071067811865476))
        + pre_act * jnp.exp(-0.5 * pre_act * pre_act) * 0.3989422804014327
    )


def contract_first(left, right):
    return lax.dot_general(
        left, right, (((0,), (0,)), ((), ())), preferred_element_type=jnp.float32
    )


def contract_last(left, right):
    return lax.dot_general(
        left, right, (((1,), (1,)), ((), ())), preferred_element_type=jnp.float32
    )


def exchange(value, axes):
    return lax.all_to_all(value, axes, split_axis=0, concat_axis=0, tiled=True)


def spread(value, axes, count):
    return exchange(jnp.broadcast_to(value[None], (count, *value.shape)), axes)


def ahead(value, axis, size, by):
    return lax.ppermute(value, axis, [(i, (i + by) % size) for i in range(size)])


def after(value, *done):
    return lax.optimization_barrier((value, *done))[0]


def request_kernel(shift, ids_ref, code_ref, query_ref):
    ids = ids_ref[...]
    q_dev, neg = ids.shape
    lane = lax.broadcasted_iota(jnp.int32, (q_dev, q_dev), 1)
    query = lax.broadcasted_iota(jnp.int32, (q_dev, q_dev), 0)
    before = (lane < query).astype(jnp.float32).astype(jnp.bfloat16)
    kind, pair_lane = lane // PAIRS, lane % PAIRS
    seen = jnp.zeros((1, q_dev), jnp.float32)
    placed = jnp.zeros((q_dev, q_dev), jnp.float32)
    for k in range(neg):
        id_k = ids[:, k : k + 1]
        owner = id_k >> shift
        odd = owner & 1
        member = owner == lane
        ones = member.astype(jnp.float32)
        counts = seen + jnp.dot(before, ones.astype(jnp.bfloat16), preferred_element_type=jnp.float32)
        rank = jnp.sum(jnp.where(member, counts, 0.0), axis=1, keepdims=True).astype(jnp.int32)
        seen = seen + jnp.sum(ones, axis=0, keepdims=True)
        slot = jnp.where(odd == 1, q_dev - 1 - rank, rank)
        at_slot = (slot == lane).astype(jnp.float32).astype(jnp.bfloat16)
        code = (odd << shift) + (id_k - (owner << shift))
        item = jnp.where(
            kind == 0, code >> 6, jnp.where(kind == 1, code & 63, jnp.where(kind == 2, query, 0))
        )
        item = jnp.where((owner >> 1) == pair_lane, item, 0)
        placed = placed + contract_first(item.astype(jnp.float32).astype(jnp.bfloat16), at_slot)
    code_ref[...] = (placed[:PAIRS] * 64.0 + placed[PAIRS : 2 * PAIRS]).astype(jnp.int32)
    query_ref[...] = placed[2 * PAIRS : 3 * PAIRS].astype(jnp.int32)


def merge_kernel(odd_ref, own_ref, next_ref, far_ref, last_ref, out_ref):
    odd = odd_ref[0] == 1
    follow, behind = next_ref[...], last_ref[...]
    out_ref[:, 0] = own_ref[...] + jnp.where(odd, behind, follow)
    out_ref[:, 1] = far_ref[...] + jnp.where(odd, follow, behind)


def score_kernel(scale, place_ref, embedded_ref, positives_ref, hidden_ref, query_ref, *refs):
    row_refs, (loss_ref, grad_ref, keep_ref, send_ref) = refs[:CHUNKS], refs[CHUNKS:]
    embedded = embedded_ref[...]
    positives = positives_ref[...].astype(jnp.float32)
    q_dev, width = embedded.shape
    pos_scores = (
        jnp.sum(embedded.astype(jnp.float32) * positives, axis=1, keepdims=True) * scale
    )
    total = jnp.exp(pos_scores)
    per = row_refs[0].shape[0]
    query = lax.broadcasted_iota(jnp.int32, (q_dev, per), 0)
    scores, members = [], []
    for c in range(CHUNKS):
        score = contract_last(embedded, row_refs[c][...]) * scale
        member = query_ref[:, c * per : (c + 1) * per] == query
        total = total + jnp.sum(jnp.where(member, jnp.exp(score), 0.0), axis=1, keepdims=True)
        scores.append(score)
        members.append(member)
    log_total = jnp.log(total)
    loss_ref[...] = log_total - pos_scores
    grad = (jnp.exp(pos_scores - log_total) - 1.0) * positives
    for c in range(CHUNKS):
        weight = jnp.where(members[c], jnp.exp(scores[c] - log_total), 0.0)
        high = weight.astype(jnp.bfloat16)
        low = (weight - high.astype(jnp.float32)).astype(jnp.bfloat16)
        rows = row_refs[c][...]
        grad = grad + jnp.dot(high, rows, preferred_element_type=jnp.float32)
        grad = grad + jnp.dot(low, rows, preferred_element_type=jnp.float32)
    query_grad = (grad * scale).astype(jnp.bfloat16)
    grad_ref[...] = query_grad
    my_core = place_ref[1]
    hid = hidden_ref.shape[1]
    deep, part, half = hid // SHARD // X, hid // Z, width // CORE
    for z in range(Z):
        outer = contract_first(hidden_ref[:, z * part : (z + 1) * part], query_grad)
        left, right = outer[:, :half], outer[:, half:]
        keep = jnp.where(my_core == 0, left, right).astype(jnp.bfloat16)
        send = jnp.where(my_core == 0, right, left).astype(jnp.bfloat16)
        for y in range(Y):
            for x in range(X):
                rows = slice((y * X + x) * deep, (y * X + x + 1) * deep)
                keep_ref[y, x, z * deep : (z + 1) * deep, :] = keep[rows]
                send_ref[y, x, z * deep : (z + 1) * deep, :] = send[rows]


def inner_kernel(place_ref, queries_ref, grad_ref, slope_ref, weight_ref, keep_ref, send_ref):
    queries, query_grad = queries_ref[...], grad_ref[...]
    part = weight_ref.shape[0] // GRP
    for by_core, out_ref in ((1, send_ref), (0, keep_ref)):
        for by_x in range(X):
            group = ((place_ref[0] + by_x) & (X - 1)) * CORE + (place_ref[1] ^ by_core)
            at = pl.ds(pl.multiple_of(group * part, part), part)
            hidden_grad = contract_last(query_grad, weight_ref[at, :])
            pre_grad = (hidden_grad * slope_ref[:, at]).astype(jnp.bfloat16)
            out_ref[by_x] = contract_first(queries, pre_grad).astype(jnp.bfloat16)


def total_of(parts):
    return sum(part.astype(jnp.float32) for part in parts)


def columns_to_rows(value, wide):
    return jnp.concatenate(
        [value[..., i : i + wide] for i in range(0, value.shape[-1], wide)], axis=-2
    )


def rows_to_columns(value, deep):
    return jnp.concatenate(
        [value[..., i : i + deep, :] for i in range(0, value.shape[-2], deep)], axis=-1
    )


def shards(queries, positives, negative_ids, passage_table, inner_weight, outer_weight):
    q_dev, width = queries.shape
    rows_dev = passage_table.shape[0]
    shift = rows_dev.bit_length() - 1
    hid = inner_weight.shape[1]
    inner_rows, outer_rows = inner_weight.shape[0], outer_weight.shape[0]
    scale = float(width) ** (-0.5)
    limits = {"compiler_params": pltpu.CompilerParams(vmem_limit_bytes=VMEM)}
    my_x, my_core, my_y = (lax.axis_index(axis) for axis in ("x", "core", "y"))
    group = my_x * CORE + my_core
    place = jnp.stack([my_x, my_core]).astype(jnp.int32)
    in_smem = pl.BlockSpec(memory_space=pltpu.SMEM)
    in_vmem = pl.BlockSpec(memory_space=pltpu.VMEM)

    slots = jax.ShapeDtypeStruct((PAIRS, q_dev), jnp.int32)
    code, slot_query = pl.pallas_call(
        functools.partial(request_kernel, shift), out_shape=[slots] * 2, **limits
    )(negative_ids)
    code = exchange(
        jnp.broadcast_to(code[:, None], (PAIRS, 2, q_dev)).reshape(SHARD, q_dev), ("z", "y")
    ).reshape(Z, Y, q_dev)
    code = jnp.stack(
        [lax.dynamic_index_in_dim(code, (my_y - by) % Y, 1, False) for by in range(Y)]
    )
    own = (code >> shift) == my_y % 2
    wanted = code & (rows_dev - 1)
    per = q_dev // CHUNKS
    odd = (my_y % 2).astype(jnp.int32).reshape(1)

    def find(c, *done):
        cut = slice(c * per, (c + 1) * per)
        ids = after(wanted[:, :, cut].reshape(-1), *done)
        found = passage_table.at[ids].get(mode="promise_in_bounds").reshape(Y, Z, per, width)
        return jnp.where(own[:, :, cut, None], found, jnp.zeros((), found.dtype))

    def fetch(found):
        return [found[0]] + [ahead(found[by], "y", Y, -by) for by in range(1, Y)]

    def merge(near, *done):
        near = after(tuple(near), *done)
        return pl.pallas_call(
            merge_kernel,
            out_shape=jax.ShapeDtypeStruct((Z, 2, per, width), near[0].dtype),
            in_specs=[in_smem] + [in_vmem] * Y,
            **limits,
        )(odd, *near).reshape(-1, width)

    wide, deep = hid // GRP, outer_rows // GRP
    inner_piece = lax.dynamic_slice(inner_weight, (0, group * wide), (inner_rows, wide))
    outer_piece = lax.dynamic_slice(outer_weight, (group * deep, 0), (deep, width))
    piece = jnp.concatenate([rows_to_columns(inner_piece, deep), outer_piece], axis=0)

    found_0 = find(0)
    near_0 = fetch(found_0)
    found_1 = find(1, found_0)
    near_1 = fetch(found_1)
    gathered = spread(after(piece, found_0), ("z", "y"), SHARD)
    merged_0 = merge(near_0, found_1)
    rows_0 = exchange(merged_0, "z")
    gathered = after(gathered, merged_0)
    parts = [gathered] + [ahead(gathered, "x", X, by) for by in range(1, X)]
    found_2 = find(2, merged_0, gathered)
    near_2 = fetch(found_2)
    merged_1 = merge(near_1, found_2)
    rows_1 = exchange(after(merged_1, rows_0), "z")
    found_3 = find(3, merged_1, rows_0)
    near_3 = fetch(found_3)
    merged_2 = merge(near_2, found_3)
    rows_2 = exchange(after(merged_2, rows_1), "z")
    parts = after(tuple(parts), rows_1, merged_2)
    gathered = jnp.zeros((X, *gathered.shape), gathered.dtype)
    for by in range(X):
        gathered = lax.dynamic_update_index_in_dim(gathered, parts[by], (my_x - by) % X, 0)
    twin = ahead(gathered, "core", CORE, 1)
    merged_3 = merge(near_3, rows_1)
    rows_3 = exchange(after(merged_3, rows_2), "z")
    gathered, twin = after((gathered, twin), merged_3)
    chunks = [rows_0, rows_1, rows_2, rows_3]
    slot_query = slot_query.reshape(Z, 2, q_dev)
    slot_query = jnp.where(my_y // 2 == 0, slot_query, slot_query[:, ::-1])
    slot_query = jnp.concatenate(
        [slot_query[:, :, c * per : (c + 1) * per].reshape(1, -1) for c in range(CHUNKS)], axis=1
    )

    halves = jnp.stack(
        [jnp.where(my_core == 0, gathered, twin), jnp.where(my_core == 0, twin, gathered)], axis=1
    )
    inner_full = [
        columns_to_rows(halves[g // CORE, g % CORE, :, :deep], wide).reshape(width, wide)
        for g in range(GRP)
    ]
    outer_full = halves[:, :, :, deep:].transpose(2, 0, 1, 3, 4).reshape(hid, width)

    pre_act = jnp.concatenate(
        [jnp.dot(queries, part, preferred_element_type=jnp.float32) for part in inner_full], axis=1
    )
    hidden = gelu_value(pre_act).astype(jnp.bfloat16)
    slope = gelu_slope(pre_act)
    projected = jnp.dot(hidden, outer_full, preferred_element_type=jnp.float32)
    embedded = (queries.astype(jnp.float32) + projected).astype(jnp.bfloat16)

    half = width // CORE
    outer_cut = jax.ShapeDtypeStruct((Y, X, hid // Y // X, half), jnp.bfloat16)
    losses, query_grad, outer, outer_sent = pl.pallas_call(
        functools.partial(score_kernel, scale),
        out_shape=[
            jax.ShapeDtypeStruct((q_dev, 1), jnp.float32),
            jax.ShapeDtypeStruct((q_dev, width), jnp.bfloat16),
            outer_cut,
            outer_cut,
        ],
        in_specs=[in_smem] + [in_vmem] * (4 + CHUNKS),
        **limits,
    )(place, embedded, positives, hidden, slot_query, *chunks)
    outer_sent = ahead(outer_sent, "core", CORE, 1)
    inner, inner_sent = pl.pallas_call(
        inner_kernel,
        out_shape=[jax.ShapeDtypeStruct((X, width, wide), jnp.bfloat16)] * 2,
        in_specs=[in_smem] + [in_vmem] * 4,
        **limits,
    )(place, queries, query_grad, slope, outer_full)
    inner_sent = ahead(inner_sent, "core", CORE, 1)

    narrow = lambda value: value.astype(jnp.bfloat16)
    outer = exchange(narrow(total_of([outer, outer_sent])), "y")
    inner = [narrow(total_of([inner[by], inner_sent[by]])) for by in range(X)]
    inner = inner[:1] + [ahead(inner[by], "x", X, by) for by in range(1, X)]
    outer = exchange(narrow(total_of(list(outer))), "x")
    inner = narrow(total_of(inner)).reshape(Z, Y, inner_rows, wide)
    inner = [lax.dynamic_index_in_dim(inner, (my_y + by) % Y, 1, False) for by in range(Y)]
    inner = inner[:1] + [ahead(inner[by], "y", Y, by) for by in range(1, Y)]
    lanes = 128
    both = jnp.concatenate(
        [
            columns_to_rows(total_of(inner), lanes),
            columns_to_rows(total_of(list(outer)).reshape(Z, -1, half), lanes),
        ],
        axis=1,
    )
    both = total_of(list(exchange(narrow(both), "z")))
    both = spread(both, ("x", "core"), GRP)
    inner_deep = inner_rows * wide // lanes
    inner = rows_to_columns(both[:, :inner_deep], inner_rows)
    outer = rows_to_columns(both[:, inner_deep:], outer_rows // X)
    inner = jnp.concatenate(list(inner), axis=1)
    outer = jnp.concatenate(
        [jnp.concatenate([outer[x * CORE + c] for c in range(CORE)], axis=1) for x in range(X)],
        axis=0,
    )
    return (losses.reshape(-1), inner, outer)


def solution(mesh):
    fine = Mesh(mesh.devices.reshape(X, CORE, Z, Y), ("x", "core", "z", "y"))
    blocks, rows = ("x", "core", "z", "y"), ("z", "y")
    return jax.shard_map(
        shards,
        mesh=fine,
        in_specs=(
            P(blocks, None),
            P(blocks, None),
            P(blocks, None),
            P(rows, None),
            P(rows, None),
            P(rows, None),
        ),
        out_specs=(P(blocks), P(rows, None), P(rows, None)),
        check_vma=False,
    )
```

```python
import functools

import jax
import jax.numpy as jnp
from jax import lax
from jax.experimental import pallas as pl
from jax.experimental.pallas import tpu as pltpu
from jax.sharding import Mesh, PartitionSpec as P

X, CORE, Z, Y = 4, 2, 8, 4
GRP, SHARD = X * CORE, Z * Y
PAIRS = SHARD // 2
CHUNKS = 4
VMEM = 50 * 1024 * 1024


def gelu_value(pre_act):
    return pre_act * 0.5 * (1.0 + lax.erf(pre_act * 0.7071067811865476))


def gelu_slope(pre_act):
    return (
        0.5 * (1.0 + lax.erf(pre_act * 0.7071067811865476))
        + pre_act * jnp.exp(-0.5 * pre_act * pre_act) * 0.3989422804014327
    )


def contract_first(left, right):
    return lax.dot_general(
        left, right, (((0,), (0,)), ((), ())), preferred_element_type=jnp.float32
    )


def contract_last(left, right):
    return lax.dot_general(
        left, right, (((1,), (1,)), ((), ())), preferred_element_type=jnp.float32
    )


def exchange(value, axes):
    return lax.all_to_all(value, axes, split_axis=0, concat_axis=0, tiled=True)


def spread(value, axes, count):
    return exchange(jnp.broadcast_to(value[None], (count, *value.shape)), axes)


def swap(value, axis, by):
    return lax.ppermute(value, axis, [(i, i ^ by) for i in range(lax.axis_size(axis))])


def after(value, *done):
    return lax.optimization_barrier((value, *done))[0]


def request_kernel(shift, ids_ref, code_ref, query_ref):
    ids = ids_ref[...]
    q_dev, neg = ids.shape
    lane = lax.broadcasted_iota(jnp.int32, (q_dev, q_dev), 1)
    query = lax.broadcasted_iota(jnp.int32, (q_dev, q_dev), 0)
    before = (lane < query).astype(jnp.float32).astype(jnp.bfloat16)
    kind, pair_lane = lane // PAIRS, lane % PAIRS
    seen = jnp.zeros((1, q_dev), jnp.float32)
    placed = jnp.zeros((q_dev, q_dev), jnp.float32)
    for k in range(neg):
        id_k = ids[:, k : k + 1]
        owner = id_k >> shift
        odd = owner & 1
        member = owner == lane
        ones = member.astype(jnp.float32)
        counts = seen + jnp.dot(before, ones.astype(jnp.bfloat16), preferred_element_type=jnp.float32)
        rank = jnp.sum(jnp.where(member, counts, 0.0), axis=1, keepdims=True).astype(jnp.int32)
        seen = seen + jnp.sum(ones, axis=0, keepdims=True)
        slot = jnp.where(odd == 1, q_dev - 1 - rank, rank)
        at_slot = (slot == lane).astype(jnp.float32).astype(jnp.bfloat16)
        code = (odd << shift) + (id_k - (owner << shift))
        item = jnp.where(
            kind == 0, code >> 6, jnp.where(kind == 1, code & 63, jnp.where(kind == 2, query, 0))
        )
        item = jnp.where((owner >> 1) == pair_lane, item, 0)
        placed = placed + contract_first(item.astype(jnp.float32).astype(jnp.bfloat16), at_slot)
    code_ref[...] = (placed[:PAIRS] * 64.0 + placed[PAIRS : 2 * PAIRS]).astype(jnp.int32)
    query_ref[...] = placed[2 * PAIRS : 3 * PAIRS].astype(jnp.int32)


def score_kernel(scale, place_ref, embedded_ref, positives_ref, hidden_ref, query_ref, *refs):
    row_refs, (loss_ref, grad_ref, keep_ref, send_ref) = refs[:CHUNKS], refs[CHUNKS:]
    embedded = embedded_ref[...]
    positives = positives_ref[...].astype(jnp.float32)
    q_dev, width = embedded.shape
    pos_scores = (
        jnp.sum(embedded.astype(jnp.float32) * positives, axis=1, keepdims=True) * scale
    )
    total = jnp.exp(pos_scores)
    per = row_refs[0].shape[0]
    query = lax.broadcasted_iota(jnp.int32, (q_dev, per), 0)
    scores, members = [], []
    for c in range(CHUNKS):
        score = contract_last(embedded, row_refs[c][...]) * scale
        member = query_ref[:, c * per : (c + 1) * per] == query
        total = total + jnp.sum(jnp.where(member, jnp.exp(score), 0.0), axis=1, keepdims=True)
        scores.append(score)
        members.append(member)
    log_total = jnp.log(total)
    loss_ref[...] = log_total - pos_scores
    grad = (jnp.exp(pos_scores - log_total) - 1.0) * positives
    for c in range(CHUNKS):
        weight = jnp.where(members[c], jnp.exp(scores[c] - log_total), 0.0)
        high = weight.astype(jnp.bfloat16)
        low = (weight - high.astype(jnp.float32)).astype(jnp.bfloat16)
        rows = row_refs[c][...]
        grad = grad + jnp.dot(high, rows, preferred_element_type=jnp.float32)
        grad = grad + jnp.dot(low, rows, preferred_element_type=jnp.float32)
    query_grad = (grad * scale).astype(jnp.bfloat16)
    grad_ref[...] = query_grad
    my_core = place_ref[1]
    hid = hidden_ref.shape[1]
    deep, part, half = hid // SHARD // X, hid // Z, width // CORE
    for z in range(Z):
        outer = contract_first(hidden_ref[:, z * part : (z + 1) * part], query_grad)
        left, right = outer[:, :half], outer[:, half:]
        keep = jnp.where(my_core == 0, left, right).astype(jnp.bfloat16)
        send = jnp.where(my_core == 0, right, left).astype(jnp.bfloat16)
        for y in range(Y):
            for x in range(X):
                rows = slice((y * X + x) * deep, (y * X + x + 1) * deep)
                keep_ref[y, x, z * deep : (z + 1) * deep, :] = keep[rows]
                send_ref[y, x, z * deep : (z + 1) * deep, :] = send[rows]


def inner_kernel(place_ref, queries_ref, grad_ref, slope_ref, weight_ref, keep_ref, send_ref):
    queries, query_grad = queries_ref[...], grad_ref[...]
    part = weight_ref.shape[0] // GRP
    for by_core, out_ref in ((1, send_ref), (0, keep_ref)):
        for by_x in range(X):
            group = (place_ref[0] ^ by_x) * CORE + (place_ref[1] ^ by_core)
            at = pl.ds(pl.multiple_of(group * part, part), part)
            hidden_grad = contract_last(query_grad, weight_ref[at, :])
            pre_grad = (hidden_grad * slope_ref[:, at]).astype(jnp.bfloat16)
            out_ref[by_x] = contract_first(queries, pre_grad).astype(jnp.bfloat16)


def total_of(parts):
    return sum(part.astype(jnp.float32) for part in parts)


def columns_to_rows(value, wide):
    return jnp.concatenate(
        [value[..., i : i + wide] for i in range(0, value.shape[-1], wide)], axis=-2
    )


def rows_to_columns(value, deep):
    return jnp.concatenate(
        [value[..., i : i + deep, :] for i in range(0, value.shape[-2], deep)], axis=-1
    )


def shards(queries, positives, negative_ids, passage_table, inner_weight, outer_weight):
    q_dev, width = queries.shape
    rows_dev = passage_table.shape[0]
    shift = rows_dev.bit_length() - 1
    hid = inner_weight.shape[1]
    inner_rows, outer_rows = inner_weight.shape[0], outer_weight.shape[0]
    scale = float(width) ** (-0.5)
    limits = {"compiler_params": pltpu.CompilerParams(vmem_limit_bytes=VMEM)}
    my_x, my_core, my_y = (lax.axis_index(axis) for axis in ("x", "core", "y"))
    group = my_x * CORE + my_core
    place = jnp.stack([my_x, my_core]).astype(jnp.int32)
    in_smem = pl.BlockSpec(memory_space=pltpu.SMEM)
    in_vmem = pl.BlockSpec(memory_space=pltpu.VMEM)

    slots = jax.ShapeDtypeStruct((PAIRS, q_dev), jnp.int32)
    code, slot_query = pl.pallas_call(
        functools.partial(request_kernel, shift), out_shape=[slots] * 2, **limits
    )(negative_ids)
    code = exchange(
        jnp.broadcast_to(code[:, None], (PAIRS, 2, q_dev)).reshape(SHARD, q_dev), ("z", "y")
    ).reshape(Z, Y, q_dev)
    code = jnp.stack([lax.dynamic_index_in_dim(code, my_y ^ by, 1, False) for by in range(Y)])
    own = (code >> shift) == my_y % 2
    wanted = code & (rows_dev - 1)
    wanted = lax.optimization_barrier((wanted[:, :, : q_dev // 2], wanted[:, :, q_dev // 2 :]))
    per = q_dev // 2
    cuts = slice(0, per), slice(per, q_dev)

    def find(picks, *done):
        ids = jnp.stack([wanted[part][by] for by, part in picks])
        ids = after(ids.reshape(-1), *done)
        found = passage_table.at[ids].get(mode="promise_in_bounds").reshape(-1, Z * per, width)
        return [
            jnp.where(own[by, :, cuts[part]].reshape(-1, 1), found[i], jnp.zeros((), found.dtype))
            for i, (by, part) in enumerate(picks)
        ]

    wide, deep = hid // GRP, outer_rows // GRP
    inner_piece = lax.dynamic_slice(inner_weight, (0, group * wide), (inner_rows, wide))
    outer_piece = lax.dynamic_slice(outer_weight, (group * deep, 0), (deep, width))
    piece = jnp.concatenate([rows_to_columns(inner_piece, deep), outer_piece], axis=0)

    (found_10,) = find([(1, 0)])
    near_10 = swap(found_10, "y", 1)
    gathered = spread(after(piece, found_10), ("z", "y"), SHARD)
    found_00, found_11 = find([(0, 0), (1, 1)], found_10)
    near_11 = swap(found_11, "y", 1)
    own_0 = after(found_00 + near_10, gathered)
    rows_0 = exchange(own_0, "z")
    gathered = after(gathered, own_0)
    parts = [gathered] + [swap(gathered, "x", by) for by in range(1, X)]
    found_30, found_01, found_20 = find([(3, 0), (0, 1), (2, 0)], own_0)
    near_30, near_20 = swap(found_30, "y", 3), swap(found_20, "y", 2)
    found_31, found_21 = find([(3, 1), (2, 1)], found_30)
    near_31, near_21 = swap(found_31, "y", 3), swap(found_21, "y", 2)
    rows_1 = exchange(after(found_01 + near_11, rows_0, near_30, found_31, parts[1], parts[3]), "z")
    other_0 = near_20 + near_30
    rows_2 = exchange(after(other_0, rows_1, near_31), "z")
    other_1 = near_21 + near_31
    rows_3 = exchange(after(other_1, rows_2), "z")
    chunks = [rows_0, rows_1, rows_2, rows_3]
    parts = after(tuple(parts), rows_1, other_0, near_31)
    gathered = jnp.zeros((X, *gathered.shape), gathered.dtype)
    for by in range(X):
        gathered = lax.dynamic_update_index_in_dim(gathered, parts[by], my_x ^ by, 0)
    twin = swap(gathered, "core", 1)
    gathered, twin = after((gathered, twin), other_1)
    slot_query = slot_query.reshape(Z, 2, q_dev)
    slot_query = jnp.where(my_y // 2 == 0, slot_query, slot_query[:, ::-1])
    slot_query = jnp.concatenate(
        [slot_query[:, pair, cut].reshape(1, -1) for pair in range(2) for cut in cuts], axis=1
    )

    halves = jnp.stack(
        [jnp.where(my_core == 0, gathered, twin), jnp.where(my_core == 0, twin, gathered)], axis=1
    )
    inner_full = [
        columns_to_rows(halves[g // CORE, g % CORE, :, :deep], wide).reshape(width, wide)
        for g in range(GRP)
    ]
    outer_full = halves[:, :, :, deep:].transpose(2, 0, 1, 3, 4).reshape(hid, width)

    pre_act = jnp.concatenate(
        [jnp.dot(queries, part, preferred_element_type=jnp.float32) for part in inner_full], axis=1
    )
    hidden = gelu_value(pre_act).astype(jnp.bfloat16)
    slope = gelu_slope(pre_act)
    projected = jnp.dot(hidden, outer_full, preferred_element_type=jnp.float32)
    embedded = (queries.astype(jnp.float32) + projected).astype(jnp.bfloat16)

    half = width // CORE
    outer_cut = jax.ShapeDtypeStruct((Y, X, hid // Y // X, half), jnp.bfloat16)
    losses, query_grad, outer, outer_sent = pl.pallas_call(
        functools.partial(score_kernel, scale),
        out_shape=[
            jax.ShapeDtypeStruct((q_dev, 1), jnp.float32),
            jax.ShapeDtypeStruct((q_dev, width), jnp.bfloat16),
            outer_cut,
            outer_cut,
        ],
        in_specs=[in_smem] + [in_vmem] * (4 + CHUNKS),
        **limits,
    )(place, embedded, positives, hidden, slot_query, *chunks)
    outer_sent = swap(outer_sent, "core", 1)
    inner, inner_sent = pl.pallas_call(
        inner_kernel,
        out_shape=[jax.ShapeDtypeStruct((X, width, wide), jnp.bfloat16)] * 2,
        in_specs=[in_smem] + [in_vmem] * 4,
        **limits,
    )(place, queries, query_grad, slope, outer_full)
    inner_sent = swap(inner_sent, "core", 1)

    narrow = lambda value: value.astype(jnp.bfloat16)
    outer = exchange(narrow(total_of([outer, outer_sent])), "y")
    inner = [narrow(total_of([inner[by], inner_sent[by]])) for by in range(X)]
    inner = inner[:1] + [swap(inner[by], "x", by) for by in range(1, X)]
    outer = narrow(total_of(list(outer)))
    inner = after(tuple(inner), outer)
    outer = exchange(outer, "x")
    inner = narrow(total_of(inner)).reshape(Z, Y, inner_rows, wide)
    inner = [lax.dynamic_index_in_dim(inner, my_y ^ by, 1, False) for by in range(Y)]
    inner = inner[:1] + [swap(inner[by], "y", by) for by in range(1, Y)]
    lanes = 128
    both = jnp.concatenate(
        [
            columns_to_rows(total_of(inner), lanes),
            columns_to_rows(total_of(list(outer)).reshape(Z, -1, half), lanes),
        ],
        axis=1,
    )
    both = total_of(list(exchange(narrow(both), "z")))
    both = spread(both, ("x", "core"), GRP)
    inner_deep = inner_rows * wide // lanes
    inner = rows_to_columns(both[:, :inner_deep], inner_rows)
    outer = rows_to_columns(both[:, inner_deep:], outer_rows // X)
    inner = jnp.concatenate(list(inner), axis=1)
    outer = jnp.concatenate(
        [jnp.concatenate([outer[x * CORE + c] for c in range(CORE)], axis=1) for x in range(X)],
        axis=0,
    )
    return (losses.reshape(-1), inner, outer)


def solution(mesh):
    fine = Mesh(mesh.devices.reshape(X, CORE, Z, Y), ("x", "core", "z", "y"))
    blocks, rows = ("x", "core", "z", "y"), ("z", "y")
    return jax.shard_map(
        shards,
        mesh=fine,
        in_specs=(
            P(blocks, None),
            P(blocks, None),
            P(blocks, None),
            P(rows, None),
            P(rows, None),
            P(rows, None),
        ),
        out_specs=(P(blocks), P(rows, None), P(rows, None)),
        check_vma=False,
    )
```

```python
import functools

import jax
import jax.numpy as jnp
from jax import lax
from jax.experimental import pallas as pl
from jax.experimental.pallas import tpu as pltpu
from jax.sharding import Mesh, PartitionSpec as P

X, CORE, Z, Y = 4, 2, 8, 4
GRP, SHARD = X * CORE, Z * Y
PAIRS = SHARD // 2
CHUNKS = 4
VMEM = 50 * 1024 * 1024


def gelu_value(pre_act):
    return pre_act * 0.5 * (1.0 + lax.erf(pre_act * 0.7071067811865476))


def gelu_slope(pre_act):
    return (
        0.5 * (1.0 + lax.erf(pre_act * 0.7071067811865476))
        + pre_act * jnp.exp(-0.5 * pre_act * pre_act) * 0.3989422804014327
    )


def contract_first(left, right):
    return lax.dot_general(
        left, right, (((0,), (0,)), ((), ())), preferred_element_type=jnp.float32
    )


def contract_last(left, right):
    return lax.dot_general(
        left, right, (((1,), (1,)), ((), ())), preferred_element_type=jnp.float32
    )


def exchange(value, axes):
    return lax.all_to_all(value, axes, split_axis=0, concat_axis=0, tiled=True)


def spread(value, axes, count):
    return exchange(jnp.broadcast_to(value[None], (count, *value.shape)), axes)


def swap(value, axis, by):
    return lax.ppermute(value, axis, [(i, i ^ by) for i in range(lax.axis_size(axis))])


def after(value, *done):
    return lax.optimization_barrier((value, *done))[0]


def request_kernel(shift, ids_ref, code_ref, query_ref):
    ids = ids_ref[...]
    q_dev, neg = ids.shape
    lane = lax.broadcasted_iota(jnp.int32, (q_dev, q_dev), 1)
    query = lax.broadcasted_iota(jnp.int32, (q_dev, q_dev), 0)
    before = (lane < query).astype(jnp.float32).astype(jnp.bfloat16)
    kind, pair_lane = lane // PAIRS, lane % PAIRS
    seen = jnp.zeros((1, q_dev), jnp.float32)
    placed = jnp.zeros((q_dev, q_dev), jnp.float32)
    for k in range(neg):
        id_k = ids[:, k : k + 1]
        owner = id_k >> shift
        odd = owner & 1
        member = owner == lane
        ones = member.astype(jnp.float32)
        counts = seen + jnp.dot(before, ones.astype(jnp.bfloat16), preferred_element_type=jnp.float32)
        rank = jnp.sum(jnp.where(member, counts, 0.0), axis=1, keepdims=True).astype(jnp.int32)
        seen = seen + jnp.sum(ones, axis=0, keepdims=True)
        slot = jnp.where(odd == 1, q_dev - 1 - rank, rank)
        at_slot = (slot == lane).astype(jnp.float32).astype(jnp.bfloat16)
        code = (odd << shift) + (id_k - (owner << shift))
        item = jnp.where(
            kind == 0, code >> 6, jnp.where(kind == 1, code & 63, jnp.where(kind == 2, query, 0))
        )
        item = jnp.where((owner >> 1) == pair_lane, item, 0)
        placed = placed + contract_first(item.astype(jnp.float32).astype(jnp.bfloat16), at_slot)
    code_ref[...] = (placed[:PAIRS] * 64.0 + placed[PAIRS : 2 * PAIRS]).astype(jnp.int32)
    query_ref[...] = placed[2 * PAIRS : 3 * PAIRS].astype(jnp.int32)


def arrange_kernel(place_ref, *refs):
    part_refs, out_ref = refs[:GRP], refs[GRP]
    for by_core in range(CORE):
        for by_x in range(X):
            at = place_ref[0] ^ by_x, place_ref[1] ^ by_core
            out_ref[at] = part_refs[by_core * X + by_x][...]


def score_kernel(scale, place_ref, embedded_ref, positives_ref, hidden_ref, query_ref, *refs):
    row_refs, (loss_ref, grad_ref, keep_ref, send_ref) = refs[:CHUNKS], refs[CHUNKS:]
    embedded = embedded_ref[...]
    positives = positives_ref[...].astype(jnp.float32)
    q_dev, width = embedded.shape
    pos_scores = (
        jnp.sum(embedded.astype(jnp.float32) * positives, axis=1, keepdims=True) * scale
    )
    total = jnp.exp(pos_scores)
    per = row_refs[0].shape[0]
    query = lax.broadcasted_iota(jnp.int32, (q_dev, per), 0)
    scores, members = [], []
    for c in range(CHUNKS):
        score = contract_last(embedded, row_refs[c][...]) * scale
        member = query_ref[:, c * per : (c + 1) * per] == query
        total = total + jnp.sum(jnp.where(member, jnp.exp(score), 0.0), axis=1, keepdims=True)
        scores.append(score)
        members.append(member)
    log_total = jnp.log(total)
    loss_ref[...] = log_total - pos_scores
    grad = (jnp.exp(pos_scores - log_total) - 1.0) * positives
    for c in range(CHUNKS):
        weight = jnp.where(members[c], jnp.exp(scores[c] - log_total), 0.0)
        high = weight.astype(jnp.bfloat16)
        low = (weight - high.astype(jnp.float32)).astype(jnp.bfloat16)
        rows = row_refs[c][...]
        grad = grad + jnp.dot(high, rows, preferred_element_type=jnp.float32)
        grad = grad + jnp.dot(low, rows, preferred_element_type=jnp.float32)
    query_grad = (grad * scale).astype(jnp.bfloat16)
    grad_ref[...] = query_grad
    my_core = place_ref[1]
    hid = hidden_ref.shape[1]
    deep, part, half = hid // SHARD // X, hid // Z, width // CORE
    for z in range(Z):
        outer = contract_first(hidden_ref[:, z * part : (z + 1) * part], query_grad)
        left, right = outer[:, :half], outer[:, half:]
        keep = jnp.where(my_core == 0, left, right).astype(jnp.bfloat16)
        send = jnp.where(my_core == 0, right, left).astype(jnp.bfloat16)
        for y in range(Y):
            for x in range(X):
                rows = slice((y * X + x) * deep, (y * X + x + 1) * deep)
                keep_ref[y, x, z * deep : (z + 1) * deep, :] = keep[rows]
                send_ref[y, x, z * deep : (z + 1) * deep, :] = send[rows]


def inner_kernel(place_ref, queries_ref, grad_ref, slope_ref, weight_ref, keep_ref, send_ref):
    queries, query_grad = queries_ref[...], grad_ref[...]
    part = weight_ref.shape[0] // GRP
    for by_core, out_ref in ((1, send_ref), (0, keep_ref)):
        for by_x in range(X):
            group = (place_ref[0] ^ by_x) * CORE + (place_ref[1] ^ by_core)
            at = pl.ds(pl.multiple_of(group * part, part), part)
            hidden_grad = contract_last(query_grad, weight_ref[at, :])
            pre_grad = (hidden_grad * slope_ref[:, at]).astype(jnp.bfloat16)
            out_ref[by_x] = contract_first(queries, pre_grad).astype(jnp.bfloat16)


def total_of(parts):
    return sum(part.astype(jnp.float32) for part in parts)


def columns_to_rows(value, wide):
    return jnp.concatenate(
        [value[..., i : i + wide] for i in range(0, value.shape[-1], wide)], axis=-2
    )


def rows_to_columns(value, deep):
    return jnp.concatenate(
        [value[..., i : i + deep, :] for i in range(0, value.shape[-2], deep)], axis=-1
    )


def shards(queries, positives, negative_ids, passage_table, inner_weight, outer_weight):
    q_dev, width = queries.shape
    rows_dev = passage_table.shape[0]
    shift = rows_dev.bit_length() - 1
    hid = inner_weight.shape[1]
    inner_rows, outer_rows = inner_weight.shape[0], outer_weight.shape[0]
    scale = float(width) ** (-0.5)
    limits = {"compiler_params": pltpu.CompilerParams(vmem_limit_bytes=VMEM)}
    my_x, my_core, my_y = (lax.axis_index(axis) for axis in ("x", "core", "y"))
    group = my_x * CORE + my_core
    place = jnp.stack([my_x, my_core]).astype(jnp.int32)
    in_smem = pl.BlockSpec(memory_space=pltpu.SMEM)
    in_vmem = pl.BlockSpec(memory_space=pltpu.VMEM)

    slots = jax.ShapeDtypeStruct((PAIRS, q_dev), jnp.int32)
    code, slot_query = pl.pallas_call(
        functools.partial(request_kernel, shift), out_shape=[slots] * 2, **limits
    )(negative_ids)
    code = exchange(
        jnp.broadcast_to(code[:, None], (PAIRS, 2, q_dev)).reshape(SHARD, q_dev), ("z", "y")
    ).reshape(Z, Y, q_dev)
    code = jnp.stack([lax.dynamic_index_in_dim(code, my_y ^ by, 1, False) for by in range(Y)])
    own = (code >> shift) == my_y % 2
    wanted = code & (rows_dev - 1)
    wanted = lax.optimization_barrier((wanted[:, :, : q_dev // 2], wanted[:, :, q_dev // 2 :]))
    per = q_dev // 2
    cuts = slice(0, per), slice(per, q_dev)

    def find(picks, *done):
        ids = jnp.stack([wanted[part][by] for by, part in picks])
        ids = after(ids.reshape(-1), *done)
        found = passage_table.at[ids].get(mode="promise_in_bounds").reshape(-1, Z * per, width)
        return [
            jnp.where(own[by, :, cuts[part]].reshape(-1, 1), found[i], jnp.zeros((), found.dtype))
            for i, (by, part) in enumerate(picks)
        ]

    wide, deep = hid // GRP, outer_rows // GRP
    inner_piece = lax.dynamic_slice(inner_weight, (0, group * wide), (inner_rows, wide))
    outer_piece = lax.dynamic_slice(outer_weight, (group * deep, 0), (deep, width))
    piece = jnp.concatenate([rows_to_columns(inner_piece, deep), outer_piece], axis=0)

    (found_10,) = find([(1, 0)])
    near_10 = swap(found_10, "y", 1)
    gathered = spread(after(piece, found_10), ("z", "y"), SHARD)
    found_00, found_11 = find([(0, 0), (1, 1)], found_10)
    near_11 = swap(found_11, "y", 1)
    own_0 = after(found_00 + after(near_10, found_11), gathered)
    rows_0 = exchange(own_0, "z")
    found_30, found_01, found_20 = find([(3, 0), (0, 1), (2, 0)], own_0)
    near_30, near_20 = swap(found_30, "y", 3), swap(found_20, "y", 2)
    gathered = after(gathered, own_0)
    parts = [gathered] + [swap(gathered, "x", by) for by in range(1, X)]
    found_31, found_21 = find([(3, 1), (2, 1)], found_30)
    near_31, near_21 = swap(found_31, "y", 3), swap(found_21, "y", 2)
    own_1 = found_01 + near_11
    rows_1 = exchange(
        after(own_1, rows_0, near_30, near_20, found_31, parts[1], parts[3]), "z"
    )
    rows_2 = exchange(after(near_20 + near_30, rows_1, near_21, parts[2]), "z")
    other_1 = near_21 + near_31
    rows_3 = exchange(after(other_1, rows_2), "z")
    chunks = [rows_0, rows_1, rows_2, rows_3]
    parts = after(tuple(parts + [swap(part, "core", 1) for part in parts]), rows_1, other_1)
    halves = pl.pallas_call(
        arrange_kernel,
        out_shape=jax.ShapeDtypeStruct((X, CORE, SHARD, *piece.shape), piece.dtype),
        in_specs=[in_smem] + [in_vmem] * GRP,
        **limits,
    )(place, *parts)
    slot_query = slot_query.reshape(Z, 2, q_dev)
    slot_query = jnp.where(my_y // 2 == 0, slot_query, slot_query[:, ::-1])
    slot_query = jnp.concatenate(
        [slot_query[:, pair, cut].reshape(1, -1) for pair in range(2) for cut in cuts], axis=1
    )

    inner_full = [
        columns_to_rows(halves[g // CORE, g % CORE, :, :deep], wide).reshape(width, wide)
        for g in range(GRP)
    ]
    outer_full = halves[:, :, :, deep:].transpose(2, 0, 1, 3, 4).reshape(hid, width)

    pre_act = jnp.concatenate(
        [jnp.dot(queries, part, preferred_element_type=jnp.float32) for part in inner_full], axis=1
    )
    hidden = gelu_value(pre_act).astype(jnp.bfloat16)
    slope = gelu_slope(pre_act)
    projected = jnp.dot(hidden, outer_full, preferred_element_type=jnp.float32)
    embedded = (queries.astype(jnp.float32) + projected).astype(jnp.bfloat16)

    half = width // CORE
    outer_cut = jax.ShapeDtypeStruct((Y, X, hid // Y // X, half), jnp.bfloat16)
    losses, query_grad, outer, outer_sent = pl.pallas_call(
        functools.partial(score_kernel, scale),
        out_shape=[
            jax.ShapeDtypeStruct((q_dev, 1), jnp.float32),
            jax.ShapeDtypeStruct((q_dev, width), jnp.bfloat16),
            outer_cut,
            outer_cut,
        ],
        in_specs=[in_smem] + [in_vmem] * (4 + CHUNKS),
        **limits,
    )(place, embedded, positives, hidden, slot_query, *chunks)
    outer_sent = swap(outer_sent, "core", 1)
    inner, inner_sent = pl.pallas_call(
        inner_kernel,
        out_shape=[jax.ShapeDtypeStruct((X, width, wide), jnp.bfloat16)] * 2,
        in_specs=[in_smem] + [in_vmem] * 4,
        **limits,
    )(place, queries, query_grad, slope, outer_full)
    inner_sent = swap(inner_sent, "core", 1)

    narrow = lambda value: value.astype(jnp.bfloat16)
    outer = exchange(narrow(total_of([outer, outer_sent])), "y")
    inner = [narrow(total_of([inner[by], inner_sent[by]])) for by in range(X)]
    inner = inner[:1] + [swap(inner[by], "x", by) for by in range(1, X)]
    outer = narrow(total_of(list(outer)))
    inner = after(tuple(inner), outer)
    outer = exchange(outer, "x")
    inner = narrow(total_of(inner)).reshape(Z, Y, inner_rows, wide)
    inner = [lax.dynamic_index_in_dim(inner, my_y ^ by, 1, False) for by in range(Y)]
    inner = inner[:1] + [swap(inner[by], "y", by) for by in range(1, Y)]
    lanes = 128
    both = jnp.concatenate(
        [
            columns_to_rows(total_of(inner), lanes),
            columns_to_rows(total_of(list(outer)).reshape(Z, -1, half), lanes),
        ],
        axis=1,
    )
    both = total_of(list(exchange(narrow(both), "z")))
    both = spread(both, ("x", "core"), GRP)
    inner_deep = inner_rows * wide // lanes
    inner = rows_to_columns(both[:, :inner_deep], inner_rows)
    outer = rows_to_columns(both[:, inner_deep:], outer_rows // X)
    inner = jnp.concatenate(list(inner), axis=1)
    outer = jnp.concatenate(
        [jnp.concatenate([outer[x * CORE + c] for c in range(CORE)], axis=1) for x in range(X)],
        axis=0,
    )
    return (losses.reshape(-1), inner, outer)


def solution(mesh):
    fine = Mesh(mesh.devices.reshape(X, CORE, Z, Y), ("x", "core", "z", "y"))
    blocks, rows = ("x", "core", "z", "y"), ("z", "y")
    return jax.shard_map(
        shards,
        mesh=fine,
        in_specs=(
            P(blocks, None),
            P(blocks, None),
            P(blocks, None),
            P(rows, None),
            P(rows, None),
            P(rows, None),
        ),
        out_specs=(P(blocks), P(rows, None), P(rows, None)),
        check_vma=False,
    )
```

```python
import functools

import jax
import jax.numpy as jnp
from jax import lax
from jax.experimental import pallas as pl
from jax.experimental.pallas import tpu as pltpu
from jax.sharding import Mesh, PartitionSpec as P

X, CORE, Z, Y = 4, 2, 8, 4
GRP, SHARD = X * CORE, Z * Y
PAIRS = SHARD // 2
CHUNKS = 4
VMEM = 50 * 1024 * 1024


def gelu_value(pre_act):
    return pre_act * 0.5 * (1.0 + lax.erf(pre_act * 0.7071067811865476))


def gelu_slope(pre_act):
    return (
        0.5 * (1.0 + lax.erf(pre_act * 0.7071067811865476))
        + pre_act * jnp.exp(-0.5 * pre_act * pre_act) * 0.3989422804014327
    )


def contract_first(left, right):
    return lax.dot_general(
        left, right, (((0,), (0,)), ((), ())), preferred_element_type=jnp.float32
    )


def contract_last(left, right):
    return lax.dot_general(
        left, right, (((1,), (1,)), ((), ())), preferred_element_type=jnp.float32
    )


def exchange(value, axes):
    return lax.all_to_all(value, axes, split_axis=0, concat_axis=0, tiled=True)


def spread(value, axes, count):
    return exchange(jnp.broadcast_to(value[None], (count, *value.shape)), axes)


def swap(value, axis, by):
    return lax.ppermute(value, axis, [(i, i ^ by) for i in range(lax.axis_size(axis))])


def after(value, *done):
    return lax.optimization_barrier((value, *done))[0]


def request_kernel(shift, ids_ref, code_ref, query_ref):
    ids = ids_ref[...]
    q_dev, neg = ids.shape
    lane = lax.broadcasted_iota(jnp.int32, (q_dev, q_dev), 1)
    query = lax.broadcasted_iota(jnp.int32, (q_dev, q_dev), 0)
    before = (lane < query).astype(jnp.float32).astype(jnp.bfloat16)
    kind, pair_lane = lane // PAIRS, lane % PAIRS
    seen = jnp.zeros((1, q_dev), jnp.float32)
    placed = jnp.zeros((q_dev, q_dev), jnp.float32)
    for k in range(neg):
        id_k = ids[:, k : k + 1]
        owner = id_k >> shift
        odd = owner & 1
        member = owner == lane
        ones = member.astype(jnp.float32)
        counts = seen + jnp.dot(before, ones.astype(jnp.bfloat16), preferred_element_type=jnp.float32)
        rank = jnp.sum(jnp.where(member, counts, 0.0), axis=1, keepdims=True).astype(jnp.int32)
        seen = seen + jnp.sum(ones, axis=0, keepdims=True)
        slot = jnp.where(odd == 1, q_dev - 1 - rank, rank)
        at_slot = (slot == lane).astype(jnp.float32).astype(jnp.bfloat16)
        code = (odd << shift) + (id_k - (owner << shift))
        item = jnp.where(
            kind == 0, code >> 6, jnp.where(kind == 1, code & 63, jnp.where(kind == 2, query, 0))
        )
        item = jnp.where((owner >> 1) == pair_lane, item, 0)
        placed = placed + contract_first(item.astype(jnp.float32).astype(jnp.bfloat16), at_slot)
    code_ref[...] = (placed[:PAIRS] * 64.0 + placed[PAIRS : 2 * PAIRS]).astype(jnp.int32)
    query_ref[...] = placed[2 * PAIRS : 3 * PAIRS].astype(jnp.int32)


def arrange_kernel(place_ref, *refs):
    part_refs, out_ref = refs[:GRP], refs[GRP]
    for by_core in range(CORE):
        for by_x in range(X):
            at = place_ref[0] ^ by_x, place_ref[1] ^ by_core
            out_ref[at] = part_refs[by_core * X + by_x][...]


def score_kernel(scale, place_ref, embedded_ref, positives_ref, hidden_ref, query_ref, *refs):
    row_refs, (loss_ref, grad_ref, keep_ref, send_ref) = refs[:CHUNKS], refs[CHUNKS:]
    embedded = embedded_ref[...]
    positives = positives_ref[...].astype(jnp.float32)
    q_dev, width = embedded.shape
    pos_scores = (
        jnp.sum(embedded.astype(jnp.float32) * positives, axis=1, keepdims=True) * scale
    )
    total = jnp.exp(pos_scores)
    per = row_refs[0].shape[0]
    query = lax.broadcasted_iota(jnp.int32, (q_dev, per), 0)
    scores, members = [], []
    for c in range(CHUNKS):
        score = contract_last(embedded, row_refs[c][...]) * scale
        member = query_ref[:, c * per : (c + 1) * per] == query
        total = total + jnp.sum(jnp.where(member, jnp.exp(score), 0.0), axis=1, keepdims=True)
        scores.append(score)
        members.append(member)
    log_total = jnp.log(total)
    loss_ref[...] = log_total - pos_scores
    grad = (jnp.exp(pos_scores - log_total) - 1.0) * positives
    for c in range(CHUNKS):
        weight = jnp.where(members[c], jnp.exp(scores[c] - log_total), 0.0)
        high = weight.astype(jnp.bfloat16)
        low = (weight - high.astype(jnp.float32)).astype(jnp.bfloat16)
        rows = row_refs[c][...]
        grad = grad + jnp.dot(high, rows, preferred_element_type=jnp.float32)
        grad = grad + jnp.dot(low, rows, preferred_element_type=jnp.float32)
    query_grad = (grad * scale).astype(jnp.bfloat16)
    grad_ref[...] = query_grad
    my_core = place_ref[1]
    hid = hidden_ref.shape[1]
    deep, part, half = hid // SHARD // X, hid // Z, width // CORE
    for z in range(Z):
        outer = contract_first(hidden_ref[:, z * part : (z + 1) * part], query_grad)
        left, right = outer[:, :half], outer[:, half:]
        keep = jnp.where(my_core == 0, left, right).astype(jnp.bfloat16)
        send = jnp.where(my_core == 0, right, left).astype(jnp.bfloat16)
        for y in range(Y):
            for x in range(X):
                rows = slice((y * X + x) * deep, (y * X + x + 1) * deep)
                keep_ref[y, x, z * deep : (z + 1) * deep, :] = keep[rows]
                send_ref[y, x, z * deep : (z + 1) * deep, :] = send[rows]


def inner_kernel(place_ref, queries_ref, grad_ref, slope_ref, weight_ref, keep_ref, send_ref):
    queries, query_grad = queries_ref[...], grad_ref[...]
    part = weight_ref.shape[0] // GRP
    for by_core, out_ref in ((1, send_ref), (0, keep_ref)):
        for by_x in range(X):
            group = (place_ref[0] ^ by_x) * CORE + (place_ref[1] ^ by_core)
            at = pl.ds(pl.multiple_of(group * part, part), part)
            hidden_grad = contract_last(query_grad, weight_ref[at, :])
            pre_grad = (hidden_grad * slope_ref[:, at]).astype(jnp.bfloat16)
            out_ref[by_x] = contract_first(queries, pre_grad).astype(jnp.bfloat16)


def total_of(parts):
    return sum(part.astype(jnp.float32) for part in parts)


def columns_to_rows(value, wide):
    return jnp.concatenate(
        [value[..., i : i + wide] for i in range(0, value.shape[-1], wide)], axis=-2
    )


def rows_to_columns(value, deep):
    return jnp.concatenate(
        [value[..., i : i + deep, :] for i in range(0, value.shape[-2], deep)], axis=-1
    )


def shards(queries, positives, negative_ids, passage_table, inner_weight, outer_weight):
    q_dev, width = queries.shape
    rows_dev = passage_table.shape[0]
    shift = rows_dev.bit_length() - 1
    hid = inner_weight.shape[1]
    inner_rows, outer_rows = inner_weight.shape[0], outer_weight.shape[0]
    scale = float(width) ** (-0.5)
    limits = {"compiler_params": pltpu.CompilerParams(vmem_limit_bytes=VMEM)}
    my_x, my_core, my_y = (lax.axis_index(axis) for axis in ("x", "core", "y"))
    group = my_x * CORE + my_core
    place = jnp.stack([my_x, my_core]).astype(jnp.int32)
    in_smem = pl.BlockSpec(memory_space=pltpu.SMEM)
    in_vmem = pl.BlockSpec(memory_space=pltpu.VMEM)

    slots = jax.ShapeDtypeStruct((PAIRS, q_dev), jnp.int32)
    code, slot_query = pl.pallas_call(
        functools.partial(request_kernel, shift), out_shape=[slots] * 2, **limits
    )(negative_ids)
    code = exchange(
        jnp.broadcast_to(code[:, None], (PAIRS, 2, q_dev)).reshape(SHARD, q_dev), ("z", "y")
    ).reshape(Z, Y, q_dev)
    code = jnp.stack([lax.dynamic_index_in_dim(code, my_y ^ by, 1, False) for by in range(Y)])
    own = (code >> shift) == my_y % 2
    wanted = code & (rows_dev - 1)
    wanted = lax.optimization_barrier((wanted[:, :, : q_dev // 2], wanted[:, :, q_dev // 2 :]))
    per = q_dev // 2
    cuts = slice(0, per), slice(per, q_dev)

    def find(picks, *done):
        ids = jnp.stack([wanted[part][by] for by, part in picks])
        ids = after(ids.reshape(-1), *done)
        found = passage_table.at[ids].get(mode="promise_in_bounds").reshape(-1, Z * per, width)
        return [
            jnp.where(own[by, :, cuts[part]].reshape(-1, 1), found[i], jnp.zeros((), found.dtype))
            for i, (by, part) in enumerate(picks)
        ]

    wide, deep = hid // GRP, outer_rows // GRP
    inner_piece = lax.dynamic_slice(inner_weight, (0, group * wide), (inner_rows, wide))
    outer_piece = lax.dynamic_slice(outer_weight, (group * deep, 0), (deep, width))
    piece = jnp.concatenate([rows_to_columns(inner_piece, deep), outer_piece], axis=0)

    (found_10,) = find([(1, 0)])
    near_10 = swap(found_10, "y", 1)
    gathered = spread(after(piece, found_10), ("z", "y"), SHARD)
    found_00, found_01 = find([(0, 0), (0, 1)], found_10)
    found_11, found_30, found_20 = find([(1, 1), (3, 0), (2, 0)], found_00, found_01)
    near_11, near_30, near_20 = swap(found_11, "y", 1), swap(found_30, "y", 3), swap(found_20, "y", 2)
    own_0 = after(found_00 + after(near_10, found_11), gathered)
    rows_0 = exchange(own_0, "z")
    gathered = after(gathered, own_0)
    parts = [gathered] + [swap(gathered, "x", by) for by in range(1, X)]
    found_31, found_21 = find([(3, 1), (2, 1)], own_0, near_11)
    near_31, near_21 = swap(found_31, "y", 3), swap(found_21, "y", 2)
    own_1 = found_01 + near_11
    rows_1 = exchange(
        after(own_1, rows_0, near_30, near_20, found_31, parts[1], parts[3]), "z"
    )
    rows_2 = exchange(after(near_20 + near_30, rows_1, near_21, parts[2]), "z")
    other_1 = near_21 + near_31
    rows_3 = exchange(after(other_1, rows_2), "z")
    chunks = [rows_0, rows_1, rows_2, rows_3]
    parts = after(tuple(parts + [swap(part, "core", 1) for part in parts]), rows_1, other_1)
    halves = pl.pallas_call(
        arrange_kernel,
        out_shape=jax.ShapeDtypeStruct((X, CORE, SHARD, *piece.shape), piece.dtype),
        in_specs=[in_smem] + [in_vmem] * GRP,
        **limits,
    )(place, *parts)
    slot_query = slot_query.reshape(Z, 2, q_dev)
    slot_query = jnp.where(my_y // 2 == 0, slot_query, slot_query[:, ::-1])
    slot_query = jnp.concatenate(
        [slot_query[:, pair, cut].reshape(1, -1) for pair in range(2) for cut in cuts], axis=1
    )

    inner_full = [
        columns_to_rows(halves[g // CORE, g % CORE, :, :deep], wide).reshape(width, wide)
        for g in range(GRP)
    ]
    outer_full = halves[:, :, :, deep:].transpose(2, 0, 1, 3, 4).reshape(hid, width)

    pre_act = jnp.concatenate(
        [jnp.dot(queries, part, preferred_element_type=jnp.float32) for part in inner_full], axis=1
    )
    hidden = gelu_value(pre_act).astype(jnp.bfloat16)
    slope = gelu_slope(pre_act)
    projected = jnp.dot(hidden, outer_full, preferred_element_type=jnp.float32)
    embedded = (queries.astype(jnp.float32) + projected).astype(jnp.bfloat16)

    half = width // CORE
    outer_cut = jax.ShapeDtypeStruct((Y, X, hid // Y // X, half), jnp.bfloat16)
    losses, query_grad, outer, outer_sent = pl.pallas_call(
        functools.partial(score_kernel, scale),
        out_shape=[
            jax.ShapeDtypeStruct((q_dev, 1), jnp.float32),
            jax.ShapeDtypeStruct((q_dev, width), jnp.bfloat16),
            outer_cut,
            outer_cut,
        ],
        in_specs=[in_smem] + [in_vmem] * (4 + CHUNKS),
        **limits,
    )(place, embedded, positives, hidden, slot_query, *chunks)
    outer_sent = swap(outer_sent, "core", 1)
    inner, inner_sent = pl.pallas_call(
        inner_kernel,
        out_shape=[jax.ShapeDtypeStruct((X, width, wide), jnp.bfloat16)] * 2,
        in_specs=[in_smem] + [in_vmem] * 4,
        **limits,
    )(place, queries, query_grad, slope, outer_full)
    inner_sent = swap(inner_sent, "core", 1)

    narrow = lambda value: value.astype(jnp.bfloat16)
    outer = exchange(narrow(total_of([outer, outer_sent])), "y")
    inner = [narrow(total_of([inner[by], inner_sent[by]])) for by in range(X)]
    inner = inner[:1] + [swap(inner[by], "x", by) for by in range(1, X)]
    outer = narrow(total_of(list(outer)))
    inner = after(tuple(inner), outer)
    outer = exchange(outer, "x")
    inner = narrow(total_of(inner)).reshape(Z, Y, inner_rows, wide)
    inner = [lax.dynamic_index_in_dim(inner, my_y ^ by, 1, False) for by in range(Y)]
    inner = inner[:1] + [swap(inner[by], "y", by) for by in range(1, Y)]
    lanes = 128
    both = jnp.concatenate(
        [
            columns_to_rows(total_of(inner), lanes),
            columns_to_rows(total_of(list(outer)).reshape(Z, -1, half), lanes),
        ],
        axis=1,
    )
    both = total_of(list(exchange(narrow(both), "z")))
    both = spread(both, ("x", "core"), GRP)
    inner_deep = inner_rows * wide // lanes
    inner = rows_to_columns(both[:, :inner_deep], inner_rows)
    outer = rows_to_columns(both[:, inner_deep:], outer_rows // X)
    inner = jnp.concatenate(list(inner), axis=1)
    outer = jnp.concatenate(
        [jnp.concatenate([outer[x * CORE + c] for c in range(CORE)], axis=1) for x in range(X)],
        axis=0,
    )
    return (losses.reshape(-1), inner, outer)


def solution(mesh):
    fine = Mesh(mesh.devices.reshape(X, CORE, Z, Y), ("x", "core", "z", "y"))
    blocks, rows = ("x", "core", "z", "y"), ("z", "y")
    return jax.shard_map(
        shards,
        mesh=fine,
        in_specs=(
            P(blocks, None),
            P(blocks, None),
            P(blocks, None),
            P(rows, None),
            P(rows, None),
            P(rows, None),
        ),
        out_specs=(P(blocks), P(rows, None), P(rows, None)),
        check_vma=False,
    )
```

```python
import functools

import jax
import jax.numpy as jnp
from jax import lax
from jax.experimental import pallas as pl
from jax.experimental.pallas import tpu as pltpu
from jax.sharding import Mesh, PartitionSpec as P

X, CORE, Z, Y = 4, 2, 8, 4
GRP, SHARD = X * CORE, Z * Y
PAIRS = SHARD // 2
CHUNKS = 4
VMEM = 50 * 1024 * 1024


def gelu_value(pre_act):
    return pre_act * 0.5 * (1.0 + lax.erf(pre_act * 0.7071067811865476))


def gelu_slope(pre_act):
    return (
        0.5 * (1.0 + lax.erf(pre_act * 0.7071067811865476))
        + pre_act * jnp.exp(-0.5 * pre_act * pre_act) * 0.3989422804014327
    )


def contract_first(left, right):
    return lax.dot_general(
        left, right, (((0,), (0,)), ((), ())), preferred_element_type=jnp.float32
    )


def contract_last(left, right):
    return lax.dot_general(
        left, right, (((1,), (1,)), ((), ())), preferred_element_type=jnp.float32
    )


def exchange(value, axes):
    return lax.all_to_all(value, axes, split_axis=0, concat_axis=0, tiled=True)


def spread(value, axes, count):
    return exchange(jnp.broadcast_to(value[None], (count, *value.shape)), axes)


def swap(value, axis, by):
    return lax.ppermute(value, axis, [(i, i ^ by) for i in range(lax.axis_size(axis))])


def after(value, *done):
    return lax.optimization_barrier((value, *done))[0]


def request_kernel(shift, ids_ref, code_ref, query_ref):
    ids = ids_ref[...]
    q_dev, neg = ids.shape
    lane = lax.broadcasted_iota(jnp.int32, (q_dev, q_dev), 1)
    query = lax.broadcasted_iota(jnp.int32, (q_dev, q_dev), 0)
    before = (lane < query).astype(jnp.float32).astype(jnp.bfloat16)
    kind, pair_lane = lane // PAIRS, lane % PAIRS
    seen = jnp.zeros((1, q_dev), jnp.float32)
    placed = jnp.zeros((q_dev, q_dev), jnp.float32)
    for k in range(neg):
        id_k = ids[:, k : k + 1]
        owner = id_k >> shift
        odd = owner & 1
        member = owner == lane
        ones = member.astype(jnp.float32)
        counts = seen + jnp.dot(before, ones.astype(jnp.bfloat16), preferred_element_type=jnp.float32)
        rank = jnp.sum(jnp.where(member, counts, 0.0), axis=1, keepdims=True).astype(jnp.int32)
        seen = seen + jnp.sum(ones, axis=0, keepdims=True)
        slot = jnp.where(odd == 1, q_dev - 1 - rank, rank)
        at_slot = (slot == lane).astype(jnp.float32).astype(jnp.bfloat16)
        code = (odd << shift) + (id_k - (owner << shift))
        item = jnp.where(
            kind == 0, code >> 6, jnp.where(kind == 1, code & 63, jnp.where(kind == 2, query, 0))
        )
        item = jnp.where((owner >> 1) == pair_lane, item, 0)
        placed = placed + contract_first(item.astype(jnp.float32).astype(jnp.bfloat16), at_slot)
    code_ref[...] = (placed[:PAIRS] * 64.0 + placed[PAIRS : 2 * PAIRS]).astype(jnp.int32)
    query_ref[...] = placed[2 * PAIRS : 3 * PAIRS].astype(jnp.int32)


def arrange_kernel(place_ref, *refs):
    part_refs, out_ref = refs[:GRP], refs[GRP]
    for by_core in range(CORE):
        for by_x in range(X):
            at = place_ref[0] ^ by_x, place_ref[1] ^ by_core
            out_ref[at] = part_refs[by_core * X + by_x][...]


def score_kernel(scale, place_ref, embedded_ref, positives_ref, hidden_ref, query_ref, *refs):
    row_refs, (loss_ref, grad_ref, keep_ref, send_ref) = refs[:CHUNKS], refs[CHUNKS:]
    embedded = embedded_ref[...]
    positives = positives_ref[...].astype(jnp.float32)
    q_dev, width = embedded.shape
    pos_scores = (
        jnp.sum(embedded.astype(jnp.float32) * positives, axis=1, keepdims=True) * scale
    )
    total = jnp.exp(pos_scores)
    per = row_refs[0].shape[0]
    query = lax.broadcasted_iota(jnp.int32, (q_dev, per), 0)
    scores, members = [], []
    for c in range(CHUNKS):
        score = contract_last(embedded, row_refs[c][...]) * scale
        member = query_ref[:, c * per : (c + 1) * per] == query
        total = total + jnp.sum(jnp.where(member, jnp.exp(score), 0.0), axis=1, keepdims=True)
        scores.append(score)
        members.append(member)
    log_total = jnp.log(total)
    loss_ref[...] = log_total - pos_scores
    grad = (jnp.exp(pos_scores - log_total) - 1.0) * positives
    for c in range(CHUNKS):
        weight = jnp.where(members[c], jnp.exp(scores[c] - log_total), 0.0)
        high = weight.astype(jnp.bfloat16)
        low = (weight - high.astype(jnp.float32)).astype(jnp.bfloat16)
        rows = row_refs[c][...]
        grad = grad + jnp.dot(high, rows, preferred_element_type=jnp.float32)
        grad = grad + jnp.dot(low, rows, preferred_element_type=jnp.float32)
    query_grad = (grad * scale).astype(jnp.bfloat16)
    grad_ref[...] = query_grad
    my_core = place_ref[1]
    hid = hidden_ref.shape[1]
    deep, part, half = hid // SHARD // X, hid // Z, width // CORE
    for z in range(Z):
        outer = contract_first(hidden_ref[:, z * part : (z + 1) * part], query_grad)
        left, right = outer[:, :half], outer[:, half:]
        keep = jnp.where(my_core == 0, left, right).astype(jnp.bfloat16)
        send = jnp.where(my_core == 0, right, left).astype(jnp.bfloat16)
        for y in range(Y):
            for x in range(X):
                rows = slice((y * X + x) * deep, (y * X + x + 1) * deep)
                keep_ref[y, x, z * deep : (z + 1) * deep, :] = keep[rows]
                send_ref[y, x, z * deep : (z + 1) * deep, :] = send[rows]


def inner_kernel(place_ref, queries_ref, grad_ref, slope_ref, weight_ref, keep_ref, send_ref):
    queries, query_grad = queries_ref[...], grad_ref[...]
    part = weight_ref.shape[0] // GRP
    for by_core, out_ref in ((1, send_ref), (0, keep_ref)):
        for by_x in range(X):
            group = (place_ref[0] ^ by_x) * CORE + (place_ref[1] ^ by_core)
            at = pl.ds(pl.multiple_of(group * part, part), part)
            hidden_grad = contract_last(query_grad, weight_ref[at, :])
            pre_grad = (hidden_grad * slope_ref[:, at]).astype(jnp.bfloat16)
            out_ref[by_x] = contract_first(queries, pre_grad).astype(jnp.bfloat16)


def total_of(parts):
    return sum(part.astype(jnp.float32) for part in parts)


def columns_to_rows(value, wide):
    return jnp.concatenate(
        [value[..., i : i + wide] for i in range(0, value.shape[-1], wide)], axis=-2
    )


def rows_to_columns(value, deep):
    return jnp.concatenate(
        [value[..., i : i + deep, :] for i in range(0, value.shape[-2], deep)], axis=-1
    )


def shards(queries, positives, negative_ids, passage_table, inner_weight, outer_weight):
    q_dev, width = queries.shape
    rows_dev = passage_table.shape[0]
    shift = rows_dev.bit_length() - 1
    hid = inner_weight.shape[1]
    inner_rows, outer_rows = inner_weight.shape[0], outer_weight.shape[0]
    scale = float(width) ** (-0.5)
    limits = {"compiler_params": pltpu.CompilerParams(vmem_limit_bytes=VMEM)}
    my_x, my_core, my_y = (lax.axis_index(axis) for axis in ("x", "core", "y"))
    group = my_x * CORE + my_core
    place = jnp.stack([my_x, my_core]).astype(jnp.int32)
    in_smem = pl.BlockSpec(memory_space=pltpu.SMEM)
    in_vmem = pl.BlockSpec(memory_space=pltpu.VMEM)

    slots = jax.ShapeDtypeStruct((PAIRS, q_dev), jnp.int32)
    code, slot_query = pl.pallas_call(
        functools.partial(request_kernel, shift), out_shape=[slots] * 2, **limits
    )(negative_ids)
    code = exchange(
        jnp.broadcast_to(code[:, None], (PAIRS, 2, q_dev)).reshape(SHARD, q_dev), ("z", "y")
    ).reshape(Z, Y, q_dev)
    code = jnp.stack([lax.dynamic_index_in_dim(code, my_y ^ by, 1, False) for by in range(Y)])
    own = (code >> shift) == my_y % 2
    wanted = code & (rows_dev - 1)
    wanted = lax.optimization_barrier((wanted[:, :, : q_dev // 2], wanted[:, :, q_dev // 2 :]))
    per = q_dev // 2
    cuts = slice(0, per), slice(per, q_dev)

    def find(picks, *done):
        ids = jnp.stack([wanted[part][by] for by, part in picks])
        ids = after(ids.reshape(-1), *done)
        found = passage_table.at[ids].get(mode="promise_in_bounds").reshape(-1, Z * per, width)
        return [
            jnp.where(own[by, :, cuts[part]].reshape(-1, 1), found[i], jnp.zeros((), found.dtype))
            for i, (by, part) in enumerate(picks)
        ]

    wide, deep = hid // GRP, outer_rows // GRP
    inner_piece = lax.dynamic_slice(inner_weight, (0, group * wide), (inner_rows, wide))
    outer_piece = lax.dynamic_slice(outer_weight, (group * deep, 0), (deep, width))
    piece = jnp.concatenate([rows_to_columns(inner_piece, deep), outer_piece], axis=0)

    found_10, found_30 = find([(1, 0), (3, 0)])
    near_10, near_30 = swap(found_10, "y", 1), swap(found_30, "y", 3)
    gathered = spread(after(piece, found_10), ("z", "y"), SHARD)
    found_11, found_31, found_00 = find([(1, 1), (3, 1), (0, 0)], found_10)
    near_11, near_31 = swap(found_11, "y", 1), swap(found_31, "y", 3)
    found_20, found_01 = find([(2, 0), (0, 1)], found_11, near_10, near_30)
    near_20 = swap(found_20, "y", 2)
    own_0 = after(found_00 + after(near_10, found_11, found_31), gathered, near_30)
    rows_0 = exchange(own_0, "z")
    gathered = after(gathered, own_0)
    parts = [gathered] + [swap(gathered, "x", by) for by in range(1, X)]
    (found_21,) = find([(2, 1)], own_0)
    near_21 = swap(found_21, "y", 2)
    own_1 = found_01 + after(near_11, own_0)
    rows_1 = exchange(
        after(own_1, rows_0, near_31, near_20, found_21, parts[1], parts[3]), "z"
    )
    rows_2 = exchange(after(near_20 + near_30, rows_1, near_21, parts[2]), "z")
    other_1 = near_21 + near_31
    rows_3 = exchange(after(other_1, rows_2), "z")
    chunks = [rows_0, rows_1, rows_2, rows_3]
    parts = after(tuple(parts + [swap(part, "core", 1) for part in parts]), rows_1, other_1)
    halves = pl.pallas_call(
        arrange_kernel,
        out_shape=jax.ShapeDtypeStruct((X, CORE, SHARD, *piece.shape), piece.dtype),
        in_specs=[in_smem] + [in_vmem] * GRP,
        **limits,
    )(place, *parts)
    slot_query = slot_query.reshape(Z, 2, q_dev)
    slot_query = jnp.where(my_y // 2 == 0, slot_query, slot_query[:, ::-1])
    slot_query = jnp.concatenate(
        [slot_query[:, pair, cut].reshape(1, -1) for pair in range(2) for cut in cuts], axis=1
    )

    inner_full = [
        columns_to_rows(halves[g // CORE, g % CORE, :, :deep], wide).reshape(width, wide)
        for g in range(GRP)
    ]
    outer_full = halves[:, :, :, deep:].transpose(2, 0, 1, 3, 4).reshape(hid, width)

    pre_act = jnp.concatenate(
        [jnp.dot(queries, part, preferred_element_type=jnp.float32) for part in inner_full], axis=1
    )
    hidden = gelu_value(pre_act).astype(jnp.bfloat16)
    slope = gelu_slope(pre_act)
    projected = jnp.dot(hidden, outer_full, preferred_element_type=jnp.float32)
    embedded = (queries.astype(jnp.float32) + projected).astype(jnp.bfloat16)

    half = width // CORE
    outer_cut = jax.ShapeDtypeStruct((Y, X, hid // Y // X, half), jnp.bfloat16)
    losses, query_grad, outer, outer_sent = pl.pallas_call(
        functools.partial(score_kernel, scale),
        out_shape=[
            jax.ShapeDtypeStruct((q_dev, 1), jnp.float32),
            jax.ShapeDtypeStruct((q_dev, width), jnp.bfloat16),
            outer_cut,
            outer_cut,
        ],
        in_specs=[in_smem] + [in_vmem] * (4 + CHUNKS),
        **limits,
    )(place, embedded, positives, hidden, slot_query, *chunks)
    outer_sent = swap(outer_sent, "core", 1)
    inner, inner_sent = pl.pallas_call(
        inner_kernel,
        out_shape=[jax.ShapeDtypeStruct((X, width, wide), jnp.bfloat16)] * 2,
        in_specs=[in_smem] + [in_vmem] * 4,
        **limits,
    )(place, queries, query_grad, slope, outer_full)
    inner_sent = swap(inner_sent, "core", 1)

    narrow = lambda value: value.astype(jnp.bfloat16)
    outer = exchange(narrow(total_of([outer, outer_sent])), "y")
    inner = [narrow(total_of([inner[by], inner_sent[by]])) for by in range(X)]
    inner = inner[:1] + [swap(inner[by], "x", by) for by in range(1, X)]
    outer = narrow(total_of(list(outer)))
    inner = after(tuple(inner), outer)
    outer = exchange(outer, "x")
    inner = narrow(total_of(inner)).reshape(Z, Y, inner_rows, wide)
    inner = [lax.dynamic_index_in_dim(inner, my_y ^ by, 1, False) for by in range(Y)]
    inner = inner[:1] + [swap(inner[by], "y", by) for by in range(1, Y)]
    lanes = 128
    both = jnp.concatenate(
        [
            columns_to_rows(total_of(inner), lanes),
            columns_to_rows(total_of(list(outer)).reshape(Z, -1, half), lanes),
        ],
        axis=1,
    )
    both = total_of(list(exchange(narrow(both), "z")))
    both = spread(both, ("x", "core"), GRP)
    inner_deep = inner_rows * wide // lanes
    inner = rows_to_columns(both[:, :inner_deep], inner_rows)
    outer = rows_to_columns(both[:, inner_deep:], outer_rows // X)
    inner = jnp.concatenate(list(inner), axis=1)
    outer = jnp.concatenate(
        [jnp.concatenate([outer[x * CORE + c] for c in range(CORE)], axis=1) for x in range(X)],
        axis=0,
    )
    return (losses.reshape(-1), inner, outer)


def solution(mesh):
    fine = Mesh(mesh.devices.reshape(X, CORE, Z, Y), ("x", "core", "z", "y"))
    blocks, rows = ("x", "core", "z", "y"), ("z", "y")
    return jax.shard_map(
        shards,
        mesh=fine,
        in_specs=(
            P(blocks, None),
            P(blocks, None),
            P(blocks, None),
            P(rows, None),
            P(rows, None),
            P(rows, None),
        ),
        out_specs=(P(blocks), P(rows, None), P(rows, None)),
        check_vma=False,
    )
```

```python
import functools

import jax
import jax.numpy as jnp
from jax import lax
from jax.experimental import pallas as pl
from jax.experimental.pallas import tpu as pltpu
from jax.sharding import Mesh, PartitionSpec as P

X, CORE, Z, Y = 4, 2, 8, 4
GRP, SHARD = X * CORE, Z * Y
PAIRS = SHARD // 2
CHUNKS = 4
VMEM = 50 * 1024 * 1024


def gelu_value(pre_act):
    return pre_act * 0.5 * (1.0 + lax.erf(pre_act * 0.7071067811865476))


def gelu_slope(pre_act):
    return (
        0.5 * (1.0 + lax.erf(pre_act * 0.7071067811865476))
        + pre_act * jnp.exp(-0.5 * pre_act * pre_act) * 0.3989422804014327
    )


def contract_first(left, right):
    return lax.dot_general(
        left, right, (((0,), (0,)), ((), ())), preferred_element_type=jnp.float32
    )


def contract_last(left, right):
    return lax.dot_general(
        left, right, (((1,), (1,)), ((), ())), preferred_element_type=jnp.float32
    )


def exchange(value, axes):
    return lax.all_to_all(value, axes, split_axis=0, concat_axis=0, tiled=True)


def spread(value, axes, count):
    return exchange(jnp.broadcast_to(value[None], (count, *value.shape)), axes)


def swap(value, axis, by):
    return lax.ppermute(value, axis, [(i, i ^ by) for i in range(lax.axis_size(axis))])


def after(value, *done):
    return lax.optimization_barrier((value, *done))[0]


def request_kernel(shift, ids_ref, code_ref, query_ref):
    ids = ids_ref[...]
    q_dev, neg = ids.shape
    lane = lax.broadcasted_iota(jnp.int32, (q_dev, q_dev), 1)
    query = lax.broadcasted_iota(jnp.int32, (q_dev, q_dev), 0)
    before = (lane < query).astype(jnp.float32).astype(jnp.bfloat16)
    kind, pair_lane = lane // PAIRS, lane % PAIRS
    seen = jnp.zeros((1, q_dev), jnp.float32)
    placed = jnp.zeros((q_dev, q_dev), jnp.float32)
    for k in range(neg):
        id_k = ids[:, k : k + 1]
        owner = id_k >> shift
        odd = owner & 1
        member = owner == lane
        ones = member.astype(jnp.float32)
        counts = seen + jnp.dot(before, ones.astype(jnp.bfloat16), preferred_element_type=jnp.float32)
        rank = jnp.sum(jnp.where(member, counts, 0.0), axis=1, keepdims=True).astype(jnp.int32)
        seen = seen + jnp.sum(ones, axis=0, keepdims=True)
        slot = jnp.where(odd == 1, q_dev - 1 - rank, rank)
        at_slot = (slot == lane).astype(jnp.float32).astype(jnp.bfloat16)
        code = (odd << shift) + (id_k - (owner << shift))
        item = jnp.where(
            kind == 0, code >> 6, jnp.where(kind == 1, code & 63, jnp.where(kind == 2, query, 0))
        )
        item = jnp.where((owner >> 1) == pair_lane, item, 0)
        placed = placed + contract_first(item.astype(jnp.float32).astype(jnp.bfloat16), at_slot)
    code_ref[...] = (placed[:PAIRS] * 64.0 + placed[PAIRS : 2 * PAIRS]).astype(jnp.int32)
    query_ref[...] = placed[2 * PAIRS : 3 * PAIRS].astype(jnp.int32)


def arrange_kernel(place_ref, *refs):
    part_refs, out_ref = refs[:GRP], refs[GRP]
    for by_core in range(CORE):
        for by_x in range(X):
            at = place_ref[0] ^ by_x, place_ref[1] ^ by_core
            out_ref[at] = part_refs[by_core * X + by_x][...]


def weighted_rows(weight, rows):
    high = weight.astype(jnp.bfloat16)
    low = (weight - high.astype(jnp.float32)).astype(jnp.bfloat16)
    return jnp.dot(high, rows, preferred_element_type=jnp.float32) + jnp.dot(
        low, rows, preferred_element_type=jnp.float32
    )


def early_kernel(scale, embedded_ref, positives_ref, query_ref, *refs):
    row_refs, (stats_ref, sum_ref) = refs[: CHUNKS - 1], refs[CHUNKS - 1 :]
    embedded = embedded_ref[...]
    positives = positives_ref[...].astype(jnp.float32)
    q_dev = embedded.shape[0]
    pos_scores = (
        jnp.sum(embedded.astype(jnp.float32) * positives, axis=1, keepdims=True) * scale
    )
    per = row_refs[0].shape[0]
    query = lax.broadcasted_iota(jnp.int32, (q_dev, per), 0)
    scores, members, largest = [], [], pos_scores
    for c in range(CHUNKS - 1):
        score = contract_last(embedded, row_refs[c][...]) * scale
        member = query_ref[:, c * per : (c + 1) * per] == query
        seen = jnp.where(member, score, pos_scores)
        largest = jnp.maximum(largest, jnp.max(seen, axis=1, keepdims=True))
        scores.append(score)
        members.append(member)
    total = jnp.exp(pos_scores - largest)
    grad = jnp.zeros(sum_ref.shape, jnp.float32)
    for c in range(CHUNKS - 1):
        weight = jnp.where(members[c], jnp.exp(scores[c] - largest), 0.0)
        total = total + jnp.sum(weight, axis=1, keepdims=True)
        grad = grad + weighted_rows(weight, row_refs[c][...])
    stats_ref[0] = pos_scores
    stats_ref[1] = largest
    stats_ref[2] = total
    sum_ref[...] = grad


def score_kernel(
    scale, place_ref, embedded_ref, positives_ref, hidden_ref, query_ref, stats_ref, sum_ref,
    rows_ref, loss_ref, grad_ref, keep_ref, send_ref,
):
    embedded = embedded_ref[...]
    positives = positives_ref[...].astype(jnp.float32)
    q_dev, width = embedded.shape
    pos_scores, early, total = stats_ref[0], stats_ref[1], stats_ref[2]
    rows = rows_ref[...]
    per = rows.shape[0]
    score = contract_last(embedded, rows) * scale
    member = query_ref[:, (CHUNKS - 1) * per :] == lax.broadcasted_iota(
        jnp.int32, (q_dev, per), 0
    )
    largest = jnp.maximum(
        early, jnp.max(jnp.where(member, score, early), axis=1, keepdims=True)
    )
    late = jnp.where(member, jnp.exp(score - largest), 0.0)
    total = total * jnp.exp(early - largest) + jnp.sum(late, axis=1, keepdims=True)
    log_total = largest + jnp.log(total)
    loss_ref[...] = log_total - pos_scores
    grad = (jnp.exp(pos_scores - log_total) - 1.0) * positives
    grad = grad + jnp.exp(early - log_total) * sum_ref[...]
    grad = grad + weighted_rows(late * (1.0 / total), rows)
    query_grad = (grad * scale).astype(jnp.bfloat16)
    grad_ref[...] = query_grad
    my_core = place_ref[1]
    hid = hidden_ref.shape[1]
    deep, part, half = hid // SHARD // X, hid // Z, width // CORE
    for z in range(Z):
        outer = contract_first(hidden_ref[:, z * part : (z + 1) * part], query_grad)
        left, right = outer[:, :half], outer[:, half:]
        keep = jnp.where(my_core == 0, left, right).astype(jnp.bfloat16)
        send = jnp.where(my_core == 0, right, left).astype(jnp.bfloat16)
        for y in range(Y):
            for x in range(X):
                rows = slice((y * X + x) * deep, (y * X + x + 1) * deep)
                keep_ref[y, x, z * deep : (z + 1) * deep, :] = keep[rows]
                send_ref[y, x, z * deep : (z + 1) * deep, :] = send[rows]


def inner_kernel(place_ref, queries_ref, grad_ref, slope_ref, weight_ref, keep_ref, send_ref):
    queries, query_grad = queries_ref[...], grad_ref[...]
    part = weight_ref.shape[0] // GRP
    for by_core, out_ref in ((1, send_ref), (0, keep_ref)):
        for by_x in range(X):
            group = (place_ref[0] ^ by_x) * CORE + (place_ref[1] ^ by_core)
            at = pl.ds(pl.multiple_of(group * part, part), part)
            hidden_grad = contract_last(query_grad, weight_ref[at, :])
            pre_grad = (hidden_grad * slope_ref[:, at]).astype(jnp.bfloat16)
            out_ref[by_x] = contract_first(queries, pre_grad).astype(jnp.bfloat16)


def total_of(parts):
    return sum(part.astype(jnp.float32) for part in parts)


def columns_to_rows(value, wide):
    return jnp.concatenate(
        [value[..., i : i + wide] for i in range(0, value.shape[-1], wide)], axis=-2
    )


def rows_to_columns(value, deep):
    return jnp.concatenate(
        [value[..., i : i + deep, :] for i in range(0, value.shape[-2], deep)], axis=-1
    )


def shards(queries, positives, negative_ids, passage_table, inner_weight, outer_weight):
    q_dev, width = queries.shape
    rows_dev = passage_table.shape[0]
    shift = rows_dev.bit_length() - 1
    hid = inner_weight.shape[1]
    inner_rows, outer_rows = inner_weight.shape[0], outer_weight.shape[0]
    scale = float(width) ** (-0.5)
    limits = {"compiler_params": pltpu.CompilerParams(vmem_limit_bytes=VMEM)}
    my_x, my_core, my_y = (lax.axis_index(axis) for axis in ("x", "core", "y"))
    group = my_x * CORE + my_core
    place = jnp.stack([my_x, my_core]).astype(jnp.int32)
    in_smem = pl.BlockSpec(memory_space=pltpu.SMEM)
    in_vmem = pl.BlockSpec(memory_space=pltpu.VMEM)

    slots = jax.ShapeDtypeStruct((PAIRS, q_dev), jnp.int32)
    code, slot_query = pl.pallas_call(
        functools.partial(request_kernel, shift), out_shape=[slots] * 2, **limits
    )(negative_ids)
    code = exchange(
        jnp.broadcast_to(code[:, None], (PAIRS, 2, q_dev)).reshape(SHARD, q_dev), ("z", "y")
    ).reshape(Z, Y, q_dev)
    code = jnp.stack([lax.dynamic_index_in_dim(code, my_y ^ by, 1, False) for by in range(Y)])
    own = (code >> shift) == my_y % 2
    wanted = code & (rows_dev - 1)
    wanted = lax.optimization_barrier((wanted[:, :, : q_dev // 2], wanted[:, :, q_dev // 2 :]))
    per = q_dev // 2
    cuts = slice(0, per), slice(per, q_dev)

    def find(picks, *done):
        ids = jnp.stack([wanted[part][by] for by, part in picks])
        ids = after(ids.reshape(-1), *done)
        found = passage_table.at[ids].get(mode="promise_in_bounds").reshape(-1, Z * per, width)
        return [
            jnp.where(own[by, :, cuts[part]].reshape(-1, 1), found[i], jnp.zeros((), found.dtype))
            for i, (by, part) in enumerate(picks)
        ]

    wide, deep = hid // GRP, outer_rows // GRP
    inner_piece = lax.dynamic_slice(inner_weight, (0, group * wide), (inner_rows, wide))
    outer_piece = lax.dynamic_slice(outer_weight, (group * deep, 0), (deep, width))
    piece = jnp.concatenate([rows_to_columns(inner_piece, deep), outer_piece], axis=0)

    found_10, found_30 = find([(1, 0), (3, 0)])
    near_10, near_30 = swap(found_10, "y", 1), swap(found_30, "y", 3)
    gathered = spread(after(piece, found_10), ("z", "y"), SHARD)
    found_11, found_31, found_00 = find([(1, 1), (3, 1), (0, 0)], found_10)
    near_11, near_31 = swap(found_11, "y", 1), swap(found_31, "y", 3)
    found_20, found_01 = find([(2, 0), (0, 1)], found_11, near_10, near_30)
    near_20 = swap(found_20, "y", 2)
    own_0 = after(found_00 + after(near_10, found_11, found_31), gathered, near_30)
    rows_0 = exchange(own_0, "z")
    gathered = after(gathered, own_0)
    parts = [gathered] + [swap(gathered, "x", by) for by in range(1, X)]
    (found_21,) = find([(2, 1)], own_0, parts[1], parts[3])
    near_21 = swap(found_21, "y", 2)
    own_1 = found_01 + after(near_11, own_0)
    rows_1 = exchange(after(own_1, rows_0, near_31), "z")
    rows_2 = exchange(after(near_20 + near_30, rows_1, parts[2], found_21), "z")
    other_1 = near_21 + near_31
    rows_3 = exchange(after(other_1, rows_2), "z")
    chunks = [rows_0, rows_1, rows_2, rows_3]
    parts = after(tuple(parts + [swap(part, "core", 1) for part in parts]), rows_1)
    halves = pl.pallas_call(
        arrange_kernel,
        out_shape=jax.ShapeDtypeStruct((X, CORE, SHARD, *piece.shape), piece.dtype),
        in_specs=[in_smem] + [in_vmem] * GRP,
        **limits,
    )(place, *parts)
    slot_query = slot_query.reshape(Z, 2, q_dev)
    slot_query = jnp.where(my_y // 2 == 0, slot_query, slot_query[:, ::-1])
    slot_query = jnp.concatenate(
        [slot_query[:, pair, cut].reshape(1, -1) for pair in range(2) for cut in cuts], axis=1
    )

    inner_full = [
        columns_to_rows(halves[g // CORE, g % CORE, :, :deep], wide).reshape(width, wide)
        for g in range(GRP)
    ]
    outer_full = halves[:, :, :, deep:].transpose(2, 0, 1, 3, 4).reshape(hid, width)

    pre_act = jnp.concatenate(
        [jnp.dot(queries, part, preferred_element_type=jnp.float32) for part in inner_full], axis=1
    )
    hidden = gelu_value(pre_act).astype(jnp.bfloat16)
    slope = gelu_slope(pre_act)
    projected = jnp.dot(hidden, outer_full, preferred_element_type=jnp.float32)
    embedded = (queries.astype(jnp.float32) + projected).astype(jnp.bfloat16)

    half = width // CORE
    outer_cut = jax.ShapeDtypeStruct((Y, X, hid // Y // X, half), jnp.bfloat16)
    stats, early_sum = pl.pallas_call(
        functools.partial(early_kernel, scale),
        out_shape=[
            jax.ShapeDtypeStruct((3, q_dev, 1), jnp.float32),
            jax.ShapeDtypeStruct((q_dev, width), jnp.float32),
        ],
        **limits,
    )(embedded, positives, slot_query, *chunks[:-1])
    losses, query_grad, outer, outer_sent = pl.pallas_call(
        functools.partial(score_kernel, scale),
        out_shape=[
            jax.ShapeDtypeStruct((q_dev, 1), jnp.float32),
            jax.ShapeDtypeStruct((q_dev, width), jnp.bfloat16),
            outer_cut,
            outer_cut,
        ],
        in_specs=[in_smem] + [in_vmem] * 7,
        **limits,
    )(place, embedded, positives, hidden, slot_query, stats, early_sum, chunks[-1])
    outer_sent = swap(outer_sent, "core", 1)
    inner, inner_sent = pl.pallas_call(
        inner_kernel,
        out_shape=[jax.ShapeDtypeStruct((X, width, wide), jnp.bfloat16)] * 2,
        in_specs=[in_smem] + [in_vmem] * 4,
        **limits,
    )(place, queries, query_grad, slope, outer_full)
    inner_sent = swap(inner_sent, "core", 1)

    narrow = lambda value: value.astype(jnp.bfloat16)
    outer = exchange(narrow(total_of([outer, outer_sent])), "y")
    inner = [narrow(total_of([inner[by], inner_sent[by]])) for by in range(X)]
    inner = inner[:1] + [swap(inner[by], "x", by) for by in range(1, X)]
    outer = narrow(total_of(list(outer)))
    inner = after(tuple(inner), outer)
    outer = exchange(outer, "x")
    inner = narrow(total_of(inner)).reshape(Z, Y, inner_rows, wide)
    inner = [lax.dynamic_index_in_dim(inner, my_y ^ by, 1, False) for by in range(Y)]
    inner = inner[:1] + [swap(inner[by], "y", by) for by in range(1, Y)]
    lanes = 128
    both = jnp.concatenate(
        [
            columns_to_rows(total_of(inner), lanes),
            columns_to_rows(total_of(list(outer)).reshape(Z, -1, half), lanes),
        ],
        axis=1,
    )
    both = total_of(list(exchange(narrow(both), "z")))
    both = spread(narrow(both), ("x", "core"), GRP).astype(jnp.float32)
    inner_deep = inner_rows * wide // lanes
    inner = rows_to_columns(both[:, :inner_deep], inner_rows)
    outer = rows_to_columns(both[:, inner_deep:], outer_rows // X)
    inner = jnp.concatenate(list(inner), axis=1)
    outer = jnp.concatenate(
        [jnp.concatenate([outer[x * CORE + c] for c in range(CORE)], axis=1) for x in range(X)],
        axis=0,
    )
    return (losses.reshape(-1), inner, outer)


def solution(mesh):
    fine = Mesh(mesh.devices.reshape(X, CORE, Z, Y), ("x", "core", "z", "y"))
    blocks, rows = ("x", "core", "z", "y"), ("z", "y")
    return jax.shard_map(
        shards,
        mesh=fine,
        in_specs=(
            P(blocks, None),
            P(blocks, None),
            P(blocks, None),
            P(rows, None),
            P(rows, None),
            P(rows, None),
        ),
        out_specs=(P(blocks), P(rows, None), P(rows, None)),
        check_vma=False,
    )
```

```python
import functools

import jax
import jax.numpy as jnp
from jax import lax
from jax.experimental import pallas as pl
from jax.experimental.pallas import tpu as pltpu
from jax.sharding import Mesh, PartitionSpec as P

X, CORE, Z, Y = 4, 2, 8, 4
GRP, SHARD = X * CORE, Z * Y
PAIRS = SHARD // 2
CHUNKS = 4
VMEM = 50 * 1024 * 1024


def gelu_value(pre_act):
    return pre_act * 0.5 * (1.0 + lax.erf(pre_act * 0.7071067811865476))


def gelu_slope(pre_act):
    return (
        0.5 * (1.0 + lax.erf(pre_act * 0.7071067811865476))
        + pre_act * jnp.exp(-0.5 * pre_act * pre_act) * 0.3989422804014327
    )


def contract_first(left, right):
    return lax.dot_general(
        left, right, (((0,), (0,)), ((), ())), preferred_element_type=jnp.float32
    )


def contract_last(left, right):
    return lax.dot_general(
        left, right, (((1,), (1,)), ((), ())), preferred_element_type=jnp.float32
    )


def exchange(value, axes):
    return lax.all_to_all(value, axes, split_axis=0, concat_axis=0, tiled=True)


def spread(value, axes, count):
    return exchange(jnp.broadcast_to(value[None], (count, *value.shape)), axes)


def swap(value, axis, by):
    return lax.ppermute(value, axis, [(i, i ^ by) for i in range(lax.axis_size(axis))])


def after(value, *done):
    return lax.optimization_barrier((value, *done))[0]


def request_kernel(shift, ids_ref, code_ref, query_ref):
    ids = ids_ref[...]
    q_dev, neg = ids.shape
    lane = lax.broadcasted_iota(jnp.int32, (q_dev, q_dev), 1)
    query = lax.broadcasted_iota(jnp.int32, (q_dev, q_dev), 0)
    before = (lane < query).astype(jnp.float32).astype(jnp.bfloat16)
    kind, pair_lane = lane // PAIRS, lane % PAIRS
    seen = jnp.zeros((1, q_dev), jnp.float32)
    placed = jnp.zeros((q_dev, q_dev), jnp.float32)
    for k in range(neg):
        id_k = ids[:, k : k + 1]
        owner = id_k >> shift
        odd = owner & 1
        member = owner == lane
        ones = member.astype(jnp.float32)
        counts = seen + jnp.dot(before, ones.astype(jnp.bfloat16), preferred_element_type=jnp.float32)
        rank = jnp.sum(jnp.where(member, counts, 0.0), axis=1, keepdims=True).astype(jnp.int32)
        seen = seen + jnp.sum(ones, axis=0, keepdims=True)
        slot = jnp.where(odd == 1, q_dev - 1 - rank, rank)
        at_slot = (slot == lane).astype(jnp.float32).astype(jnp.bfloat16)
        code = (odd << shift) + (id_k - (owner << shift))
        item = jnp.where(
            kind == 0, code >> 6, jnp.where(kind == 1, code & 63, jnp.where(kind == 2, query, 0))
        )
        item = jnp.where((owner >> 1) == pair_lane, item, 0)
        placed = placed + contract_first(item.astype(jnp.float32).astype(jnp.bfloat16), at_slot)
    code_ref[...] = (placed[:PAIRS] * 64.0 + placed[PAIRS : 2 * PAIRS]).astype(jnp.int32)
    query_ref[...] = placed[2 * PAIRS : 3 * PAIRS].astype(jnp.int32)


def arrange_kernel(place_ref, *refs):
    part_refs, out_ref = refs[:GRP], refs[GRP]
    for by_core in range(CORE):
        for by_x in range(X):
            at = place_ref[0] ^ by_x, place_ref[1] ^ by_core
            out_ref[at] = part_refs[by_core * X + by_x][...]


def weighted_rows(weight, rows):
    high = weight.astype(jnp.bfloat16)
    low = (weight - high.astype(jnp.float32)).astype(jnp.bfloat16)
    return jnp.dot(high, rows, preferred_element_type=jnp.float32) + jnp.dot(
        low, rows, preferred_element_type=jnp.float32
    )


def early_kernel(scale, embedded_ref, positives_ref, query_ref, *refs):
    row_refs, (stats_ref, sum_ref) = refs[: CHUNKS - 1], refs[CHUNKS - 1 :]
    embedded = embedded_ref[...]
    positives = positives_ref[...].astype(jnp.float32)
    q_dev = embedded.shape[0]
    pos_scores = (
        jnp.sum(embedded.astype(jnp.float32) * positives, axis=1, keepdims=True) * scale
    )
    per = row_refs[0].shape[0]
    query = lax.broadcasted_iota(jnp.int32, (q_dev, per), 0)
    scores, members, largest = [], [], pos_scores
    for c in range(CHUNKS - 1):
        score = contract_last(embedded, row_refs[c][...]) * scale
        member = query_ref[:, c * per : (c + 1) * per] == query
        seen = jnp.where(member, score, pos_scores)
        largest = jnp.maximum(largest, jnp.max(seen, axis=1, keepdims=True))
        scores.append(score)
        members.append(member)
    total = jnp.exp(pos_scores - largest)
    grad = jnp.zeros(sum_ref.shape, jnp.float32)
    for c in range(CHUNKS - 1):
        weight = jnp.where(members[c], jnp.exp(scores[c] - largest), 0.0)
        total = total + jnp.sum(weight, axis=1, keepdims=True)
        grad = grad + weighted_rows(weight, row_refs[c][...])
    stats_ref[0] = pos_scores
    stats_ref[1] = largest
    stats_ref[2] = total
    sum_ref[...] = grad


def score_kernel(
    scale, place_ref, embedded_ref, positives_ref, hidden_ref, query_ref, stats_ref, sum_ref,
    rows_ref, loss_ref, grad_ref, keep_ref, send_ref,
):
    embedded = embedded_ref[...]
    positives = positives_ref[...].astype(jnp.float32)
    q_dev, width = embedded.shape
    pos_scores, early, total = stats_ref[0], stats_ref[1], stats_ref[2]
    rows = rows_ref[...]
    per = rows.shape[0]
    score = contract_last(embedded, rows) * scale
    member = query_ref[:, (CHUNKS - 1) * per :] == lax.broadcasted_iota(
        jnp.int32, (q_dev, per), 0
    )
    largest = jnp.maximum(
        early, jnp.max(jnp.where(member, score, early), axis=1, keepdims=True)
    )
    late = jnp.where(member, jnp.exp(score - largest), 0.0)
    total = total * jnp.exp(early - largest) + jnp.sum(late, axis=1, keepdims=True)
    log_total = largest + jnp.log(total)
    loss_ref[...] = log_total - pos_scores
    grad = (jnp.exp(pos_scores - log_total) - 1.0) * positives
    grad = grad + jnp.exp(early - log_total) * sum_ref[...]
    grad = grad + weighted_rows(late * (1.0 / total), rows)
    query_grad = (grad * scale).astype(jnp.bfloat16)
    grad_ref[...] = query_grad
    my_core = place_ref[1]
    hid = hidden_ref.shape[1]
    deep, part, half = hid // SHARD // X, hid // Z, width // CORE
    for z in range(Z):
        outer = contract_first(hidden_ref[:, z * part : (z + 1) * part], query_grad)
        left, right = outer[:, :half], outer[:, half:]
        keep = jnp.where(my_core == 0, left, right).astype(jnp.bfloat16)
        send = jnp.where(my_core == 0, right, left).astype(jnp.bfloat16)
        for y in range(Y):
            for x in range(X):
                rows = slice((y * X + x) * deep, (y * X + x + 1) * deep)
                keep_ref[y, x, z * deep : (z + 1) * deep, :] = keep[rows]
                send_ref[y, x, z * deep : (z + 1) * deep, :] = send[rows]


def inner_kernel(place_ref, queries_ref, grad_ref, slope_ref, weight_ref, keep_ref, send_ref):
    queries, query_grad = queries_ref[...], grad_ref[...]
    part = weight_ref.shape[0] // GRP
    for by_core, out_ref in ((1, send_ref), (0, keep_ref)):
        for by_x in range(X):
            group = (place_ref[0] ^ by_x) * CORE + (place_ref[1] ^ by_core)
            at = pl.ds(pl.multiple_of(group * part, part), part)
            hidden_grad = contract_last(query_grad, weight_ref[at, :])
            pre_grad = (hidden_grad * slope_ref[:, at]).astype(jnp.bfloat16)
            out_ref[by_x] = contract_first(queries, pre_grad).astype(jnp.bfloat16)


def total_of(parts):
    return sum(part.astype(jnp.float32) for part in parts)


def columns_to_rows(value, wide):
    return jnp.concatenate(
        [value[..., i : i + wide] for i in range(0, value.shape[-1], wide)], axis=-2
    )


def rows_to_columns(value, deep):
    return jnp.concatenate(
        [value[..., i : i + deep, :] for i in range(0, value.shape[-2], deep)], axis=-1
    )


def shards(queries, positives, negative_ids, passage_table, inner_weight, outer_weight):
    q_dev, width = queries.shape
    rows_dev = passage_table.shape[0]
    shift = rows_dev.bit_length() - 1
    hid = inner_weight.shape[1]
    inner_rows, outer_rows = inner_weight.shape[0], outer_weight.shape[0]
    scale = float(width) ** (-0.5)
    limits = {"compiler_params": pltpu.CompilerParams(vmem_limit_bytes=VMEM)}
    my_x, my_core, my_y = (lax.axis_index(axis) for axis in ("x", "core", "y"))
    group = my_x * CORE + my_core
    place = jnp.stack([my_x, my_core]).astype(jnp.int32)
    in_smem = pl.BlockSpec(memory_space=pltpu.SMEM)
    in_vmem = pl.BlockSpec(memory_space=pltpu.VMEM)

    slots = jax.ShapeDtypeStruct((PAIRS, q_dev), jnp.int32)
    code, slot_query = pl.pallas_call(
        functools.partial(request_kernel, shift), out_shape=[slots] * 2, **limits
    )(negative_ids)
    code = exchange(
        jnp.broadcast_to(code[:, None], (PAIRS, 2, q_dev)).reshape(SHARD, q_dev), ("z", "y")
    ).reshape(Z, Y, q_dev)
    code = jnp.stack([lax.dynamic_index_in_dim(code, my_y ^ by, 1, False) for by in range(Y)])
    own = (code >> shift) == my_y % 2
    wanted = code & (rows_dev - 1)
    wanted = lax.optimization_barrier((wanted[:, :, : q_dev // 2], wanted[:, :, q_dev // 2 :]))
    per = q_dev // 2
    cuts = slice(0, per), slice(per, q_dev)

    def find(picks, *done):
        ids = jnp.stack([wanted[part][by] for by, part in picks])
        ids = after(ids.reshape(-1), *done)
        found = passage_table.at[ids].get(mode="promise_in_bounds").reshape(-1, Z * per, width)
        return [
            jnp.where(own[by, :, cuts[part]].reshape(-1, 1), found[i], jnp.zeros((), found.dtype))
            for i, (by, part) in enumerate(picks)
        ]

    wide, deep = hid // GRP, outer_rows // GRP
    inner_piece = lax.dynamic_slice(inner_weight, (0, group * wide), (inner_rows, wide))
    outer_piece = lax.dynamic_slice(outer_weight, (group * deep, 0), (deep, width))
    piece = jnp.concatenate([rows_to_columns(inner_piece, deep), outer_piece], axis=0)

    found_10, found_30 = find([(1, 0), (3, 0)])
    near_10, near_30 = swap(found_10, "y", 1), swap(found_30, "y", 3)
    gathered = spread(after(piece, found_10), ("z", "y"), SHARD)
    found_11, found_31, found_00 = find([(1, 1), (3, 1), (0, 0)], found_10)
    near_11, near_31 = swap(found_11, "y", 1), swap(found_31, "y", 3)
    found_20, found_01 = find([(2, 0), (0, 1)], found_11, near_10, near_30)
    near_20 = swap(found_20, "y", 2)
    own_0 = after(found_00 + after(near_10, found_11, found_31), gathered, near_30)
    rows_0 = exchange(own_0, "z")
    gathered = after(gathered, own_0)
    parts = [gathered] + [swap(gathered, "x", by) for by in range(1, X)]
    (found_21,) = find([(2, 1)], found_20)
    near_21 = swap(found_21, "y", 2)
    own_1 = found_01 + after(near_11, own_0)
    rows_1 = exchange(after(own_1, rows_0, near_31, found_21), "z")
    rows_2 = exchange(after(near_20 + near_30, rows_1, found_21), "z")
    other_1 = near_21 + near_31
    rows_3 = exchange(after(other_1, rows_2), "z")
    chunks = [rows_0, rows_1, rows_2, rows_3]
    parts = after(tuple(parts + [swap(part, "core", 1) for part in parts]), rows_1)
    halves = pl.pallas_call(
        arrange_kernel,
        out_shape=jax.ShapeDtypeStruct((X, CORE, SHARD, *piece.shape), piece.dtype),
        in_specs=[in_smem] + [in_vmem] * GRP,
        **limits,
    )(place, *parts)
    slot_query = slot_query.reshape(Z, 2, q_dev)
    slot_query = jnp.where(my_y // 2 == 0, slot_query, slot_query[:, ::-1])
    slot_query = jnp.concatenate(
        [slot_query[:, pair, cut].reshape(1, -1) for pair in range(2) for cut in cuts], axis=1
    )

    inner_full = [
        columns_to_rows(halves[g // CORE, g % CORE, :, :deep], wide).reshape(width, wide)
        for g in range(GRP)
    ]
    outer_full = halves[:, :, :, deep:].transpose(2, 0, 1, 3, 4).reshape(hid, width)

    pre_act = jnp.concatenate(
        [jnp.dot(queries, part, preferred_element_type=jnp.float32) for part in inner_full], axis=1
    )
    hidden = gelu_value(pre_act).astype(jnp.bfloat16)
    slope = gelu_slope(pre_act)
    projected = jnp.dot(hidden, outer_full, preferred_element_type=jnp.float32)
    embedded = (queries.astype(jnp.float32) + projected).astype(jnp.bfloat16)

    half = width // CORE
    outer_cut = jax.ShapeDtypeStruct((Y, X, hid // Y // X, half), jnp.bfloat16)
    stats, early_sum = pl.pallas_call(
        functools.partial(early_kernel, scale),
        out_shape=[
            jax.ShapeDtypeStruct((3, q_dev, 1), jnp.float32),
            jax.ShapeDtypeStruct((q_dev, width), jnp.float32),
        ],
        **limits,
    )(embedded, positives, slot_query, *chunks[:-1])
    losses, query_grad, outer, outer_sent = pl.pallas_call(
        functools.partial(score_kernel, scale),
        out_shape=[
            jax.ShapeDtypeStruct((q_dev, 1), jnp.float32),
            jax.ShapeDtypeStruct((q_dev, width), jnp.bfloat16),
            outer_cut,
            outer_cut,
        ],
        in_specs=[in_smem] + [in_vmem] * 7,
        **limits,
    )(place, embedded, positives, hidden, slot_query, stats, early_sum, chunks[-1])
    outer_sent = swap(outer_sent, "core", 1)
    inner, inner_sent = pl.pallas_call(
        inner_kernel,
        out_shape=[jax.ShapeDtypeStruct((X, width, wide), jnp.bfloat16)] * 2,
        in_specs=[in_smem] + [in_vmem] * 4,
        **limits,
    )(place, queries, query_grad, slope, outer_full)
    inner_sent = swap(inner_sent, "core", 1)

    narrow = lambda value: value.astype(jnp.bfloat16)
    outer = exchange(narrow(total_of([outer, outer_sent])), "y")
    inner = [narrow(total_of([inner[by], inner_sent[by]])) for by in range(X)]
    inner = inner[:1] + [swap(inner[by], "x", by) for by in range(1, X)]
    outer = narrow(total_of(list(outer)))
    inner = after(tuple(inner), outer)
    outer = exchange(outer, "x")
    inner = narrow(total_of(inner)).reshape(Z, Y, inner_rows, wide)
    inner = [lax.dynamic_index_in_dim(inner, my_y ^ by, 1, False) for by in range(Y)]
    inner = inner[:1] + [swap(inner[by], "y", by) for by in range(1, Y)]
    lanes = 128
    both = jnp.concatenate(
        [
            columns_to_rows(total_of(inner), lanes),
            columns_to_rows(total_of(list(outer)).reshape(Z, -1, half), lanes),
        ],
        axis=1,
    )
    both = total_of(list(exchange(narrow(both), "z")))
    both = spread(narrow(both), ("x", "core"), GRP).astype(jnp.float32)
    inner_deep = inner_rows * wide // lanes
    inner = rows_to_columns(both[:, :inner_deep], inner_rows)
    outer = rows_to_columns(both[:, inner_deep:], outer_rows // X)
    inner = jnp.concatenate(list(inner), axis=1)
    outer = jnp.concatenate(
        [jnp.concatenate([outer[x * CORE + c] for c in range(CORE)], axis=1) for x in range(X)],
        axis=0,
    )
    return (losses.reshape(-1), inner, outer)


def solution(mesh):
    fine = Mesh(mesh.devices.reshape(X, CORE, Z, Y), ("x", "core", "z", "y"))
    blocks, rows = ("x", "core", "z", "y"), ("z", "y")
    return jax.shard_map(
        shards,
        mesh=fine,
        in_specs=(
            P(blocks, None),
            P(blocks, None),
            P(blocks, None),
            P(rows, None),
            P(rows, None),
            P(rows, None),
        ),
        out_specs=(P(blocks), P(rows, None), P(rows, None)),
        check_vma=False,
    )
```

```python
import functools

import jax
import jax.numpy as jnp
from jax import lax
from jax.experimental import pallas as pl
from jax.experimental.pallas import tpu as pltpu
from jax.sharding import Mesh, PartitionSpec as P

X, CORE, Z, Y = 4, 2, 8, 4
GRP, SHARD = X * CORE, Z * Y
PAIRS = SHARD // 2
CHUNKS = 4
VMEM = 50 * 1024 * 1024


def gelu_value(pre_act):
    return pre_act * 0.5 * (1.0 + lax.erf(pre_act * 0.7071067811865476))


def gelu_slope(pre_act):
    return (
        0.5 * (1.0 + lax.erf(pre_act * 0.7071067811865476))
        + pre_act * jnp.exp(-0.5 * pre_act * pre_act) * 0.3989422804014327
    )


def contract_first(left, right):
    return lax.dot_general(
        left, right, (((0,), (0,)), ((), ())), preferred_element_type=jnp.float32
    )


def contract_last(left, right):
    return lax.dot_general(
        left, right, (((1,), (1,)), ((), ())), preferred_element_type=jnp.float32
    )


def exchange(value, axes):
    return lax.all_to_all(value, axes, split_axis=0, concat_axis=0, tiled=True)


def spread(value, axes, count):
    return exchange(jnp.broadcast_to(value[None], (count, *value.shape)), axes)


def swap(value, axis, by):
    return lax.ppermute(value, axis, [(i, i ^ by) for i in range(lax.axis_size(axis))])


def after(value, *done):
    return lax.optimization_barrier((value, *done))[0]


def request_kernel(shift, ids_ref, code_ref, query_ref):
    ids = ids_ref[...]
    q_dev, neg = ids.shape
    lane = lax.broadcasted_iota(jnp.int32, (q_dev, q_dev), 1)
    query = lax.broadcasted_iota(jnp.int32, (q_dev, q_dev), 0)
    before = (lane < query).astype(jnp.float32).astype(jnp.bfloat16)
    kind, pair_lane = lane // PAIRS, lane % PAIRS
    seen = jnp.zeros((1, q_dev), jnp.float32)
    placed = jnp.zeros((q_dev, q_dev), jnp.float32)
    for k in range(neg):
        id_k = ids[:, k : k + 1]
        owner = id_k >> shift
        odd = owner & 1
        member = owner == lane
        ones = member.astype(jnp.float32)
        counts = seen + jnp.dot(before, ones.astype(jnp.bfloat16), preferred_element_type=jnp.float32)
        rank = jnp.sum(jnp.where(member, counts, 0.0), axis=1, keepdims=True).astype(jnp.int32)
        seen = seen + jnp.sum(ones, axis=0, keepdims=True)
        slot = jnp.where(odd == 1, q_dev - 1 - rank, rank)
        at_slot = (slot == lane).astype(jnp.float32).astype(jnp.bfloat16)
        code = (odd << shift) + (id_k - (owner << shift))
        item = jnp.where(
            kind == 0, code >> 6, jnp.where(kind == 1, code & 63, jnp.where(kind == 2, query, 0))
        )
        item = jnp.where((owner >> 1) == pair_lane, item, 0)
        placed = placed + contract_first(item.astype(jnp.float32).astype(jnp.bfloat16), at_slot)
    code_ref[...] = (placed[:PAIRS] * 64.0 + placed[PAIRS : 2 * PAIRS]).astype(jnp.int32)
    query_ref[...] = placed[2 * PAIRS : 3 * PAIRS].astype(jnp.int32)


def arrange_kernel(place_ref, *refs):
    part_refs, out_ref = refs[:GRP], refs[GRP]
    for by_core in range(CORE):
        for by_x in range(X):
            at = place_ref[0] ^ by_x, place_ref[1] ^ by_core
            out_ref[at] = part_refs[by_core * X + by_x][...]


def weighted_rows(weight, rows):
    high = weight.astype(jnp.bfloat16)
    low = (weight - high.astype(jnp.float32)).astype(jnp.bfloat16)
    return jnp.dot(high, rows, preferred_element_type=jnp.float32) + jnp.dot(
        low, rows, preferred_element_type=jnp.float32
    )


def early_kernel(scale, embedded_ref, positives_ref, query_ref, *refs):
    row_refs, (stats_ref, sum_ref) = refs[: CHUNKS - 1], refs[CHUNKS - 1 :]
    embedded = embedded_ref[...]
    positives = positives_ref[...].astype(jnp.float32)
    q_dev = embedded.shape[0]
    pos_scores = (
        jnp.sum(embedded.astype(jnp.float32) * positives, axis=1, keepdims=True) * scale
    )
    per = row_refs[0].shape[0]
    query = lax.broadcasted_iota(jnp.int32, (q_dev, per), 0)
    scores, members, largest = [], [], pos_scores
    for c in range(CHUNKS - 1):
        score = contract_last(embedded, row_refs[c][...]) * scale
        member = query_ref[:, c * per : (c + 1) * per] == query
        seen = jnp.where(member, score, pos_scores)
        largest = jnp.maximum(largest, jnp.max(seen, axis=1, keepdims=True))
        scores.append(score)
        members.append(member)
    total = jnp.exp(pos_scores - largest)
    grad = jnp.zeros(sum_ref.shape, jnp.float32)
    for c in range(CHUNKS - 1):
        weight = jnp.where(members[c], jnp.exp(scores[c] - largest), 0.0)
        total = total + jnp.sum(weight, axis=1, keepdims=True)
        grad = grad + weighted_rows(weight, row_refs[c][...])
    stats_ref[0] = pos_scores
    stats_ref[1] = largest
    stats_ref[2] = total
    sum_ref[...] = grad


def score_kernel(
    scale, place_ref, embedded_ref, positives_ref, hidden_ref, query_ref, stats_ref, sum_ref,
    rows_ref, loss_ref, grad_ref, keep_ref, send_ref,
):
    embedded = embedded_ref[...]
    positives = positives_ref[...].astype(jnp.float32)
    q_dev, width = embedded.shape
    pos_scores, early, total = stats_ref[0], stats_ref[1], stats_ref[2]
    rows = rows_ref[...]
    per = rows.shape[0]
    score = contract_last(embedded, rows) * scale
    member = query_ref[:, (CHUNKS - 1) * per :] == lax.broadcasted_iota(
        jnp.int32, (q_dev, per), 0
    )
    largest = jnp.maximum(
        early, jnp.max(jnp.where(member, score, early), axis=1, keepdims=True)
    )
    late = jnp.where(member, jnp.exp(score - largest), 0.0)
    total = total * jnp.exp(early - largest) + jnp.sum(late, axis=1, keepdims=True)
    log_total = largest + jnp.log(total)
    loss_ref[...] = log_total - pos_scores
    grad = (jnp.exp(pos_scores - log_total) - 1.0) * positives
    grad = grad + jnp.exp(early - log_total) * sum_ref[...]
    grad = grad + weighted_rows(late * (1.0 / total), rows)
    query_grad = (grad * scale).astype(jnp.bfloat16)
    grad_ref[...] = query_grad
    my_core = place_ref[1]
    hid = hidden_ref.shape[1]
    deep, part, half = hid // SHARD // X, hid // Z, width // CORE
    for z in range(Z):
        outer = contract_first(hidden_ref[:, z * part : (z + 1) * part], query_grad)
        left, right = outer[:, :half], outer[:, half:]
        keep = jnp.where(my_core == 0, left, right).astype(jnp.bfloat16)
        send = jnp.where(my_core == 0, right, left).astype(jnp.bfloat16)
        for y in range(Y):
            for x in range(X):
                rows = slice((y * X + x) * deep, (y * X + x + 1) * deep)
                keep_ref[y, x, z * deep : (z + 1) * deep, :] = keep[rows]
                send_ref[y, x, z * deep : (z + 1) * deep, :] = send[rows]


def inner_kernel(place_ref, queries_ref, grad_ref, slope_ref, weight_ref, keep_ref, send_ref):
    queries, query_grad = queries_ref[...], grad_ref[...]
    part = weight_ref.shape[0] // GRP
    for by_core, out_ref in ((1, send_ref), (0, keep_ref)):
        for by_x in range(X):
            group = (place_ref[0] ^ by_x) * CORE + (place_ref[1] ^ by_core)
            at = pl.ds(pl.multiple_of(group * part, part), part)
            hidden_grad = contract_last(query_grad, weight_ref[at, :])
            pre_grad = (hidden_grad * slope_ref[:, at]).astype(jnp.bfloat16)
            out_ref[by_x] = contract_first(queries, pre_grad).astype(jnp.bfloat16)


def total_of(parts):
    return sum(part.astype(jnp.float32) for part in parts)


def columns_to_rows(value, wide):
    return jnp.concatenate(
        [value[..., i : i + wide] for i in range(0, value.shape[-1], wide)], axis=-2
    )


def rows_to_columns(value, deep):
    return jnp.concatenate(
        [value[..., i : i + deep, :] for i in range(0, value.shape[-2], deep)], axis=-1
    )


def shards(queries, positives, negative_ids, passage_table, inner_weight, outer_weight):
    q_dev, width = queries.shape
    rows_dev = passage_table.shape[0]
    shift = rows_dev.bit_length() - 1
    hid = inner_weight.shape[1]
    inner_rows, outer_rows = inner_weight.shape[0], outer_weight.shape[0]
    scale = float(width) ** (-0.5)
    limits = {"compiler_params": pltpu.CompilerParams(vmem_limit_bytes=VMEM)}
    my_x, my_core, my_y = (lax.axis_index(axis) for axis in ("x", "core", "y"))
    group = my_x * CORE + my_core
    place = jnp.stack([my_x, my_core]).astype(jnp.int32)
    in_smem = pl.BlockSpec(memory_space=pltpu.SMEM)
    in_vmem = pl.BlockSpec(memory_space=pltpu.VMEM)

    slots = jax.ShapeDtypeStruct((PAIRS, q_dev), jnp.int32)
    code, slot_query = pl.pallas_call(
        functools.partial(request_kernel, shift), out_shape=[slots] * 2, **limits
    )(negative_ids)
    code = exchange(
        jnp.broadcast_to(code[:, None], (PAIRS, 2, q_dev)).reshape(SHARD, q_dev), ("z", "y")
    ).reshape(Z, Y, q_dev)
    code = jnp.stack([lax.dynamic_index_in_dim(code, my_y ^ by, 1, False) for by in range(Y)])
    own = (code >> shift) == my_y % 2
    wanted = code & (rows_dev - 1)
    wanted = lax.optimization_barrier((wanted[:, :, : q_dev // 2], wanted[:, :, q_dev // 2 :]))
    per = q_dev // 2
    cuts = slice(0, per), slice(per, q_dev)

    def find(picks, *done):
        ids = jnp.stack([wanted[part][by] for by, part in picks])
        ids = after(ids.reshape(-1), *done)
        found = passage_table.at[ids].get(mode="promise_in_bounds").reshape(-1, Z * per, width)
        return [
            jnp.where(own[by, :, cuts[part]].reshape(-1, 1), found[i], jnp.zeros((), found.dtype))
            for i, (by, part) in enumerate(picks)
        ]

    wide, deep = hid // GRP, outer_rows // GRP
    inner_piece = lax.dynamic_slice(inner_weight, (0, group * wide), (inner_rows, wide))
    outer_piece = lax.dynamic_slice(outer_weight, (group * deep, 0), (deep, width))
    piece = jnp.concatenate([rows_to_columns(inner_piece, deep), outer_piece], axis=0)

    found_10, found_30 = find([(1, 0), (3, 0)])
    near_10, near_30 = swap(found_10, "y", 1), swap(found_30, "y", 3)
    gathered = spread(after(piece, found_10), ("z", "y"), SHARD)
    found_11, found_31, found_00 = find([(1, 1), (3, 1), (0, 0)], found_10)
    near_11, near_31 = swap(found_11, "y", 1), swap(found_31, "y", 3)
    found_20, found_01 = find([(2, 0), (0, 1)], found_11, near_10, near_30)
    near_20 = swap(found_20, "y", 2)
    own_0 = after(found_00 + after(near_10, found_11, found_31), gathered, near_30)
    rows_0 = exchange(own_0, "z")
    gathered = after(gathered, own_0)
    parts = [gathered] + [swap(gathered, "x", by) for by in range(1, X)]
    (found_21,) = find([(2, 1)], found_20, near_31)
    near_21 = swap(found_21, "y", 2)
    own_1 = found_01 + after(near_11, own_0)
    rows_1 = exchange(after(own_1, rows_0, near_31, found_21), "z")
    rows_2 = exchange(after(near_20 + near_30, rows_1, found_21), "z")
    other_1 = near_21 + near_31
    rows_3 = exchange(after(other_1, rows_2), "z")
    chunks = [rows_0, rows_1, rows_2, rows_3]
    parts = after(tuple(parts + [swap(part, "core", 1) for part in parts]), rows_1)
    halves = pl.pallas_call(
        arrange_kernel,
        out_shape=jax.ShapeDtypeStruct((X, CORE, SHARD, *piece.shape), piece.dtype),
        in_specs=[in_smem] + [in_vmem] * GRP,
        **limits,
    )(place, *parts)
    slot_query = slot_query.reshape(Z, 2, q_dev)
    slot_query = jnp.where(my_y // 2 == 0, slot_query, slot_query[:, ::-1])
    slot_query = jnp.concatenate(
        [slot_query[:, pair, cut].reshape(1, -1) for pair in range(2) for cut in cuts], axis=1
    )

    inner_full = [
        columns_to_rows(halves[g // CORE, g % CORE, :, :deep], wide).reshape(width, wide)
        for g in range(GRP)
    ]
    outer_full = halves[:, :, :, deep:].transpose(2, 0, 1, 3, 4).reshape(hid, width)

    pre_act = jnp.concatenate(
        [jnp.dot(queries, part, preferred_element_type=jnp.float32) for part in inner_full], axis=1
    )
    hidden = gelu_value(pre_act).astype(jnp.bfloat16)
    slope = gelu_slope(pre_act)
    projected = jnp.dot(hidden, outer_full, preferred_element_type=jnp.float32)
    embedded = (queries.astype(jnp.float32) + projected).astype(jnp.bfloat16)

    half = width // CORE
    outer_cut = jax.ShapeDtypeStruct((Y, X, hid // Y // X, half), jnp.bfloat16)
    stats, early_sum = pl.pallas_call(
        functools.partial(early_kernel, scale),
        out_shape=[
            jax.ShapeDtypeStruct((3, q_dev, 1), jnp.float32),
            jax.ShapeDtypeStruct((q_dev, width), jnp.float32),
        ],
        **limits,
    )(embedded, positives, slot_query, *chunks[:-1])
    losses, query_grad, outer, outer_sent = pl.pallas_call(
        functools.partial(score_kernel, scale),
        out_shape=[
            jax.ShapeDtypeStruct((q_dev, 1), jnp.float32),
            jax.ShapeDtypeStruct((q_dev, width), jnp.bfloat16),
            outer_cut,
            outer_cut,
        ],
        in_specs=[in_smem] + [in_vmem] * 7,
        **limits,
    )(place, embedded, positives, hidden, slot_query, stats, early_sum, chunks[-1])
    outer_sent = swap(outer_sent, "core", 1)
    inner, inner_sent = pl.pallas_call(
        inner_kernel,
        out_shape=[jax.ShapeDtypeStruct((X, width, wide), jnp.bfloat16)] * 2,
        in_specs=[in_smem] + [in_vmem] * 4,
        **limits,
    )(place, queries, query_grad, slope, outer_full)
    inner_sent = swap(inner_sent, "core", 1)

    narrow = lambda value: value.astype(jnp.bfloat16)
    outer = exchange(narrow(total_of([outer, outer_sent])), "y")
    inner = [narrow(total_of([inner[by], inner_sent[by]])) for by in range(X)]
    inner = inner[:1] + [swap(inner[by], "x", by) for by in range(1, X)]
    outer = narrow(total_of(list(outer)))
    inner = after(tuple(inner), outer)
    outer = exchange(outer, "x")
    inner = narrow(total_of(inner)).reshape(Z, Y, inner_rows, wide)
    inner = [lax.dynamic_index_in_dim(inner, my_y ^ by, 1, False) for by in range(Y)]
    inner = inner[:1] + [swap(inner[by], "y", by) for by in range(1, Y)]
    lanes = 128
    both = jnp.concatenate(
        [
            columns_to_rows(total_of(inner), lanes),
            columns_to_rows(total_of(list(outer)).reshape(Z, -1, half), lanes),
        ],
        axis=1,
    )
    both = total_of(list(exchange(narrow(both), "z")))
    both = spread(narrow(both), ("x", "core"), GRP).astype(jnp.float32)
    inner_deep = inner_rows * wide // lanes
    inner = rows_to_columns(both[:, :inner_deep], inner_rows)
    outer = rows_to_columns(both[:, inner_deep:], outer_rows // X)
    inner = jnp.concatenate(list(inner), axis=1)
    outer = jnp.concatenate(
        [jnp.concatenate([outer[x * CORE + c] for c in range(CORE)], axis=1) for x in range(X)],
        axis=0,
    )
    return (losses.reshape(-1), inner, outer)


def solution(mesh):
    fine = Mesh(mesh.devices.reshape(X, CORE, Z, Y), ("x", "core", "z", "y"))
    blocks, rows = ("x", "core", "z", "y"), ("z", "y")
    return jax.shard_map(
        shards,
        mesh=fine,
        in_specs=(
            P(blocks, None),
            P(blocks, None),
            P(blocks, None),
            P(rows, None),
            P(rows, None),
            P(rows, None),
        ),
        out_specs=(P(blocks), P(rows, None), P(rows, None)),
        check_vma=False,
    )
```

```python
import functools

import jax
import jax.numpy as jnp
from jax import lax
from jax.experimental import pallas as pl
from jax.experimental.pallas import tpu as pltpu
from jax.sharding import Mesh, PartitionSpec as P

X, CORE, Z, Y = 4, 2, 8, 4
GRP, SHARD = X * CORE, Z * Y
PAIRS = SHARD // 2
CHUNKS = 4
VMEM = 50 * 1024 * 1024


def gelu_value(pre_act):
    return pre_act * 0.5 * (1.0 + lax.erf(pre_act * 0.7071067811865476))


def gelu_slope(pre_act):
    return (
        0.5 * (1.0 + lax.erf(pre_act * 0.7071067811865476))
        + pre_act * jnp.exp(-0.5 * pre_act * pre_act) * 0.3989422804014327
    )


def contract_first(left, right):
    return lax.dot_general(
        left, right, (((0,), (0,)), ((), ())), preferred_element_type=jnp.float32
    )


def contract_last(left, right):
    return lax.dot_general(
        left, right, (((1,), (1,)), ((), ())), preferred_element_type=jnp.float32
    )


def exchange(value, axes):
    return lax.all_to_all(value, axes, split_axis=0, concat_axis=0, tiled=True)


def spread(value, axes, count):
    return exchange(jnp.broadcast_to(value[None], (count, *value.shape)), axes)


def swap(value, axis, by):
    return lax.ppermute(value, axis, [(i, i ^ by) for i in range(lax.axis_size(axis))])


def after(value, *done):
    return lax.optimization_barrier((value, *done))[0]


def request_kernel(shift, ids_ref, code_ref, query_ref):
    neg, q_dev = ids_ref.shape
    owner_row = lax.broadcasted_iota(jnp.int32, (SHARD, q_dev), 0)
    first = lax.broadcasted_iota(jnp.int32, (q_dev, q_dev), 0)
    before = (first < lax.broadcasted_iota(jnp.int32, (q_dev, q_dev), 1)).astype(jnp.float32)
    before = before.astype(jnp.bfloat16)
    rows = 2 * SHARD + PAIRS
    row = lax.broadcasted_iota(jnp.int32, (rows, q_dev), 0)
    query = lax.broadcasted_iota(jnp.int32, (1, q_dev), 1)
    pair_row = jnp.where(row < 2 * SHARD, (row & (SHARD - 1)) >> 1, row - 2 * SHARD)
    seen = jnp.zeros((SHARD, 1), jnp.float32)
    placed = jnp.zeros((rows, q_dev), jnp.float32)
    for k in range(neg):
        ids = ids_ref[k : k + 1, :]
        owner = ids >> shift
        odd = owner & 1
        member = owner == owner_row
        ones = member.astype(jnp.float32)
        counts = seen + jnp.dot(ones.astype(jnp.bfloat16), before, preferred_element_type=jnp.float32)
        rank = jnp.sum(jnp.where(member, counts, 0.0), axis=0, keepdims=True).astype(jnp.int32)
        seen = seen + jnp.sum(ones, axis=1, keepdims=True)
        slot = jnp.where(odd == 1, q_dev - 1 - rank, rank)
        at_slot = (slot == first).astype(jnp.float32).astype(jnp.bfloat16)
        code = (odd << shift) + (ids - (owner << shift))
        item = jnp.where(
            row < SHARD, code >> 6, jnp.where(row < 2 * SHARD, code & 63, query)
        )
        item = jnp.where((owner >> 1) == pair_row, item, 0)
        placed = placed + contract_last(item.astype(jnp.float32).astype(jnp.bfloat16), at_slot)
    code_ref[...] = (placed[:SHARD] * 64.0 + placed[SHARD : 2 * SHARD]).astype(jnp.int32)
    query_ref[...] = placed[2 * SHARD :].astype(jnp.int32)


def arrange_kernel(place_ref, *refs):
    part_refs, out_ref = refs[:GRP], refs[GRP]
    for by_core in range(CORE):
        for by_x in range(X):
            at = place_ref[0] ^ by_x, place_ref[1] ^ by_core
            out_ref[at] = part_refs[by_core * X + by_x][...]


def weighted_rows(weight, rows):
    high = weight.astype(jnp.bfloat16)
    low = (weight - high.astype(jnp.float32)).astype(jnp.bfloat16)
    return jnp.dot(high, rows, preferred_element_type=jnp.float32) + jnp.dot(
        low, rows, preferred_element_type=jnp.float32
    )


def early_kernel(scale, embedded_ref, positives_ref, query_ref, *refs):
    row_refs, (stats_ref, sum_ref) = refs[: CHUNKS - 1], refs[CHUNKS - 1 :]
    embedded = embedded_ref[...]
    positives = positives_ref[...].astype(jnp.float32)
    q_dev = embedded.shape[0]
    pos_scores = (
        jnp.sum(embedded.astype(jnp.float32) * positives, axis=1, keepdims=True) * scale
    )
    per = row_refs[0].shape[0]
    query = lax.broadcasted_iota(jnp.int32, (q_dev, per), 0)
    scores, members, largest = [], [], pos_scores
    for c in range(CHUNKS - 1):
        score = contract_last(embedded, row_refs[c][...]) * scale
        member = query_ref[:, c * per : (c + 1) * per] == query
        seen = jnp.where(member, score, pos_scores)
        largest = jnp.maximum(largest, jnp.max(seen, axis=1, keepdims=True))
        scores.append(score)
        members.append(member)
    total = jnp.exp(pos_scores - largest)
    grad = jnp.zeros(sum_ref.shape, jnp.float32)
    for c in range(CHUNKS - 1):
        weight = jnp.where(members[c], jnp.exp(scores[c] - largest), 0.0)
        total = total + jnp.sum(weight, axis=1, keepdims=True)
        grad = grad + weighted_rows(weight, row_refs[c][...])
    stats_ref[0] = pos_scores
    stats_ref[1] = largest
    stats_ref[2] = total
    sum_ref[...] = grad


def score_kernel(
    scale, place_ref, embedded_ref, positives_ref, hidden_ref, query_ref, stats_ref, sum_ref,
    rows_ref, loss_ref, grad_ref, keep_ref, send_ref,
):
    embedded = embedded_ref[...]
    positives = positives_ref[...].astype(jnp.float32)
    q_dev, width = embedded.shape
    pos_scores, early, total = stats_ref[0], stats_ref[1], stats_ref[2]
    rows = rows_ref[...]
    per = rows.shape[0]
    score = contract_last(embedded, rows) * scale
    member = query_ref[:, (CHUNKS - 1) * per :] == lax.broadcasted_iota(
        jnp.int32, (q_dev, per), 0
    )
    largest = jnp.maximum(
        early, jnp.max(jnp.where(member, score, early), axis=1, keepdims=True)
    )
    late = jnp.where(member, jnp.exp(score - largest), 0.0)
    total = total * jnp.exp(early - largest) + jnp.sum(late, axis=1, keepdims=True)
    log_total = largest + jnp.log(total)
    loss_ref[...] = log_total - pos_scores
    grad = (jnp.exp(pos_scores - log_total) - 1.0) * positives
    grad = grad + jnp.exp(early - log_total) * sum_ref[...]
    grad = grad + weighted_rows(late * (1.0 / total), rows)
    query_grad = (grad * scale).astype(jnp.bfloat16)
    grad_ref[...] = query_grad
    my_core = place_ref[1]
    hid = hidden_ref.shape[1]
    deep, part, half = hid // SHARD // X, hid // Z, width // CORE
    for z in range(Z):
        outer = contract_first(hidden_ref[:, z * part : (z + 1) * part], query_grad)
        left, right = outer[:, :half], outer[:, half:]
        keep = jnp.where(my_core == 0, left, right).astype(jnp.bfloat16)
        send = jnp.where(my_core == 0, right, left).astype(jnp.bfloat16)
        for y in range(Y):
            for x in range(X):
                rows = slice((y * X + x) * deep, (y * X + x + 1) * deep)
                keep_ref[y, x, z * deep : (z + 1) * deep, :] = keep[rows]
                send_ref[y, x, z * deep : (z + 1) * deep, :] = send[rows]


def inner_kernel(place_ref, queries_ref, grad_ref, slope_ref, weight_ref, keep_ref, send_ref):
    queries, query_grad = queries_ref[...], grad_ref[...]
    part = weight_ref.shape[0] // GRP
    for by_core, out_ref in ((1, send_ref), (0, keep_ref)):
        for by_x in range(X):
            group = (place_ref[0] ^ by_x) * CORE + (place_ref[1] ^ by_core)
            at = pl.ds(pl.multiple_of(group * part, part), part)
            hidden_grad = contract_last(query_grad, weight_ref[at, :])
            pre_grad = (hidden_grad * slope_ref[:, at]).astype(jnp.bfloat16)
            out_ref[by_x] = contract_first(queries, pre_grad).astype(jnp.bfloat16)


def total_of(parts):
    return sum(part.astype(jnp.float32) for part in parts)


def columns_to_rows(value, wide):
    return jnp.concatenate(
        [value[..., i : i + wide] for i in range(0, value.shape[-1], wide)], axis=-2
    )


def rows_to_columns(value, deep):
    return jnp.concatenate(
        [value[..., i : i + deep, :] for i in range(0, value.shape[-2], deep)], axis=-1
    )


def shards(queries, positives, negative_ids, passage_table, inner_weight, outer_weight):
    q_dev, width = queries.shape
    rows_dev = passage_table.shape[0]
    shift = rows_dev.bit_length() - 1
    hid = inner_weight.shape[1]
    inner_rows, outer_rows = inner_weight.shape[0], outer_weight.shape[0]
    scale = float(width) ** (-0.5)
    limits = {"compiler_params": pltpu.CompilerParams(vmem_limit_bytes=VMEM)}
    my_x, my_core, my_y = (lax.axis_index(axis) for axis in ("x", "core", "y"))
    group = my_x * CORE + my_core
    place = jnp.stack([my_x, my_core]).astype(jnp.int32)
    in_smem = pl.BlockSpec(memory_space=pltpu.SMEM)
    in_vmem = pl.BlockSpec(memory_space=pltpu.VMEM)

    code, slot_query = pl.pallas_call(
        functools.partial(request_kernel, shift),
        out_shape=[
            jax.ShapeDtypeStruct((SHARD, q_dev), jnp.int32),
            jax.ShapeDtypeStruct((PAIRS, q_dev), jnp.int32),
        ],
        **limits,
    )(negative_ids.T)
    code = exchange(code, ("z", "y")).reshape(Z, Y, q_dev)
    code = jnp.stack([lax.dynamic_index_in_dim(code, my_y ^ by, 1, False) for by in range(Y)])
    own = (code >> shift) == my_y % 2
    wanted = code & (rows_dev - 1)
    wanted = lax.optimization_barrier((wanted[:, :, : q_dev // 2], wanted[:, :, q_dev // 2 :]))
    per = q_dev // 2
    cuts = slice(0, per), slice(per, q_dev)

    def find(picks, *done):
        ids = jnp.stack([wanted[part][by] for by, part in picks])
        ids = after(ids.reshape(-1), *done)
        found = passage_table.at[ids].get(mode="promise_in_bounds").reshape(-1, Z * per, width)
        return [
            jnp.where(own[by, :, cuts[part]].reshape(-1, 1), found[i], jnp.zeros((), found.dtype))
            for i, (by, part) in enumerate(picks)
        ]

    wide, deep = hid // GRP, outer_rows // GRP
    inner_piece = lax.dynamic_slice(inner_weight, (0, group * wide), (inner_rows, wide))
    outer_piece = lax.dynamic_slice(outer_weight, (group * deep, 0), (deep, width))
    piece = jnp.concatenate([rows_to_columns(inner_piece, deep), outer_piece], axis=0)

    found_10, found_30 = find([(1, 0), (3, 0)])
    near_10, near_30 = swap(found_10, "y", 1), swap(found_30, "y", 3)
    gathered = spread(after(piece, found_10), ("z", "y"), SHARD)
    found_11, found_31, found_00 = find([(1, 1), (3, 1), (0, 0)], found_10)
    near_11, near_31 = swap(found_11, "y", 1), swap(found_31, "y", 3)
    found_20, found_01 = find([(2, 0), (0, 1)], found_11, near_10, near_30)
    near_20 = swap(found_20, "y", 2)
    own_0 = after(found_00 + after(near_10, found_11, found_31), gathered, near_30)
    rows_0 = exchange(own_0, "z")
    gathered = after(gathered, own_0)
    parts = [gathered] + [swap(gathered, "x", by) for by in range(1, X)]
    (found_21,) = find([(2, 1)], found_20, near_31)
    near_21 = swap(found_21, "y", 2)
    own_1 = found_01 + after(near_11, own_0)
    rows_1 = exchange(after(own_1, rows_0, near_31, found_21), "z")
    rows_2 = exchange(after(near_20 + near_30, rows_1, found_21), "z")
    other_1 = near_21 + near_31
    rows_3 = exchange(after(other_1, rows_2), "z")
    chunks = [rows_0, rows_1, rows_2, rows_3]
    parts = after(tuple(parts + [swap(part, "core", 1) for part in parts]), rows_1)
    halves = pl.pallas_call(
        arrange_kernel,
        out_shape=jax.ShapeDtypeStruct((X, CORE, SHARD, *piece.shape), piece.dtype),
        in_specs=[in_smem] + [in_vmem] * GRP,
        **limits,
    )(place, *parts)
    slot_query = slot_query.reshape(Z, 2, q_dev)
    slot_query = jnp.where(my_y // 2 == 0, slot_query, slot_query[:, ::-1])
    slot_query = jnp.concatenate(
        [slot_query[:, pair, cut].reshape(1, -1) for pair in range(2) for cut in cuts], axis=1
    )

    inner_full = [
        columns_to_rows(halves[g // CORE, g % CORE, :, :deep], wide).reshape(width, wide)
        for g in range(GRP)
    ]
    outer_full = halves[:, :, :, deep:].transpose(2, 0, 1, 3, 4).reshape(hid, width)

    pre_act = jnp.concatenate(
        [jnp.dot(queries, part, preferred_element_type=jnp.float32) for part in inner_full], axis=1
    )
    hidden = gelu_value(pre_act).astype(jnp.bfloat16)
    slope = gelu_slope(pre_act)
    projected = jnp.dot(hidden, outer_full, preferred_element_type=jnp.float32)
    embedded = (queries.astype(jnp.float32) + projected).astype(jnp.bfloat16)

    half = width // CORE
    outer_cut = jax.ShapeDtypeStruct((Y, X, hid // Y // X, half), jnp.bfloat16)
    stats, early_sum = pl.pallas_call(
        functools.partial(early_kernel, scale),
        out_shape=[
            jax.ShapeDtypeStruct((3, q_dev, 1), jnp.float32),
            jax.ShapeDtypeStruct((q_dev, width), jnp.float32),
        ],
        **limits,
    )(embedded, positives, slot_query, *chunks[:-1])
    losses, query_grad, outer, outer_sent = pl.pallas_call(
        functools.partial(score_kernel, scale),
        out_shape=[
            jax.ShapeDtypeStruct((q_dev, 1), jnp.float32),
            jax.ShapeDtypeStruct((q_dev, width), jnp.bfloat16),
            outer_cut,
            outer_cut,
        ],
        in_specs=[in_smem] + [in_vmem] * 7,
        **limits,
    )(place, embedded, positives, hidden, slot_query, stats, early_sum, chunks[-1])
    outer_sent = swap(outer_sent, "core", 1)
    inner, inner_sent = pl.pallas_call(
        inner_kernel,
        out_shape=[jax.ShapeDtypeStruct((X, width, wide), jnp.bfloat16)] * 2,
        in_specs=[in_smem] + [in_vmem] * 4,
        **limits,
    )(place, queries, query_grad, slope, outer_full)
    inner_sent = swap(inner_sent, "core", 1)

    narrow = lambda value: value.astype(jnp.bfloat16)
    outer = exchange(narrow(total_of([outer, outer_sent])), "y")
    inner = [narrow(total_of([inner[by], inner_sent[by]])) for by in range(X)]
    inner = inner[:1] + [swap(inner[by], "x", by) for by in range(1, X)]
    outer = narrow(total_of(list(outer)))
    inner = after(tuple(inner), outer)
    outer = exchange(outer, "x")
    inner = narrow(total_of(inner)).reshape(Z, Y, inner_rows, wide)
    inner = [lax.dynamic_index_in_dim(inner, my_y ^ by, 1, False) for by in range(Y)]
    inner = inner[:1] + [swap(inner[by], "y", by) for by in range(1, Y)]
    lanes = 128
    both = jnp.concatenate(
        [
            columns_to_rows(total_of(inner), lanes),
            columns_to_rows(total_of(list(outer)).reshape(Z, -1, half), lanes),
        ],
        axis=1,
    )
    both = total_of(list(exchange(narrow(both), "z")))
    both = spread(narrow(both), ("x", "core"), GRP).astype(jnp.float32)
    inner_deep = inner_rows * wide // lanes
    inner = rows_to_columns(both[:, :inner_deep], inner_rows)
    outer = rows_to_columns(both[:, inner_deep:], outer_rows // X)
    inner = jnp.concatenate(list(inner), axis=1)
    outer = jnp.concatenate(
        [jnp.concatenate([outer[x * CORE + c] for c in range(CORE)], axis=1) for x in range(X)],
        axis=0,
    )
    return (losses.reshape(-1), inner, outer)


def solution(mesh):
    fine = Mesh(mesh.devices.reshape(X, CORE, Z, Y), ("x", "core", "z", "y"))
    blocks, rows = ("x", "core", "z", "y"), ("z", "y")
    return jax.shard_map(
        shards,
        mesh=fine,
        in_specs=(
            P(blocks, None),
            P(blocks, None),
            P(blocks, None),
            P(rows, None),
            P(rows, None),
            P(rows, None),
        ),
        out_specs=(P(blocks), P(rows, None), P(rows, None)),
        check_vma=False,
    )
```

```python
import functools

import jax
import jax.numpy as jnp
from jax import lax
from jax.experimental import pallas as pl
from jax.experimental.pallas import tpu as pltpu
from jax.sharding import Mesh, PartitionSpec as P

X, CORE, Z, Y = 4, 2, 8, 4
GRP, SHARD = X * CORE, Z * Y
PAIRS = SHARD // 2
CHUNKS = 4
LANES = 128
VMEM = 50 * 1024 * 1024


def gelu_value(pre_act):
    return pre_act * 0.5 * (1.0 + lax.erf(pre_act * 0.7071067811865476))


def gelu_slope(pre_act):
    return (
        0.5 * (1.0 + lax.erf(pre_act * 0.7071067811865476))
        + pre_act * jnp.exp(-0.5 * pre_act * pre_act) * 0.3989422804014327
    )


def contract_first(left, right):
    return lax.dot_general(
        left, right, (((0,), (0,)), ((), ())), preferred_element_type=jnp.float32
    )


def contract_last(left, right):
    return lax.dot_general(
        left, right, (((1,), (1,)), ((), ())), preferred_element_type=jnp.float32
    )


def exchange(value, axes):
    return lax.all_to_all(value, axes, split_axis=0, concat_axis=0, tiled=True)


def spread(value, axes, count):
    return exchange(jnp.broadcast_to(value[None], (count, *value.shape)), axes)


def swap(value, axis, by):
    return lax.ppermute(value, axis, [(i, i ^ by) for i in range(lax.axis_size(axis))])


def after(value, *done):
    return lax.optimization_barrier((value, *done))[0]


def request_kernel(shift, ids_ref, code_ref, query_ref):
    neg, q_dev = ids_ref.shape
    owner_row = lax.broadcasted_iota(jnp.int32, (SHARD, q_dev), 0)
    first = lax.broadcasted_iota(jnp.int32, (q_dev, q_dev), 0)
    before = (first < lax.broadcasted_iota(jnp.int32, (q_dev, q_dev), 1)).astype(jnp.float32)
    before = before.astype(jnp.bfloat16)
    rows = 2 * SHARD + PAIRS
    row = lax.broadcasted_iota(jnp.int32, (rows, q_dev), 0)
    query = lax.broadcasted_iota(jnp.int32, (1, q_dev), 1)
    pair_row = jnp.where(row < 2 * SHARD, (row & (SHARD - 1)) >> 1, row - 2 * SHARD)
    seen = jnp.zeros((SHARD, 1), jnp.float32)
    placed = jnp.zeros((rows, q_dev), jnp.float32)
    for k in range(neg):
        ids = ids_ref[k : k + 1, :]
        owner = ids >> shift
        odd = owner & 1
        member = owner == owner_row
        ones = member.astype(jnp.float32)
        counts = seen + jnp.dot(ones.astype(jnp.bfloat16), before, preferred_element_type=jnp.float32)
        rank = jnp.sum(jnp.where(member, counts, 0.0), axis=0, keepdims=True).astype(jnp.int32)
        seen = seen + jnp.sum(ones, axis=1, keepdims=True)
        slot = jnp.where(odd == 1, q_dev - 1 - rank, rank)
        at_slot = (slot == first).astype(jnp.float32).astype(jnp.bfloat16)
        code = (odd << shift) + (ids - (owner << shift))
        item = jnp.where(
            row < SHARD, code >> 6, jnp.where(row < 2 * SHARD, code & 63, query)
        )
        item = jnp.where((owner >> 1) == pair_row, item, 0)
        placed = placed + contract_last(item.astype(jnp.float32).astype(jnp.bfloat16), at_slot)
    code_ref[...] = (placed[:SHARD] * 64.0 + placed[SHARD : 2 * SHARD]).astype(jnp.int32)
    query_ref[...] = placed[2 * SHARD :].astype(jnp.int32)


def arrange_kernel(place_ref, *refs):
    part_refs, out_ref = refs[:GRP], refs[GRP]
    for by_core in range(CORE):
        for by_x in range(X):
            at = place_ref[0] ^ by_x, place_ref[1] ^ by_core
            out_ref[at] = part_refs[by_core * X + by_x][...]


def weighted_rows(weight, rows):
    high = weight.astype(jnp.bfloat16)
    low = (weight - high.astype(jnp.float32)).astype(jnp.bfloat16)
    return jnp.dot(high, rows, preferred_element_type=jnp.float32) + jnp.dot(
        low, rows, preferred_element_type=jnp.float32
    )


def early_kernel(scale, embedded_ref, positives_ref, query_ref, *refs):
    row_refs, out_ref = refs[: CHUNKS - 1], refs[CHUNKS - 1]
    embedded = embedded_ref[...]
    positives = positives_ref[...].astype(jnp.float32)
    q_dev, width = embedded.shape
    pos_scores = (
        jnp.sum(embedded.astype(jnp.float32) * positives, axis=1, keepdims=True) * scale
    )
    per = row_refs[0].shape[0]
    query = lax.broadcasted_iota(jnp.int32, (q_dev, per), 0)
    scores, members, largest = [], [], pos_scores
    for c in range(CHUNKS - 1):
        score = contract_last(embedded, row_refs[c][...]) * scale
        member = query_ref[:, c * per : (c + 1) * per] == query
        seen = jnp.where(member, score, pos_scores)
        largest = jnp.maximum(largest, jnp.max(seen, axis=1, keepdims=True))
        scores.append(score)
        members.append(member)
    total = jnp.exp(pos_scores - largest)
    grad = jnp.zeros((q_dev, width), jnp.float32)
    for c in range(CHUNKS - 1):
        weight = jnp.where(members[c], jnp.exp(scores[c] - largest), 0.0)
        total = total + jnp.sum(weight, axis=1, keepdims=True)
        grad = grad + weighted_rows(weight, row_refs[c][...])
    lane = lax.broadcasted_iota(jnp.int32, (q_dev, LANES), 1)
    out_ref[:, :width] = grad
    out_ref[:, width:] = jnp.where(lane == 0, pos_scores, jnp.where(lane == 1, largest, total))


def score_kernel(
    scale, place_ref, embedded_ref, positives_ref, hidden_ref, query_ref, early_ref,
    rows_ref, loss_ref, grad_ref, keep_ref, send_ref,
):
    embedded = embedded_ref[...]
    positives = positives_ref[...].astype(jnp.float32)
    q_dev, width = embedded.shape
    pos_scores, early, total = (early_ref[:, width + i : width + i + 1] for i in range(3))
    rows = rows_ref[...]
    per = rows.shape[0]
    score = contract_last(embedded, rows) * scale
    member = query_ref[:, (CHUNKS - 1) * per :] == lax.broadcasted_iota(
        jnp.int32, (q_dev, per), 0
    )
    largest = jnp.maximum(
        early, jnp.max(jnp.where(member, score, early), axis=1, keepdims=True)
    )
    late = jnp.where(member, jnp.exp(score - largest), 0.0)
    total = total * jnp.exp(early - largest) + jnp.sum(late, axis=1, keepdims=True)
    log_total = largest + jnp.log(total)
    loss_ref[...] = log_total - pos_scores
    grad = (jnp.exp(pos_scores - log_total) - 1.0) * positives
    grad = grad + jnp.exp(early - log_total) * early_ref[:, :width]
    grad = grad + weighted_rows(late * (1.0 / total), rows)
    query_grad = (grad * scale).astype(jnp.bfloat16)
    grad_ref[...] = query_grad
    my_core = place_ref[1]
    hid = hidden_ref.shape[1]
    deep, part, half = hid // SHARD // X, hid // Z, width // CORE
    for z in range(Z):
        outer = contract_first(hidden_ref[:, z * part : (z + 1) * part], query_grad)
        left, right = outer[:, :half], outer[:, half:]
        keep = jnp.where(my_core == 0, left, right).astype(jnp.bfloat16)
        send = jnp.where(my_core == 0, right, left).astype(jnp.bfloat16)
        for y in range(Y):
            for x in range(X):
                rows = slice((y * X + x) * deep, (y * X + x + 1) * deep)
                keep_ref[y, x, z * deep : (z + 1) * deep, :] = keep[rows]
                send_ref[y, x, z * deep : (z + 1) * deep, :] = send[rows]


def inner_kernel(place_ref, queries_ref, grad_ref, slope_ref, weight_ref, keep_ref, send_ref):
    queries, query_grad = queries_ref[...], grad_ref[...]
    part = weight_ref.shape[0] // GRP
    for by_core, out_ref in ((1, send_ref), (0, keep_ref)):
        for by_x in range(X):
            group = (place_ref[0] ^ by_x) * CORE + (place_ref[1] ^ by_core)
            at = pl.ds(pl.multiple_of(group * part, part), part)
            hidden_grad = contract_last(query_grad, weight_ref[at, :])
            pre_grad = (hidden_grad * slope_ref[:, at]).astype(jnp.bfloat16)
            out_ref[by_x] = contract_first(queries, pre_grad).astype(jnp.bfloat16)


def total_of(parts):
    return sum(part.astype(jnp.float32) for part in parts)


def columns_to_rows(value, wide):
    return jnp.concatenate(
        [value[..., i : i + wide] for i in range(0, value.shape[-1], wide)], axis=-2
    )


def rows_to_columns(value, deep):
    return jnp.concatenate(
        [value[..., i : i + deep, :] for i in range(0, value.shape[-2], deep)], axis=-1
    )


def shards(queries, positives, negative_ids, passage_table, inner_weight, outer_weight):
    q_dev, width = queries.shape
    rows_dev = passage_table.shape[0]
    shift = rows_dev.bit_length() - 1
    hid = inner_weight.shape[1]
    inner_rows, outer_rows = inner_weight.shape[0], outer_weight.shape[0]
    scale = float(width) ** (-0.5)
    limits = {"compiler_params": pltpu.CompilerParams(vmem_limit_bytes=VMEM)}
    my_x, my_core, my_y = (lax.axis_index(axis) for axis in ("x", "core", "y"))
    group = my_x * CORE + my_core
    place = jnp.stack([my_x, my_core]).astype(jnp.int32)
    in_smem = pl.BlockSpec(memory_space=pltpu.SMEM)
    in_vmem = pl.BlockSpec(memory_space=pltpu.VMEM)

    code, slot_query = pl.pallas_call(
        functools.partial(request_kernel, shift),
        out_shape=[
            jax.ShapeDtypeStruct((SHARD, q_dev), jnp.int32),
            jax.ShapeDtypeStruct((PAIRS, q_dev), jnp.int32),
        ],
        **limits,
    )(negative_ids.T)
    code = exchange(code, ("z", "y")).reshape(Z, Y, q_dev)
    code = jnp.stack([lax.dynamic_index_in_dim(code, my_y ^ by, 1, False) for by in range(Y)])
    own = (code >> shift) == my_y % 2
    wanted = code & (rows_dev - 1)
    wanted = lax.optimization_barrier((wanted[:, :, : q_dev // 2], wanted[:, :, q_dev // 2 :]))
    per = q_dev // 2
    cuts = slice(0, per), slice(per, q_dev)

    def find(picks, *done):
        ids = jnp.stack([wanted[part][by] for by, part in picks])
        ids = after(ids.reshape(-1), *done)
        found = passage_table.at[ids].get(mode="promise_in_bounds").reshape(-1, Z * per, width)
        return [
            jnp.where(own[by, :, cuts[part]].reshape(-1, 1), found[i], jnp.zeros((), found.dtype))
            for i, (by, part) in enumerate(picks)
        ]

    wide, deep = hid // GRP, outer_rows // GRP
    inner_piece = lax.dynamic_slice(inner_weight, (0, group * wide), (inner_rows, wide))
    outer_piece = lax.dynamic_slice(outer_weight, (group * deep, 0), (deep, width))
    piece = jnp.concatenate([rows_to_columns(inner_piece, deep), outer_piece], axis=0)

    found_10, found_30 = find([(1, 0), (3, 0)])
    near_10, near_30 = swap(found_10, "y", 1), swap(found_30, "y", 3)
    gathered = spread(after(piece, found_10), ("z", "y"), SHARD)
    found_11, found_31, found_00 = find([(1, 1), (3, 1), (0, 0)], found_10)
    near_11, near_31 = swap(found_11, "y", 1), swap(found_31, "y", 3)
    found_20, found_01 = find([(2, 0), (0, 1)], found_11, near_10, near_30)
    near_20 = swap(found_20, "y", 2)
    own_0 = after(found_00 + after(near_10, found_11, found_31), gathered, near_30)
    rows_0 = exchange(own_0, "z")
    gathered = after(gathered, own_0)
    parts = [gathered] + [swap(gathered, "x", by) for by in range(1, X)]
    (found_21,) = find([(2, 1)], found_20, near_31)
    near_21 = swap(found_21, "y", 2)
    own_1 = found_01 + after(near_11, own_0)
    rows_1 = exchange(after(own_1, rows_0, near_31, found_21), "z")
    rows_2 = exchange(after(near_20 + near_30, rows_1, found_21), "z")
    other_1 = near_21 + near_31
    rows_3 = exchange(after(other_1, rows_2), "z")
    chunks = [rows_0, rows_1, rows_2, rows_3]
    parts = after(tuple(parts + [swap(part, "core", 1) for part in parts]), rows_1)
    halves = pl.pallas_call(
        arrange_kernel,
        out_shape=jax.ShapeDtypeStruct((X, CORE, SHARD, *piece.shape), piece.dtype),
        in_specs=[in_smem] + [in_vmem] * GRP,
        **limits,
    )(place, *parts)
    slot_query = slot_query.reshape(Z, 2, q_dev)
    slot_query = jnp.where(my_y // 2 == 0, slot_query, slot_query[:, ::-1])
    slot_query = jnp.concatenate(
        [slot_query[:, pair, cut].reshape(1, -1) for pair in range(2) for cut in cuts], axis=1
    )

    inner_full = [
        columns_to_rows(halves[g // CORE, g % CORE, :, :deep], wide).reshape(width, wide)
        for g in range(GRP)
    ]
    outer_full = halves[:, :, :, deep:].transpose(2, 0, 1, 3, 4).reshape(hid, width)

    pre_act = jnp.concatenate(
        [jnp.dot(queries, part, preferred_element_type=jnp.float32) for part in inner_full], axis=1
    )
    hidden = gelu_value(pre_act).astype(jnp.bfloat16)
    slope = gelu_slope(pre_act)
    projected = jnp.dot(hidden, outer_full, preferred_element_type=jnp.float32)
    embedded = (queries.astype(jnp.float32) + projected).astype(jnp.bfloat16)

    half = width // CORE
    outer_cut = jax.ShapeDtypeStruct((Y, X, hid // Y // X, half), jnp.bfloat16)
    early = pl.pallas_call(
        functools.partial(early_kernel, scale),
        out_shape=jax.ShapeDtypeStruct((q_dev, width + LANES), jnp.float32),
        **limits,
    )(embedded, positives, slot_query, *chunks[:-1])
    losses, query_grad, outer, outer_sent = pl.pallas_call(
        functools.partial(score_kernel, scale),
        out_shape=[
            jax.ShapeDtypeStruct((q_dev, 1), jnp.float32),
            jax.ShapeDtypeStruct((q_dev, width), jnp.bfloat16),
            outer_cut,
            outer_cut,
        ],
        in_specs=[in_smem] + [in_vmem] * 6,
        **limits,
    )(place, embedded, positives, hidden, slot_query, early, chunks[-1])
    outer_sent = swap(outer_sent, "core", 1)
    inner, inner_sent = pl.pallas_call(
        inner_kernel,
        out_shape=[jax.ShapeDtypeStruct((X, width, wide), jnp.bfloat16)] * 2,
        in_specs=[in_smem] + [in_vmem] * 4,
        **limits,
    )(place, queries, query_grad, slope, outer_full)
    inner_sent = swap(inner_sent, "core", 1)

    narrow = lambda value: value.astype(jnp.bfloat16)
    outer = exchange(narrow(total_of([outer, outer_sent])), "y")
    inner = [narrow(total_of([inner[by], inner_sent[by]])) for by in range(X)]
    inner = inner[:1] + [swap(inner[by], "x", by) for by in range(1, X)]
    outer = narrow(total_of(list(outer)))
    inner = after(tuple(inner), outer)
    outer = exchange(outer, "x")
    inner = narrow(total_of(inner)).reshape(Z, Y, inner_rows, wide)
    inner = [lax.dynamic_index_in_dim(inner, my_y ^ by, 1, False) for by in range(Y)]
    inner = inner[:1] + [swap(inner[by], "y", by) for by in range(1, Y)]
    lanes = 128
    both = jnp.concatenate(
        [
            columns_to_rows(total_of(inner), lanes),
            columns_to_rows(total_of(list(outer)).reshape(Z, -1, half), lanes),
        ],
        axis=1,
    )
    both = total_of(list(exchange(narrow(both), "z")))
    both = spread(narrow(both), ("x", "core"), GRP).astype(jnp.float32)
    inner_deep = inner_rows * wide // lanes
    inner = rows_to_columns(both[:, :inner_deep], inner_rows)
    outer = rows_to_columns(both[:, inner_deep:], outer_rows // X)
    inner = jnp.concatenate(list(inner), axis=1)
    outer = jnp.concatenate(
        [jnp.concatenate([outer[x * CORE + c] for c in range(CORE)], axis=1) for x in range(X)],
        axis=0,
    )
    return (losses.reshape(-1), inner, outer)


def solution(mesh):
    fine = Mesh(mesh.devices.reshape(X, CORE, Z, Y), ("x", "core", "z", "y"))
    blocks, rows = ("x", "core", "z", "y"), ("z", "y")
    return jax.shard_map(
        shards,
        mesh=fine,
        in_specs=(
            P(blocks, None),
            P(blocks, None),
            P(blocks, None),
            P(rows, None),
            P(rows, None),
            P(rows, None),
        ),
        out_specs=(P(blocks), P(rows, None), P(rows, None)),
        check_vma=False,
    )
```
